128 devices in a mesh: kv: 16 (over y, x), head: 8 (over z, core).
Axes of the slice: x: 4, y: 4, z: 4, core: 2. Of those that a mesh axis runs over, the one named last changes fastest.
Arguments:
- hidden_in: bfloat16 [64, 6144], P(None, 'kv'), may hold values from -1 to 1
- attn_gain: float32 [6144], P('kv'), may hold values from 0.1 to 1.9
- attn_weight: bfloat16 [6144, 10240], P('kv', 'head'), may hold values from -0.078125 to 0.078125
- attn_out_weight: bfloat16 [8192, 6144], P('head', 'kv'), may hold values from -0.25 to 0.25
- cache_keys: bfloat16 [1024, 8, 256, 128], P('kv', 'head'), may hold values from -600 to 600
- cache_values: bfloat16 [1024, 8, 256, 128], P('kv', 'head'), may hold values from -6 to 6
- stretch_counts: int32 [64], replicated, may hold values from 1 to 64, 896 in all
- tail_tokens: int32 [64], replicated, may hold values from 0 to 255
- slot_stretch: int32 [1024], P('kv'), may hold values from 0 to 1023, each once
- lin_gain: float32 [6144], P('kv'), may hold values from 0.1 to 1.9
- lin_weight: bfloat16 [6144, 32768], P('kv', 'head'), may hold values from -0.078125 to 0.078125
- decay_rate: float32 [64], P('head'), may hold values from 0.02 to 2
- states: float32 [64, 64, 128, 128], P('kv', 'head'), may hold values from -2 to 2
- out_gain: float32 [8192], P('head'), may hold values from 0.1 to 1.9
- lin_out_weight: bfloat16 [8192, 6144], P('head', 'kv'), may hold values from -0.0625 to 0.0625
- state_request: int32 [64], replicated, may hold values from 0 to 63, each once
Outputs:
- hidden_out: bfloat16 [64, 6144], P(None, 'kv')
- new_states: float32 [64, 64, 128, 128], P('kv', 'head')
The draws below stay inside these ranges and needn't reach their ends.
Inputs may be any that keep to these rules, and one draw needn't show every extreme that they name: `stretch_counts`: the counts sum to 896; some request has exactly 64 stretches. `slot_stretch`: each id of 0 to 1023 once; ids of 896 or more mark empty slots. `state_request`: each request once.
All inputs are finite; a program needn't handle non-finite values.
Results may differ from the reference program's by a relative error of at most 0.014.
The reference program's roundings to bfloat16 on the way count: a program that leaves them out, or rounds other values in their place, can miss the bound.
Values may be sent and summed in bfloat16 or wider, within the bound.
No kernel may reach another device: no remote copies, remote signals or barrier semaphores. Data moves between devices by JAX's collectives and lax.ppermute only.
A program may use at most 64 MiB of HBM per device.

```python
import math
import jax
import jax.numpy as jnp
import numpy as np
from jax import lax

D = 6144
QH = 64
KVH = 8
HD = 128
LH = 64
CH = 256
GQ = 8
REQ = 64
SLOTS = 1024
STRETCHES = 896
MOSTC = 64


def draw_hidden_in(key, part):
    key = jax.random.fold_in(key, 5)
    first, second, third = jax.random.split(key, 3)
    rows = jnp.exp(jax.random.uniform(second, (REQ, 1), jnp.float32, math.log(0.2), math.log(2.0)))
    rise = 1.0 + 2.0 * jnp.arange(D, dtype=jnp.float32)[None, :] / (D - 1)
    columns = jnp.exp(jax.random.uniform(third, (1, D), jnp.float32, math.log(0.3), math.log(1.0))) * rise
    base = jax.random.normal(first, (REQ, D), jnp.float32)
    return jnp.clip(0.25 * base * rows * columns, -1.0, 1.0).astype(jnp.bfloat16)


def draw_cache_keys(key, part):
    key = jax.random.fold_in(key, 3)
    first = jax.random.fold_in(key, 0)
    shape = (SLOTS, KVH, CH, HD)
    base = 2.0 * jax.random.normal(first, shape, jnp.float32)
    return jnp.clip(base, -10.0, 10.0).astype(jnp.bfloat16)


def draw_states(key, part):
    key = jax.random.fold_in(key, 7)
    first = jax.random.fold_in(key, 0)
    shape = (REQ, LH, HD, HD)
    rise = 0.1 * (1.0 + 2.0 * jnp.arange(LH, dtype=jnp.float32) / (LH - 1))[None, :, None, None]
    base = jax.random.normal(first, shape, jnp.float32)
    return jnp.clip(base * rise, -2.0, 2.0)


def touch_ends(values, rng, least, top_value):
    shape = values.shape
    spot = [jax.random.randint(jax.random.fold_in(rng, axis), (), 0, shape[axis]) for axis in range(len(shape))]
    values = values.at[tuple(spot)].set(least)
    longest = shape.index(max(shape))
    spot[longest] = (spot[longest] + 1) % shape[longest]
    return values.at[tuple(spot)].set(top_value)


def shard_levels(key, dims, shards, least, high):
    loudness, own = 1.0, jax.random.fold_in(key, 6)
    for dim, parts in shards:
        draws = jnp.exp(jax.random.uniform(jax.random.fold_in(own, dim), (parts,), jnp.float32, least / len(shards), high / len(shards)))
        loudness = loudness * jnp.repeat(draws, dims[dim] // parts).reshape([-1 if axis == dim else 1 for axis in range(len(dims))])
    return loudness


def profile(count, total, reach, slope):
    loads = [(1 << 20) // math.isqrt(rank ** slope) + 1 for rank in range(2, count + 1)]
    surplus, given = total - reach - (count - 1), [1] * (count - 1)
    while surplus > 0:
        movable = [i for i in range(count - 1) if given[i] < reach]
        mass, budget = sum([loads[i] for i in movable]), surplus
        for i in movable:
            more = min(reach - given[i], max(1, budget * loads[i] // mass), surplus)
            given[i] = given[i] + more
            surplus = surplus - more
    return np.array([reach] + given)


def ragged_sizes(key, count, total, bound, skew):
    if count == 2:
        one = jax.random.randint(key, (), max(1, total - bound), min(bound, total - 1) + 1)
        return jnp.stack([one, total - one])
    sizes = jnp.asarray(profile(count, total, bound, skew), jnp.int32)
    twos = (count - 1) // 2
    source_of, taker = sizes[1:1 + 2 * twos:2], sizes[2:2 + 2 * twos:2]
    slack = jnp.minimum(source_of - 1, bound - taker)
    shifted = jax.random.randint(jax.random.fold_in(key, 1), (twos,), 0, 1 << 20) % (slack + 1)
    sizes = sizes.at[1:1 + 2 * twos:2].set(source_of - shifted).at[2:2 + 2 * twos:2].set(taker + shifted)
    return sizes[jax.random.permutation(jax.random.fold_in(key, 2), count)]


def bell_draw(own_key, dims, scale, reach, cuts=(), kind=jnp.bfloat16):
    entries = scale * jax.random.normal(own_key, dims, jnp.float32)
    if cuts:
        entries = entries * shard_levels(own_key, dims, cuts, -0.22, 0.18)
    return jnp.clip(entries, -reach, reach).astype(kind)


def setup_inputs(seed: int = 0) -> dict:
    streams_of = jax.random.split(jax.random.key(seed), 17)
    hidden_in = draw_hidden_in(jax.random.fold_in(streams_of[16], 71), 0)
    attn_gain = jnp.clip(1.0 + 0.18 * jax.random.normal(streams_of[1], (D,), jnp.float32), 0.1, 1.9)
    attn_weight = bell_draw(streams_of[2], (D, KVH * (GQ + 2) * HD), D ** -0.5, 0.078125, ((0, 16), (1, 8)))
    attn_out_weight = bell_draw(streams_of[3], (QH * HD, D), (4 * HD) ** -0.5, 0.25, ((0, 8), (1, 16)))
    cache_keys = draw_cache_keys(jax.random.fold_in(streams_of[16], 71), 0)
    cache_values = bell_draw(streams_of[5], (SLOTS, KVH, CH, HD), 1.0, 6.0, ((0, 16), (1, 8)))
    stretch_counts = ragged_sizes(streams_of[6], REQ, STRETCHES, MOSTC, 2).astype(jnp.int32)
    tail_tokens = touch_ends(jax.random.randint(streams_of[7], (REQ,), 0, CH), jax.random.fold_in(streams_of[7], 1), 0, CH - 1).astype(jnp.int32)
    slot_stretch = jax.random.permutation(streams_of[8], SLOTS).astype(jnp.int32)
    lin_gain = jnp.clip(1.0 + 0.18 * jax.random.normal(streams_of[9], (D,), jnp.float32), 0.1, 1.9)
    lin_weight = bell_draw(streams_of[10], (D, LH * 4 * HD), D ** -0.5, 0.078125, ((0, 16), (1, 8)))
    decay_rate = jnp.clip(jnp.exp(math.log(2.0) - 4.6051702 * jax.random.uniform(streams_of[11], (LH,), jnp.float32) ** shard_levels(streams_of[11], (LH,), ((0, 8),), -0.2, 0.2)), 0.02, 2.0)
    states = draw_states(jax.random.fold_in(streams_of[16], 71), 0)
    out_gain = jnp.clip(1.0 + 0.18 * jax.random.normal(streams_of[13], (LH * HD,), jnp.float32), 0.1, 1.9)
    lin_out_weight = bell_draw(streams_of[14], (LH * HD, D), (LH * HD) ** -0.5, 0.0625, ((0, 8), (1, 16)))
    state_request = jax.random.permutation(streams_of[15], REQ).astype(jnp.int32)
    return {"hidden_in": hidden_in, "attn_gain": attn_gain, "attn_weight": attn_weight, "attn_out_weight": attn_out_weight, "cache_keys": cache_keys, "cache_values": cache_values, "stretch_counts": stretch_counts, "tail_tokens": tail_tokens, "slot_stretch": slot_stretch, "lin_gain": lin_gain, "lin_weight": lin_weight, "decay_rate": decay_rate, "states": states, "out_gain": out_gain, "lin_out_weight": lin_out_weight, "state_request": state_request}


EPS = 1e-05
NEGATIVE = -1e+30

def stretch_table(stretch_counts, tail_tokens, slot_stretch, span):
    number = stretch_counts.shape[0]
    ends = jnp.cumsum(stretch_counts).astype(jnp.int32)
    starts = ends - stretch_counts
    limits = stretch_counts * span - tail_tokens
    owner = lax.optimization_barrier(jnp.sum((slot_stretch[:, None] >= ends[None, :]).astype(jnp.int32), axis=1))
    hits = owner[:, None] == jnp.arange(number, dtype=jnp.int32)[None, :]
    first = lax.optimization_barrier(jnp.sum(jnp.where(hits, starts[None, :], 0), axis=1)).astype(jnp.int32)
    limit = lax.optimization_barrier(jnp.sum(jnp.where(hits, limits[None, :], 0), axis=1)).astype(jnp.int32)
    offset = (slot_stretch - first) * span
    valid = offset[:, None] + jnp.arange(span, dtype=jnp.int32)[None, :] < limit[:, None]
    return (hits, valid)

def slot_partials(picked, keys, values, valid):
    scores = jnp.einsum('sgd,std->sgt', picked.astype(jnp.float32), keys.astype(jnp.float32)) / math.sqrt(keys.shape[-1])
    mask = valid[:, None, :]
    highest = lax.optimization_barrier(jnp.max(jnp.where(mask, scores, NEGATIVE), axis=-1))
    weights = jnp.where(mask, jnp.exp(scores - highest[..., None]), 0.0)
    totals = lax.optimization_barrier(jnp.sum(weights, axis=-1))
    rounded = weights.astype(jnp.bfloat16)
    partial_value = jnp.einsum('sgt,std->sgd', rounded.astype(jnp.float32), values.astype(jnp.float32))
    return (highest, totals, partial_value)

def fold_slots(hits, highest, totals, partial_value):
    chosen = hits.T[:, :, None, None]
    best = lax.optimization_barrier(jnp.max(jnp.where(chosen, highest[None], NEGATIVE), axis=1))
    factor = jnp.where(chosen, jnp.exp(jnp.minimum(highest[None] - best[:, None], 0.0)), 0.0)
    summed = lax.optimization_barrier(jnp.sum(factor * totals[None], axis=1))
    mixed = jnp.einsum('rskg,skgd->rkgd', factor, partial_value, precision=lax.Precision.HIGHEST)
    return (best, summed, mixed)

def finish(best, summed, mixed, queries, fresh_key, fresh_value):
    fresh = jnp.einsum('rkgd,rkd->rkg', queries.astype(jnp.float32), fresh_key.astype(jnp.float32)) / math.sqrt(queries.shape[-1])
    peak = jnp.maximum(best, fresh)
    earlier = jnp.exp(best - peak)
    latest = jnp.exp(fresh - peak)
    result = (earlier[..., None] * mixed + latest[..., None] * fresh_value.astype(jnp.float32)[:, :, None, :]) / (earlier * summed + latest)[..., None]
    return result.astype(jnp.bfloat16)

def reference(hidden_in, attn_gain, attn_weight, attn_out_weight, cache_keys, cache_values, stretch_counts, tail_tokens, slot_stretch, lin_gain, lin_weight, decay_rate, states, out_gain, lin_out_weight, state_request):
    inputs = hidden_in.astype(jnp.float32)
    mean_one = lax.optimization_barrier(jnp.mean(inputs * inputs, axis=1))
    scaled = (inputs * attn_gain).astype(jnp.bfloat16)
    projected = jnp.dot(scaled, attn_weight, preferred_element_type=jnp.float32) / jnp.sqrt(mean_one + EPS)[:, None]
    projected = projected.astype(jnp.bfloat16).reshape(REQ, KVH, GQ + 2, HD)
    queries = projected[:, :, :GQ]
    fresh_key = projected[:, :, GQ]
    fresh_value = projected[:, :, GQ + 1]
    hits, valid = stretch_table(stretch_counts, tail_tokens, slot_stretch, CH)
    picked = jnp.einsum('sr,rkgd->ksgd', hits.astype(jnp.float32), queries.astype(jnp.float32))

    def per_head(pieces):
        return slot_partials(pieces[0], pieces[1], pieces[2], valid)
    highest, totals, partial_value = lax.map(per_head, (picked, jnp.moveaxis(cache_keys, 1, 0), jnp.moveaxis(cache_values, 1, 0)))
    highest = jnp.moveaxis(highest, 0, 1)
    totals = jnp.moveaxis(totals, 0, 1)
    partial_value = jnp.moveaxis(partial_value, 0, 1)
    best, summed, mixed = fold_slots(hits, highest, totals, partial_value)
    attended = finish(best, summed, mixed, queries, fresh_key, fresh_value).reshape(REQ, KVH * GQ * HD)
    first_out = jnp.dot(attended, attn_out_weight, preferred_element_type=jnp.float32)
    middle = (inputs + first_out).astype(jnp.bfloat16)
    inner = middle.astype(jnp.float32)
    mean_two = lax.optimization_barrier(jnp.mean(inner * inner, axis=1))
    scaled_two = (inner * lin_gain).astype(jnp.bfloat16)
    ordered = scaled_two[state_request]
    mixing = jnp.dot(ordered, lin_weight, preferred_element_type=jnp.float32) / jnp.sqrt(mean_two[state_request] + EPS)[:, None]
    mixing = mixing.reshape(REQ, LH, 4, HD)
    query = jax.nn.silu(mixing[:, :, 0])
    keyed = jax.nn.silu(mixing[:, :, 1])
    valued = jax.nn.silu(mixing[:, :, 2])
    gate = jax.nn.sigmoid(mixing[:, :, 3])
    keep = jnp.exp(-decay_rate)[None, :, None, None]
    renewed = keep * states + keyed[..., :, None] * valued[..., None, :]
    readout = jnp.einsum('rhi,rhij->rhj', query, renewed, precision=lax.Precision.HIGHEST)
    mean_three = lax.optimization_barrier(jnp.mean(readout * readout, axis=(1, 2)))
    gated = (readout / jnp.sqrt(mean_three + EPS)[:, None, None] * out_gain.reshape(LH, HD) * gate).astype(jnp.bfloat16).reshape(REQ, LH * HD)
    second_out = jnp.dot(gated, lin_out_weight, preferred_element_type=jnp.float32)
    placed = jnp.zeros_like(second_out).at[state_request].set(second_out)
    hidden_out = (inner + placed).astype(jnp.bfloat16)
    return (hidden_out, renewed)
```

```python
import functools
import math

import jax
import jax.numpy as jnp
from jax import lax
from jax.experimental import pallas as pl
from jax.experimental.pallas import tpu as pltpu
from jax.sharding import PartitionSpec as P

D = 6144
HD = 128
LH = 64
CH = 256
GQ = 8
REQ = 64
EPS = 1e-05
NEGATIVE = -1e30
F32 = jnp.float32
BF16 = jnp.bfloat16
MIB = 1 << 20


def iota(shape, dim):
    return lax.broadcasted_iota(jnp.int32, shape, dim)


def as_column(row):
    n = row.shape[1]
    eye = iota((n, n), 0) == iota((n, n), 1)
    return jnp.sum(jnp.where(eye, row, jnp.zeros_like(row)), axis=1, keepdims=True)


def as_row(column):
    n = column.shape[0]
    eye = iota((n, n), 0) == iota((n, n), 1)
    return jnp.sum(jnp.where(eye, column, jnp.zeros_like(column)), axis=0, keepdims=True)


def kernel_call(body, outs, ins, limit, flops, moved, scratch=()):
    return pl.pallas_call(
        body,
        out_shape=outs,
        in_specs=ins,
        out_specs=jax.tree.map(lambda _: pl.BlockSpec(memory_space=pltpu.VMEM), outs),
        scratch_shapes=scratch,
        compiler_params=pltpu.CompilerParams(vmem_limit_bytes=limit),
        cost_estimate=pl.CostEstimate(flops=flops, bytes_accessed=moved, transcendentals=0),
    )


VMEM = pl.BlockSpec(memory_space=pltpu.VMEM)
SMEM = pl.BlockSpec(memory_space=pltpu.SMEM)


def project_kernel(hidden, gain, weight, counts, tails, slots, out, info):
    x = hidden[...].astype(F32)
    scaled = (x * gain[...]).astype(BF16)
    squares = jnp.sum(x * x, axis=1, keepdims=True)
    y = jnp.dot(scaled, weight[...], preferred_element_type=F32)
    groups, rows, _ = out.shape
    width = weight.shape[1]
    wide = jnp.broadcast_to(squares, (x.shape[0], HD))
    for p in range(groups):
        out[p, :, :width] = y[p * rows:(p + 1) * rows]
        out[p, :, width:] = wide[p * rows:(p + 1) * rows]
    number = counts[...]
    n = number.shape[1]
    below = iota((n, n), 1) <= iota((n, n), 0)
    ends = jnp.sum(jnp.where(below, number, 0), axis=1, keepdims=True)
    count = as_column(number)
    starts = ends - count
    limits = count * CH - as_column(tails[...])
    slot = slots[...]
    owner = jnp.sum((slot >= ends).astype(jnp.int32), axis=0, keepdims=True)
    hits = iota((n, slot.shape[1]), 0) == owner
    first = jnp.sum(jnp.where(hits, starts, 0), axis=0, keepdims=True)
    limit = jnp.sum(jnp.where(hits, limits, 0), axis=0, keepdims=True)
    live = jnp.clip(limit - (slot - first) * CH, 0, CH)
    info[0:1, :] = owner
    info[1:2, :] = jnp.where(owner < n, live, 0)


def normalise_kernel(parts, out, own):
    total = parts[0]
    for p in range(1, parts.shape[0]):
        total = total + parts[p]
    width = own.shape[1] * HD
    mean = total[:, width:width + 1] / D
    projected = (total[:, :width] / jnp.sqrt(mean + EPS)).astype(BF16).astype(F32)
    for g in range(own.shape[1]):
        own[:, g, :] = projected[:, g * HD:(g + 1) * HD]
    queries = own[:, :GQ, :].astype(BF16)
    for p in range(out.shape[0]):
        out[p] = queries


def attention_kernel(queries, keys, values, info, out, slot_max, slot_sum, slot_value, best, summed, mixed):
    slots = keys.shape[0]
    rows = out.shape[1] // (GQ + 2)
    best[...] = jnp.full(best.shape, NEGATIVE, F32)
    summed[...] = jnp.zeros(summed.shape, F32)
    mixed[...] = jnp.zeros(mixed.shape, F32)
    token = iota((GQ, CH), 1)
    scale = 1.0 / math.sqrt(HD)
    batch = 8

    @pl.loop(0, slots, step=batch)
    def _(base):
        for u in range(batch):
            s = base + u
            owner = info[0, s]
            q = queries[jnp.minimum(owner, REQ - 1)]
            scores = lax.dot_general(
                q, keys[s], (((1,), (1,)), ((), ())), preferred_element_type=F32
            ) * scale
            live = token < info[1, s]
            top = jnp.max(jnp.where(live, scores, NEGATIVE), axis=1, keepdims=True)
            weights = jnp.where(live, jnp.exp(scores - top), 0.0)
            slot_sum[s] = jnp.broadcast_to(jnp.sum(weights, axis=1, keepdims=True), (GQ, HD))
            slot_max[s] = jnp.broadcast_to(top, (GQ, HD))
            slot_value[s] = jnp.dot(weights.astype(BF16), values[s], preferred_element_type=F32)

    @pl.loop(0, slots, step=batch)
    def _(base):
        for u in range(batch):
            s = base + u
            r = info[0, s]
            best[r] = jnp.maximum(best[r], slot_max[s])

    @pl.loop(0, slots, step=batch)
    def _(base):
        for u in range(batch):
            s = base + u
            r = info[0, s]
            factor = jnp.exp(slot_max[s] - best[r])
            summed[r] = summed[r] + factor * slot_sum[s]
            mixed[r] = mixed[r] + factor * slot_value[s]

    lane, sub = iota((GQ, HD), 1), iota((GQ, HD), 0)

    @pl.loop(0, out.shape[0])
    def _(p):
        for i in range(rows):
            r = p * rows + i
            out[p, i * GQ:(i + 1) * GQ, :] = mixed[r]
            packed = jnp.where(lane == sub, best[r], 0.0) + jnp.where(lane == sub + GQ, summed[r], 0.0)
            out[p, rows * GQ + i:rows * GQ + i + 1, :] = jnp.sum(packed, axis=0, keepdims=True)


def finish_kernel(parts, own, out, flat, fresh_rows):
    peers, rows = parts.shape[0], own.shape[0]
    lane, sub = iota((GQ, HD), 1), iota((GQ, HD), 0)
    diagonal = lane == sub
    for i in range(rows):
        fresh = jnp.sum(own[i, :GQ, :] * own[i, GQ:GQ + 1, :], axis=1, keepdims=True) / math.sqrt(HD)
        fresh_rows[i:i + 1, :] = jnp.sum(jnp.where(diagonal, fresh, 0.0), axis=0, keepdims=True)
    fresh = fresh_rows[0:rows, :]
    stats = [parts[p, rows * GQ:rows * GQ + rows, :] for p in range(peers)]
    top = fresh
    for p in range(peers):
        top = jnp.maximum(top, stats[p])
    latest = jnp.exp(fresh - top)
    below = latest
    factors = []
    for p in range(peers):
        factor = jnp.exp(stats[p] - top)
        below = below + factor * pltpu.roll(stats[p], HD - GQ, axis=1)
        factors.append(factor)
    for i in range(rows):
        def column(value):
            return jnp.sum(jnp.where(diagonal, value[i:i + 1, :], 0.0), axis=1, keepdims=True)

        above = column(latest) * own[i, GQ + 1:GQ + 2, :]
        for p in range(peers):
            above = above + column(factors[p]) * parts[p, i * GQ:(i + 1) * GQ, :]
        result = above / column(below)
        for g in range(GQ):
            flat[i:i + 1, g * HD:(g + 1) * HD] = result[g:g + 1, :]
    attended = flat[0:rows, :].astype(BF16)
    for p in range(out.shape[0]):
        out[p] = attended


def stacked(blocks, flat):
    peers, rows, _ = blocks.shape
    for p in range(peers):
        flat[p * rows:(p + 1) * rows, :] = blocks[p].astype(F32)


def attention_out_kernel(attended, weight, out, flat):
    stacked(attended, flat)
    out[...] = jnp.dot(flat[...].astype(BF16), weight[...], preferred_element_type=F32)


def mixing_kernel(one, two, hidden, gain, request, weight, out, middle):
    total = hidden[...].astype(F32) + (one[...] + two[...])
    inner = total.astype(BF16)
    middle[...] = inner
    n = request.shape[1]
    pick = (as_column(request[...]) == iota((n, n), 1)).astype(F32).astype(BF16)
    ordered = jnp.dot(pick, inner, preferred_element_type=F32)
    squares = jnp.broadcast_to(jnp.sum(ordered * ordered, axis=1, keepdims=True), (n, HD))
    scaled = (ordered * gain[...]).astype(BF16)
    groups, rows, _ = out.shape
    width = weight.shape[1]
    step = 512
    for c in range(0, width, step):
        y = jnp.dot(scaled, weight[:, c:c + step], preferred_element_type=F32)
        for p in range(groups):
            out[p, :, c:c + step] = y[p * rows:(p + 1) * rows].astype(out.dtype)
    for p in range(groups):
        out[p, :, width:] = squares[p * rows:(p + 1) * rows].astype(out.dtype)


def lightning_kernel(parts, decay, states, gain, renewed, out, flat, mixing, columns):
    total = parts[0].astype(F32)
    for p in range(1, parts.shape[0]):
        total = total + parts[p].astype(F32)
    rows, heads = states.shape[0], states.shape[1]
    width = heads * 4 * HD
    mixing[0:rows, :] = total[:, :width] / jnp.sqrt(total[:, width:width + 1] / D + EPS)
    keep_row = jnp.exp(-decay[...])
    squares = jnp.zeros((rows, 1), F32)
    for h in range(heads):
        at = h * 4 * HD
        mixed = [mixing[0:rows, at + k * HD:at + (k + 1) * HD] for k in range(4)]
        gate = 1.0 / (1.0 + jnp.exp(-mixed[3]))
        query, key, value = (m / (1.0 + jnp.exp(-m)) for m in mixed[:3])
        columns[0:rows, :] = query
        columns[rows:2 * rows, :] = key
        turned = columns[...].T
        inner = jnp.sum(query * key, axis=1, keepdims=True)
        keep = keep_row[:, h:h + 1]
        for j in range(rows):
            state = keep * states[j, h]
            renewed[j, h] = state + turned[:, rows + j:rows + j + 1] * value[j:j + 1, :]
            read = jnp.sum(turned[:, j:j + 1] * state, axis=0, keepdims=True)
            flat[j:j + 1, h * HD:(h + 1) * HD] = read + inner[j:j + 1, :] * value[j:j + 1, :]
        read = flat[0:rows, h * HD:(h + 1) * HD]
        squares = squares + jnp.sum(read * read, axis=1, keepdims=True)
        flat[0:rows, h * HD:(h + 1) * HD] = read * gain[:, h * HD:(h + 1) * HD] * gate
    size = heads * HD
    gated = flat[0:rows, 0:size].astype(BF16)
    upper = squares.astype(BF16).astype(F32)
    lane = iota((rows, HD), 1)
    tail = jnp.where(lane == 0, upper, jnp.where(lane == 1, squares - upper, 0.0)).astype(BF16)
    for p in range(out.shape[0]):
        out[p, :, :size] = gated
        out[p, :, size:] = tail


def lightning_out_kernel(blocks, request, weight, out, flat):
    stacked(blocks, flat)
    n = request.shape[1]
    size = weight.shape[0]
    pick = (iota((n, n), 0) == request[...]).astype(F32).astype(BF16)
    placed = jnp.dot(pick, flat[...].astype(BF16), preferred_element_type=F32)
    out[0:n, :] = jnp.dot(placed[:, :size].astype(BF16), weight[...], preferred_element_type=F32)
    squares = as_row(placed[:, size:size + 1] + placed[:, size + 1:size + 2])
    out[n:, :] = jnp.zeros((out.shape[0] - n, out.shape[1]), F32)
    out[n:n + 1, 0:n] = squares


def last_kernel(one, two, middle, out):
    n = middle.shape[0]
    squares = as_column(one[n:n + 1, 0:n] + two[n:n + 1, 0:n])
    scale = 1.0 / jnp.sqrt(squares / (LH * HD) + EPS)
    out[...] = (middle[...].astype(F32) + (one[0:n, :] + two[0:n, :]) * scale).astype(BF16)


def exchange(blocks):
    return lax.all_to_all(blocks, "kv", 0, 0, tiled=True)


def all_but_last_sum(value):
    size = lax.axis_size("head")
    value = value + lax.ppermute(value, "head", [(i, i ^ 1) for i in range(size)])
    value = value + lax.ppermute(value, "head", [(i, i ^ 2) for i in range(size)])
    last = [(i, (3 - i // 2) * 2 + i % 2) for i in range(size)]
    return value, lax.ppermute(value, "head", last)


def per_device(
    hidden_in,
    attn_gain,
    attn_weight,
    attn_out_weight,
    cache_keys,
    cache_values,
    stretch_counts,
    tail_tokens,
    slot_stretch,
    lin_gain,
    lin_weight,
    decay_rate,
    states,
    out_gain,
    lin_out_weight,
    state_request,
):
    peers = lax.axis_size("kv")
    requests, features = hidden_in.shape
    rows = requests // peers
    width = attn_weight.shape[1]
    slots = cache_keys.shape[0]
    heads = decay_rate.shape[0]
    lin_width = lin_weight.shape[1]
    size = heads * HD
    S = jax.ShapeDtypeStruct
    request = state_request[None, :]

    parts, info = kernel_call(
        project_kernel,
        (S((peers, rows, width + HD), F32), S((2, slots), jnp.int32)),
        [VMEM] * 6, 8 * MIB, 2 * requests * features * width, 2 * features * width,
    )(hidden_in, attn_gain[None, :], attn_weight, stretch_counts[None, :], tail_tokens[None, :], slot_stretch[None, :])
    queries, own = kernel_call(
        normalise_kernel,
        (S((peers, rows, GQ, HD), BF16), S((rows, GQ + 2, HD), F32)),
        [VMEM], 8 * MIB, 0, 8 * peers * rows * width,
    )(exchange(parts))
    queries = exchange(queries).reshape(requests, GQ, HD)
    tiles = [pltpu.VMEM((slots, GQ, HD), F32)] * 3 + [pltpu.VMEM((requests + 1, GQ, HD), F32)] * 3
    partial = kernel_call(
        attention_kernel,
        S((peers, rows * (GQ + 2), HD), F32),
        [VMEM, VMEM, VMEM, SMEM], 24 * MIB, 4 * slots * GQ * CH * HD, 4 * slots * CH * HD, tiles,
    )(queries, cache_keys.reshape(slots, CH, HD), cache_values.reshape(slots, CH, HD), info)
    attended = kernel_call(
        finish_kernel,
        S((peers, rows, GQ * HD), BF16),
        [VMEM, VMEM], 8 * MIB, 0, 8 * peers * rows * GQ * HD,
        [pltpu.VMEM((8, GQ * HD), F32), pltpu.VMEM((8, HD), F32)],
    )(exchange(partial), own)
    first = kernel_call(
        attention_out_kernel,
        S((requests, features), F32),
        [VMEM, VMEM], 8 * MIB, 2 * requests * GQ * HD * features, 2 * GQ * HD * features,
        [pltpu.VMEM((requests, GQ * HD), F32)],
    )(exchange(attended), attn_out_weight)
    one, two = all_but_last_sum(first)
    mixing, middle = kernel_call(
        mixing_kernel,
        (S((peers, rows, lin_width + HD), F32), S((requests, features), BF16)),
        [VMEM] * 6, 16 * MIB, 2 * requests * features * lin_width, 2 * features * lin_width,
    )(one, two, hidden_in, lin_gain[None, :], request, lin_weight)
    renewed, gated = kernel_call(
        lightning_kernel,
        (S(states.shape, F32), S((peers, rows, size + HD), BF16)),
        [VMEM] * 4, 16 * MIB, 0, 8 * rows * size * HD,
        [pltpu.VMEM((8, size), F32), pltpu.VMEM((8, lin_width), F32), pltpu.VMEM((2 * rows, HD), F32)],
    )(exchange(mixing), decay_rate[None, :], states, out_gain[None, :])
    second = kernel_call(
        lightning_out_kernel,
        S((requests + 8, features), F32),
        [VMEM] * 3, 8 * MIB, 2 * requests * size * features, 2 * size * features,
        [pltpu.VMEM((requests, size + HD), F32)],
    )(exchange(gated), request, lin_out_weight)
    one, two = all_but_last_sum(second)
    hidden_out = kernel_call(
        last_kernel,
        S((requests, features), BF16),
        [VMEM] * 3, 4 * MIB, 0, 16 * requests * features,
    )(one, two, middle)
    return hidden_out, renewed


def solution(mesh):
    placed = (
        P(None, "kv"),
        P("kv"),
        P("kv", "head"),
        P("head", "kv"),
        P("kv", "head", None, None),
        P("kv", "head", None, None),
        P(),
        P(),
        P("kv"),
        P("kv"),
        P("kv", "head"),
        P("head"),
        P("kv", "head", None, None),
        P("head"),
        P("head", "kv"),
        P(),
    )
    return jax.shard_map(
        per_device,
        mesh=mesh,
        in_specs=placed,
        out_specs=(P(None, "kv"), P("kv", "head", None, None)),
        check_vma=False,
    )
```

```python
import functools
import math

import jax
import jax.numpy as jnp
from jax import lax
from jax.experimental import pallas as pl
from jax.experimental.pallas import tpu as pltpu
from jax.sharding import PartitionSpec as P

D = 6144
HD = 128
LH = 64
CH = 256
GQ = 8
REQ = 64
EPS = 1e-05
NEGATIVE = -1e30
F32 = jnp.float32
BF16 = jnp.bfloat16
MIB = 1 << 20


def iota(shape, dim):
    return lax.broadcasted_iota(jnp.int32, shape, dim)


def as_column(row):
    n = row.shape[1]
    eye = iota((n, n), 0) == iota((n, n), 1)
    return jnp.sum(jnp.where(eye, row, jnp.zeros_like(row)), axis=1, keepdims=True)


def as_row(column):
    n = column.shape[0]
    eye = iota((n, n), 0) == iota((n, n), 1)
    return jnp.sum(jnp.where(eye, column, jnp.zeros_like(column)), axis=0, keepdims=True)


def kernel_call(body, outs, ins, limit, flops, moved, scratch=()):
    return pl.pallas_call(
        body,
        out_shape=outs,
        in_specs=ins,
        out_specs=jax.tree.map(lambda _: pl.BlockSpec(memory_space=pltpu.VMEM), outs),
        scratch_shapes=scratch,
        compiler_params=pltpu.CompilerParams(vmem_limit_bytes=limit),
        cost_estimate=pl.CostEstimate(flops=flops, bytes_accessed=moved, transcendentals=0),
    )


VMEM = pl.BlockSpec(memory_space=pltpu.VMEM)
SMEM = pl.BlockSpec(memory_space=pltpu.SMEM)
HBM = pl.BlockSpec(memory_space=pltpu.HBM)


def in_hbm(value):
    return pltpu.with_memory_space_constraint(value, pltpu.HBM)


def project_kernel(hidden_hbm, gain_hbm, weight_hbm, counts, tails, slots, out, hidden, gain, weight, sems):
    chunks = gain.shape[0]
    copies = [
        pltpu.make_async_copy(hidden_hbm, hidden, sems.at[0]),
        pltpu.make_async_copy(gain_hbm, gain, sems.at[1]),
    ]
    blocks = [
        pltpu.make_async_copy(
            weight_hbm.at[c * HD:(c + 1) * HD, :], weight.at[c * HD:(c + 1) * HD, :], sems.at[2 + c]
        )
        for c in range(chunks)
    ]
    for copy in copies + blocks:
        copy.start()
    for copy in copies:
        copy.wait()
    x = hidden[...].astype(F32)
    squares = jnp.sum(x * x, axis=1, keepdims=True)
    y = jnp.zeros((x.shape[0], weight.shape[1]), F32)
    for c in range(chunks):
        scaled = (x[:, c * HD:(c + 1) * HD] * gain[c:c + 1, :]).astype(BF16)
        blocks[c].wait()
        y = y + jnp.dot(scaled, weight[c * HD:(c + 1) * HD, :], preferred_element_type=F32)
    groups, rows, _ = out.shape
    width = weight.shape[1]
    wide = jnp.broadcast_to(squares, (x.shape[0], HD))
    for p in range(groups):
        out[p, :, :width] = y[p * rows:(p + 1) * rows]
        out[p, :, width:] = wide[p * rows:(p + 1) * rows]


def normalise_kernel(parts, counts, tails, slots, keys, values, out, own, info):
    total = parts[0]
    for p in range(1, parts.shape[0]):
        total = total + parts[p]
    width = own.shape[1] * HD
    mean = total[:, width:width + 1] / D
    projected = (total[:, :width] / jnp.sqrt(mean + EPS)).astype(BF16).astype(F32)
    for g in range(own.shape[1]):
        own[:, g, :] = projected[:, g * HD:(g + 1) * HD]
    queries = own[:, :GQ, :].astype(BF16)
    for p in range(out.shape[0]):
        out[p] = queries
    number = counts[...]
    n = number.shape[1]
    below = iota((n, n), 1) <= iota((n, n), 0)
    ends = jnp.sum(jnp.where(below, number, 0), axis=1, keepdims=True)
    count = as_column(number)
    starts = ends - count
    limits = count * CH - as_column(tails[...])
    slot = slots[...]
    owner = jnp.sum((slot >= ends).astype(jnp.int32), axis=0, keepdims=True)
    hits = iota((n, slot.shape[1]), 0) == owner
    first = jnp.sum(jnp.where(hits, starts, 0), axis=0, keepdims=True)
    limit = jnp.sum(jnp.where(hits, limits, 0), axis=0, keepdims=True)
    live = jnp.clip(limit - (slot - first) * CH, 0, CH)
    info[0:1, :] = owner
    info[1:2, :] = jnp.where(owner < n, live, 0)


def attention_kernel(queries, keys, values, info, out, slot_max, slot_sum, slot_value, best, summed, mixed):
    slots = keys.shape[0]
    rows = out.shape[1] // (GQ + 2)
    best[...] = jnp.full(best.shape, NEGATIVE, F32)
    summed[...] = jnp.zeros(summed.shape, F32)
    mixed[...] = jnp.zeros(mixed.shape, F32)
    token = iota((GQ, CH), 1)
    scale = 1.0 / math.sqrt(HD)
    batch = 32

    @pl.loop(0, slots, step=batch)
    def _(base):
        span = [base + u for u in range(batch)]
        scores = [
            lax.dot_general(
                queries[jnp.minimum(info[0, s], REQ - 1)], keys[s], (((1,), (1,)), ((), ())),
                preferred_element_type=F32,
            ) * scale
            for s in span
        ]
        live = [token < info[1, s] for s in span]
        scores = [jnp.where(m, x, NEGATIVE) for m, x in zip(live, scores)]
        tops = [jnp.max(x, axis=1, keepdims=True) for x in scores]
        weights = [jnp.where(m, jnp.exp(x - t), 0.0) for m, x, t in zip(live, scores, tops)]
        totals = [jnp.sum(w, axis=1, keepdims=True) for w in weights]
        mixes = [
            jnp.dot(w.astype(BF16), values[s], preferred_element_type=F32) for w, s in zip(weights, span)
        ]
        for s, top, total, mix in zip(span, tops, totals, mixes):
            slot_max[s] = jnp.broadcast_to(top, (GQ, HD))
            slot_sum[s] = jnp.broadcast_to(total, (GQ, HD))
            slot_value[s] = mix

    step = 8

    @pl.loop(0, slots, step=step)
    def _(base):
        for u in range(step):
            r = info[0, base + u]
            best[r] = jnp.maximum(best[r], slot_max[base + u])

    @pl.loop(0, slots, step=step)
    def _(base):
        for u in range(step):
            s = base + u
            r = info[0, s]
            factor = jnp.exp(slot_max[s] - best[r])
            summed[r] = summed[r] + factor * slot_sum[s]
            mixed[r] = mixed[r] + factor * slot_value[s]

    lane, sub = iota((GQ, HD), 1), iota((GQ, HD), 0)

    @pl.loop(0, out.shape[0])
    def _(p):
        for i in range(rows):
            r = p * rows + i
            out[p, i * GQ:(i + 1) * GQ, :] = mixed[r]
            packed = jnp.where(lane == sub, best[r], 0.0) + jnp.where(lane == sub + GQ, summed[r], 0.0)
            out[p, rows * GQ + i:rows * GQ + i + 1, :] = jnp.sum(packed, axis=0, keepdims=True)


def finish_kernel(parts, own, out, flat, fresh_rows):
    peers, rows = parts.shape[0], own.shape[0]
    lane, sub = iota((GQ, HD), 1), iota((GQ, HD), 0)
    diagonal = lane == sub
    for i in range(rows):
        fresh = jnp.sum(own[i, :GQ, :] * own[i, GQ:GQ + 1, :], axis=1, keepdims=True) / math.sqrt(HD)
        fresh_rows[i:i + 1, :] = jnp.sum(jnp.where(diagonal, fresh, 0.0), axis=0, keepdims=True)
    fresh = fresh_rows[0:rows, :]
    stats = [parts[p, rows * GQ:rows * GQ + rows, :] for p in range(peers)]
    top = fresh
    for p in range(peers):
        top = jnp.maximum(top, stats[p])
    latest = jnp.exp(fresh - top)
    below = latest
    factors = []
    for p in range(peers):
        factor = jnp.exp(stats[p] - top)
        below = below + factor * pltpu.roll(stats[p], HD - GQ, axis=1)
        factors.append(factor)
    for i in range(rows):
        def column(value):
            return jnp.sum(jnp.where(diagonal, value[i:i + 1, :], 0.0), axis=1, keepdims=True)

        above = column(latest) * own[i, GQ + 1:GQ + 2, :]
        for p in range(peers):
            above = above + column(factors[p]) * parts[p, i * GQ:(i + 1) * GQ, :]
        result = above / column(below)
        for g in range(GQ):
            flat[i:i + 1, g * HD:(g + 1) * HD] = result[g:g + 1, :]
    attended = flat[0:rows, :].astype(BF16)
    for p in range(out.shape[0]):
        out[p] = attended


def stacked(blocks, flat):
    peers, rows, _ = blocks.shape
    for p in range(peers):
        flat[p * rows:(p + 1) * rows, :] = blocks[p].astype(F32)


def attention_out_kernel(attended, weight, out, flat):
    stacked(attended, flat)
    out[...] = jnp.dot(flat[...].astype(BF16), weight[...], preferred_element_type=F32)


def mixing_kernel(own, near, far, cross, hidden, gain, request, weight, out, middle, turned):
    total = hidden[...].astype(F32) + ((own[...] + near[...]) + (far[...] + cross[...]))
    inner = total.astype(BF16)
    middle[...] = inner
    n = request.shape[1]
    pick = (as_column(request[...]) == iota((n, n), 1)).astype(F32).astype(BF16)
    ordered = jnp.dot(pick, inner, preferred_element_type=F32)
    squares = jnp.sum(ordered * ordered, axis=1, keepdims=True)
    upper = squares.astype(BF16).astype(F32)
    scaled = jnp.concatenate(
        [(ordered[:, c * HD:(c + 1) * HD] * gain[c:c + 1, :]).astype(BF16) for c in range(gain.shape[0])], axis=1
    )
    groups, height, _ = out.shape
    rows = n // groups
    width = weight.shape[1]
    used = rows * (width // HD)
    step = 4
    for c in range(0, width // HD, step):
        y = jnp.dot(scaled, weight[:, c * HD:(c + step) * HD], preferred_element_type=F32)
        for p in range(groups):
            for k in range(step):
                turned[p, k * rows:(k + 1) * rows, :] = y[p * rows:(p + 1) * rows, k * HD:(k + 1) * HD]
        for p in range(groups):
            out[p, c * rows:(c + step) * rows, :] = turned[p].astype(BF16)
    lane, sub = iota((rows, HD), 1), iota((rows, HD), 0)
    for p in range(groups):
        at = slice(p * rows, (p + 1) * rows)
        both = jnp.where(lane == sub, upper[at], 0.0) + jnp.where(lane == sub + rows, (squares - upper)[at], 0.0)
        line = jnp.sum(both, axis=0, keepdims=True)
        out[p, used:, :] = jnp.where(iota((height - used, HD), 0) == 0, line, 0.0).astype(BF16)


def lightning_kernel(parts, decay, states, gain, out, turned, mixed, flat):
    rows, heads = states.shape[0], states.shape[1]
    used = 4 * rows * heads
    total = parts[0].astype(F32)
    for p in range(1, parts.shape[0]):
        total = total + parts[p].astype(F32)
    line = total[used:used + 1, :]
    sums = line + pltpu.roll(line, HD - rows, axis=1)
    block = 4 * rows
    pattern = iota((block, HD), 1) == lax.rem(iota((block, HD), 0), rows)
    squares = jnp.sum(jnp.where(pattern, sums, 0.0), axis=1, keepdims=True)
    scale = jnp.sqrt(squares / D + EPS)
    keep_row = jnp.exp(-decay[...])
    read_squares = jnp.zeros((rows, 1), F32)
    for h in range(heads):
        mixing = total[block * h:block * (h + 1), :] / scale
        below = 1.0 + jnp.exp(-mixing)
        mixed[h] = mixing / below
        gate = 1.0 / below[3 * rows:, :]
        query, key, value = (mixed[h, k * rows:(k + 1) * rows, :] for k in range(3))
        turned[h] = mixed[h, :2 * rows, :].T
        inner = jnp.sum(query * key, axis=1, keepdims=True)
        keep = keep_row[:, h:h + 1]
        for j in range(rows):
            read = jnp.sum(turned[h, :, j:j + 1] * states[j, h], axis=0, keepdims=True)
            flat[j:j + 1, h * HD:(h + 1) * HD] = keep * read + inner[j:j + 1, :] * value[j:j + 1, :]
        read = flat[0:rows, h * HD:(h + 1) * HD]
        read_squares = read_squares + jnp.sum(read * read, axis=1, keepdims=True)
        flat[0:rows, h * HD:(h + 1) * HD] = read * gain[h:h + 1, :] * gate
    size = heads * HD
    gated = flat[0:rows, 0:size].astype(BF16)
    upper = read_squares.astype(BF16).astype(F32)
    lane = iota((rows, HD), 1)
    tail = jnp.where(lane == 0, upper, jnp.where(lane == 1, read_squares - upper, 0.0)).astype(BF16)
    for p in range(out.shape[0]):
        out[p, :, :size] = gated
        out[p, :, size:] = tail


def renew_kernel(turned, mixed, decay, states, renewed):
    rows, heads = states.shape[0], states.shape[1]
    keep_row = jnp.exp(-decay[...])
    for h in range(heads):
        keep = keep_row[:, h:h + 1]
        for j in range(rows):
            value = mixed[h, 2 * rows + j:2 * rows + j + 1, :]
            renewed[j, h] = keep * states[j, h] + turned[h, :, rows + j:rows + j + 1] * value


def lightning_out_kernel(blocks, request, weight, out, flat):
    stacked(blocks, flat)
    n = request.shape[1]
    size = weight.shape[0]
    pick = (iota((n, n), 0) == request[...]).astype(F32).astype(BF16)
    placed = jnp.dot(pick, flat[...].astype(BF16), preferred_element_type=F32)
    out[0:n, :] = jnp.dot(placed[:, :size].astype(BF16), weight[...], preferred_element_type=F32)
    squares = as_row(placed[:, size:size + 1] + placed[:, size + 1:size + 2])
    out[n:, :] = jnp.zeros((out.shape[0] - n, out.shape[1]), F32)
    out[n:n + 1, 0:n] = squares


def last_kernel(own, near, far, cross, middle, out):
    n = middle.shape[0]
    total = (own[...] + near[...]) + (far[...] + cross[...])
    squares = as_column(total[n:n + 1, 0:n])
    scale = 1.0 / jnp.sqrt(squares / (LH * HD) + EPS)
    out[...] = (middle[...].astype(F32) + total[0:n, :] * scale).astype(BF16)


def exchange(blocks):
    return lax.all_to_all(blocks, "kv", 0, 0, tiled=True)


def head_parts(value):
    size = lax.axis_size("head")
    value = value + lax.ppermute(value, "head", [(i, i ^ 1) for i in range(size)])
    near = lax.ppermute(value, "head", [(i, i ^ 2) for i in range(size)])
    far = lax.ppermute(value, "head", [(i, (3 - i // 2) * 2 + i % 2) for i in range(size)])
    cross = lax.ppermute(value, "head", [(i, i ^ 4) for i in range(size)])
    return value, near, far, cross


def per_device(
    hidden_in,
    attn_gain,
    attn_weight,
    attn_out_weight,
    cache_keys,
    cache_values,
    stretch_counts,
    tail_tokens,
    slot_stretch,
    lin_gain,
    lin_weight,
    decay_rate,
    states,
    out_gain,
    lin_out_weight,
    state_request,
):
    peers = lax.axis_size("kv")
    requests, features = hidden_in.shape
    rows = requests // peers
    width = attn_weight.shape[1]
    slots = cache_keys.shape[0]
    heads = decay_rate.shape[0]
    lin_width = lin_weight.shape[1]
    size = heads * HD
    S = jax.ShapeDtypeStruct
    request = state_request[None, :]

    chunks = features // HD
    keys = cache_keys.reshape(slots, CH, HD)
    values = cache_values.reshape(slots, CH, HD)
    plan = stretch_counts[None, :], tail_tokens[None, :], slot_stretch[None, :]

    parts = kernel_call(
        project_kernel,
        S((peers, rows, width + HD), F32),
        [HBM] * 6, 8 * MIB, 2 * requests * features * width, 2 * features * width,
        [
            pltpu.VMEM((requests, features), BF16),
            pltpu.VMEM((chunks, HD), F32),
            pltpu.VMEM((features, width), BF16),
            pltpu.SemaphoreType.DMA((2 + chunks,)),
        ],
    )(
        in_hbm(hidden_in), in_hbm(attn_gain.reshape(chunks, HD)), in_hbm(attn_weight),
        *(in_hbm(row) for row in plan),
    )
    queries, own, info = kernel_call(
        normalise_kernel,
        (S((peers, rows, GQ, HD), BF16), S((rows, GQ + 2, HD), F32), S((2, slots), jnp.int32)),
        [VMEM] * 4 + [HBM] * 2, 8 * MIB, 0, 8 * peers * rows * width,
    )(
        exchange(parts), *plan, in_hbm(keys), in_hbm(values)
    )
    queries = exchange(queries).reshape(requests, GQ, HD)
    tiles = [pltpu.VMEM((slots, GQ, HD), F32)] * 3 + [pltpu.VMEM((requests + 1, GQ, HD), F32)] * 3
    partial = kernel_call(
        attention_kernel,
        S((peers, rows * (GQ + 2), HD), F32),
        [VMEM, VMEM, VMEM, SMEM], 24 * MIB, 4 * slots * GQ * CH * HD, 4 * slots * CH * HD, tiles,
    )(queries, keys, values, info)
    attended = kernel_call(
        finish_kernel,
        S((peers, rows, GQ * HD), BF16),
        [VMEM, VMEM], 8 * MIB, 0, 8 * peers * rows * GQ * HD,
        [pltpu.VMEM((8, GQ * HD), F32), pltpu.VMEM((8, HD), F32)],
    )(exchange(partial), own)
    first = kernel_call(
        attention_out_kernel,
        S((requests, features), F32),
        [VMEM, VMEM], 8 * MIB, 2 * requests * GQ * HD * features, 2 * GQ * HD * features,
        [pltpu.VMEM((requests, GQ * HD), F32)],
    )(exchange(attended), attn_out_weight)
    height = rows * (lin_width // HD) + 16
    mixing, middle = kernel_call(
        mixing_kernel,
        (S((peers, height, HD), BF16), S((requests, features), BF16)),
        [VMEM] * 8, 16 * MIB, 2 * requests * features * lin_width, 2 * features * lin_width,
        [pltpu.VMEM((peers, 4 * rows, HD), F32)],
    )(*head_parts(first), hidden_in, lin_gain.reshape(chunks, HD), request, lin_weight)
    decay = decay_rate[None, :]
    gated, turned, mixed = kernel_call(
        lightning_kernel,
        (
            S((peers, rows, size + HD), BF16),
            S((heads, HD, 2 * rows), F32),
            S((heads, 4 * rows, HD), F32),
        ),
        [VMEM] * 4, 16 * MIB, 0, 8 * rows * size * HD,
        [pltpu.VMEM((8, size), F32)],
    )(exchange(mixing), decay, states, out_gain.reshape(heads, HD))
    second = kernel_call(
        lightning_out_kernel,
        S((requests + 8, features), F32),
        [VMEM] * 3, 8 * MIB, 2 * requests * size * features, 2 * size * features,
        [pltpu.VMEM((requests, size + HD), F32)],
    )(exchange(gated), request, lin_out_weight)
    renewed = kernel_call(
        renew_kernel, S(states.shape, F32), [VMEM] * 4, 8 * MIB, 0, 8 * rows * size * HD,
    )(turned, mixed, decay, states)
    hidden_out = kernel_call(
        last_kernel,
        S((requests, features), BF16),
        [VMEM] * 5, 4 * MIB, 0, 16 * requests * features,
    )(*head_parts(second), middle)
    return hidden_out, renewed


def solution(mesh):
    placed = (
        P(None, "kv"),
        P("kv"),
        P("kv", "head"),
        P("head", "kv"),
        P("kv", "head", None, None),
        P("kv", "head", None, None),
        P(),
        P(),
        P("kv"),
        P("kv"),
        P("kv", "head"),
        P("head"),
        P("kv", "head", None, None),
        P("head"),
        P("head", "kv"),
        P(),
    )
    return jax.shard_map(
        per_device,
        mesh=mesh,
        in_specs=placed,
        out_specs=(P(None, "kv"), P("kv", "head", None, None)),
        check_vma=False,
    )
```

```python
import functools
import math

import jax
import jax.numpy as jnp
from jax import lax
from jax.experimental import pallas as pl
from jax.experimental.pallas import tpu as pltpu
from jax.sharding import PartitionSpec as P

D = 6144
HD = 128
LH = 64
CH = 256
GQ = 8
REQ = 64
EPS = 1e-05
NEGATIVE = -1e30
F32 = jnp.float32
BF16 = jnp.bfloat16
MIB = 1 << 20


def iota(shape, dim):
    return lax.broadcasted_iota(jnp.int32, shape, dim)


def as_column(row):
    n = row.shape[1]
    eye = iota((n, n), 0) == iota((n, n), 1)
    return jnp.sum(jnp.where(eye, row, jnp.zeros_like(row)), axis=1, keepdims=True)


def as_row(column):
    n = column.shape[0]
    eye = iota((n, n), 0) == iota((n, n), 1)
    return jnp.sum(jnp.where(eye, column, jnp.zeros_like(column)), axis=0, keepdims=True)


def kernel_call(body, outs, ins, limit, flops, moved, scratch=()):
    return pl.pallas_call(
        body,
        out_shape=outs,
        in_specs=ins,
        out_specs=jax.tree.map(lambda _: pl.BlockSpec(memory_space=pltpu.VMEM), outs),
        scratch_shapes=scratch,
        compiler_params=pltpu.CompilerParams(vmem_limit_bytes=limit),
        cost_estimate=pl.CostEstimate(flops=flops, bytes_accessed=moved, transcendentals=0),
    )


VMEM = pl.BlockSpec(memory_space=pltpu.VMEM)
SMEM = pl.BlockSpec(memory_space=pltpu.SMEM)
HBM = pl.BlockSpec(memory_space=pltpu.HBM)


def in_hbm(value):
    return pltpu.with_memory_space_constraint(value, pltpu.HBM)


def halves(value):
    upper = value.astype(BF16).astype(F32)
    return upper, (value - upper).astype(BF16).astype(F32)


def project_kernel(
    hidden_hbm, gain_hbm, weight_hbm, counts_hbm, tails_hbm, slots_hbm, out, info,
    hidden, gain, weight, counts, tails, slots, sems,
):
    chunks = gain.shape[0]
    first = [(hidden_hbm, hidden), (gain_hbm, gain)]
    blocks = [
        (weight_hbm.at[c * HD:(c + 1) * HD, :], weight.at[c * HD:(c + 1) * HD, :]) for c in range(chunks)
    ]
    last = [(counts_hbm, counts), (tails_hbm, tails), (slots_hbm, slots)]
    copies = [
        pltpu.make_async_copy(source, target, sems.at[k])
        for k, (source, target) in enumerate(first + blocks + last)
    ]
    for copy in copies:
        copy.start()
    for copy in copies[:2] + copies[2 + chunks:]:
        copy.wait()
    x = hidden[...].astype(F32)
    squares = jnp.sum(x * x, axis=1, keepdims=True)
    scaled = [(x[:, c * HD:(c + 1) * HD] * gain[c:c + 1, :]).astype(BF16) for c in range(chunks)]
    number = counts[...]
    n = number.shape[1]
    below = iota((n, n), 1) <= iota((n, n), 0)
    ends = jnp.sum(jnp.where(below, number, 0), axis=1, keepdims=True)
    count = as_column(number)
    starts = ends - count
    limits = count * CH - as_column(tails[...])
    slot = slots[...]
    owner = jnp.sum((slot >= ends).astype(jnp.int32), axis=0, keepdims=True)
    hits = iota((n, slot.shape[1]), 0) == owner
    begin = jnp.sum(jnp.where(hits, starts, 0), axis=0, keepdims=True)
    limit = jnp.sum(jnp.where(hits, limits, 0), axis=0, keepdims=True)
    live = jnp.clip(limit - (slot - begin) * CH, 0, CH)
    info[0:1, :] = owner
    info[1:2, :] = jnp.where(owner < n, live, 0)
    y = jnp.zeros((x.shape[0], weight.shape[1]), F32)
    for c in range(chunks):
        copies[2 + c].wait()
        y = y + jnp.dot(scaled[c], weight[c * HD:(c + 1) * HD, :], preferred_element_type=F32)
    groups, rows, _ = out.shape
    width = weight.shape[1]
    wide = jnp.broadcast_to(squares, (x.shape[0], HD))
    for p in range(groups):
        out[p, :, :width] = y[p * rows:(p + 1) * rows]
        out[p, :, width:] = wide[p * rows:(p + 1) * rows]


def normalise_kernel(parts, keys, values, out, own):
    total = parts[0]
    for p in range(1, parts.shape[0]):
        total = total + parts[p]
    width = own.shape[1] * HD
    mean = total[:, width:width + 1] / D
    projected = (total[:, :width] / jnp.sqrt(mean + EPS)).astype(BF16).astype(F32)
    for g in range(own.shape[1]):
        own[:, g, :] = projected[:, g * HD:(g + 1) * HD]
    queries = own[:, :GQ, :].astype(BF16)
    for p in range(out.shape[0]):
        out[p] = queries


def attention_kernel(queries, keys, values, info, out, slot_max, slot_sum, slot_value, best, summed, mixed):
    slots = keys.shape[0]
    rows = REQ // out.shape[0]
    best[...] = jnp.full(best.shape, NEGATIVE, F32)
    summed[...] = jnp.zeros(summed.shape, F32)
    mixed[...] = jnp.zeros(mixed.shape, F32)
    token = iota((GQ, CH), 1)
    scale = 1.0 / math.sqrt(HD)
    batch = 32

    @pl.loop(0, slots, step=batch)
    def _(base):
        span = [base + u for u in range(batch)]
        owners = [info[0, s] for s in span]
        scores = [
            lax.dot_general(
                queries[jnp.minimum(r, REQ - 1)], keys[s], (((1,), (1,)), ((), ())),
                preferred_element_type=F32,
            ) * scale
            for r, s in zip(owners, span)
        ]
        live = [token < info[1, s] for s in span]
        scores = [jnp.where(m, x, NEGATIVE) for m, x in zip(live, scores)]
        tops = [jnp.max(x, axis=1, keepdims=True) for x in scores]
        weights = [jnp.where(m, jnp.exp(x - t), 0.0) for m, x, t in zip(live, scores, tops)]
        totals = [jnp.sum(w, axis=1, keepdims=True) for w in weights]
        mixes = [
            jnp.dot(w.astype(BF16), values[s], preferred_element_type=F32) for w, s in zip(weights, span)
        ]
        for r, s, top, total, mix in zip(owners, span, tops, totals, mixes):
            wide = jnp.broadcast_to(top, (GQ, HD))
            best[r] = jnp.maximum(best[r], wide)
            slot_max[s] = wide
            slot_sum[s] = jnp.broadcast_to(total, (GQ, HD))
            slot_value[s] = mix

    upper, lower = halves(best[...])
    best[...] = upper + lower
    step = 8

    @pl.loop(0, slots, step=step)
    def _(base):
        for u in range(step):
            s = base + u
            r = info[0, s]
            factor = jnp.exp(slot_max[s] - best[r])
            summed[r] = summed[r] + factor * slot_sum[s]
            mixed[r] = mixed[r] + factor * slot_value[s]

    lane, sub = iota((GQ, HD), 1), iota((GQ, HD), 0)
    line = iota((2 * GQ, HD), 0)

    @pl.loop(0, out.shape[0])
    def _(p):
        stats = jnp.zeros((2 * GQ, HD), F32)
        for i in range(rows):
            r = p * rows + i
            packed = jnp.zeros((GQ, HD), F32)
            for k, part in enumerate(halves(best[r]) + halves(summed[r])):
                packed = jnp.where(lane == sub + k * GQ, part, packed)
            stats = jnp.where(line == i, jnp.sum(packed, axis=0, keepdims=True), stats)
        out[p, :rows * GQ, :] = mixed[pl.ds(p * rows, rows)].reshape(rows * GQ, HD).astype(BF16)
        out[p, rows * GQ:, :] = stats.astype(BF16)


def finish_kernel(parts, own, out, flat, fresh_rows):
    peers, rows = parts.shape[0], own.shape[0]
    lane, sub = iota((GQ, HD), 1), iota((GQ, HD), 0)
    diagonal = lane == sub
    for i in range(rows):
        fresh = jnp.sum(own[i, :GQ, :] * own[i, GQ:GQ + 1, :], axis=1, keepdims=True) / math.sqrt(HD)
        fresh_rows[i:i + 1, :] = jnp.sum(jnp.where(diagonal, fresh, 0.0), axis=0, keepdims=True)
    fresh = fresh_rows[0:rows, :]
    lines = [parts[p, rows * GQ:, :].astype(F32)[0:rows] for p in range(peers)]
    tops = [x + pltpu.roll(x, HD - GQ, axis=1) for x in lines]
    sums = [pltpu.roll(x, HD - 2 * GQ, axis=1) for x in tops]
    top = fresh
    for p in range(peers):
        top = jnp.maximum(top, tops[p])
    latest = jnp.exp(fresh - top)
    below = latest
    factors = [jnp.exp(x - top) for x in tops]
    for p in range(peers):
        below = below + factors[p] * sums[p]

    def column(value, i):
        return jnp.sum(jnp.where(diagonal, value[i:i + 1, :], 0.0), axis=1, keepdims=True)

    above = [column(latest, i) * own[i, GQ + 1:GQ + 2, :] for i in range(rows)]
    for p in range(peers):
        values = parts[p, :rows * GQ, :].astype(F32)
        for i in range(rows):
            above[i] = above[i] + column(factors[p], i) * values[i * GQ:(i + 1) * GQ]
    for i in range(rows):
        result = above[i] / column(below, i)
        for g in range(GQ):
            flat[i:i + 1, g * HD:(g + 1) * HD] = result[g:g + 1, :]
    attended = flat[0:rows, :].astype(BF16)
    for p in range(out.shape[0]):
        out[p] = attended


def stacked(blocks, flat):
    peers, rows, _ = blocks.shape
    for p in range(peers):
        flat[p * rows:(p + 1) * rows, :] = blocks[p].astype(F32)


def four(own, near, far, cross):
    return (own[...].astype(F32) + near[...].astype(F32)) + (far[...].astype(F32) + cross[...].astype(F32))


def attention_out_kernel(attended, weight, out, flat):
    stacked(attended, flat)
    out[...] = jnp.dot(flat[...].astype(BF16), weight[...], preferred_element_type=F32)


def mixing_kernel(own, near, far, cross, hidden, gain, request, weight, out, middle, turned):
    total = hidden[...].astype(F32) + four(own, near, far, cross)
    inner = total.astype(BF16)
    middle[...] = inner
    n = request.shape[1]
    pick = (as_column(request[...]) == iota((n, n), 1)).astype(F32).astype(BF16)
    ordered = jnp.dot(pick, inner, preferred_element_type=F32)
    squares = jnp.sum(ordered * ordered, axis=1, keepdims=True)
    upper = squares.astype(BF16).astype(F32)
    scaled = jnp.concatenate(
        [(ordered[:, c * HD:(c + 1) * HD] * gain[c:c + 1, :]).astype(BF16) for c in range(gain.shape[0])], axis=1
    )
    groups, height, _ = out.shape
    rows = n // groups
    width = weight.shape[1]
    used = rows * (width // HD)
    step = 4
    for c in range(0, width // HD, step):
        y = jnp.dot(scaled, weight[:, c * HD:(c + step) * HD], preferred_element_type=F32)
        for p in range(groups):
            for k in range(step):
                turned[p, k * rows:(k + 1) * rows, :] = y[p * rows:(p + 1) * rows, k * HD:(k + 1) * HD]
        for p in range(groups):
            out[p, c * rows:(c + step) * rows, :] = turned[p].astype(BF16)
    lane, sub = iota((rows, HD), 1), iota((rows, HD), 0)
    for p in range(groups):
        at = slice(p * rows, (p + 1) * rows)
        both = jnp.where(lane == sub, upper[at], 0.0) + jnp.where(lane == sub + rows, (squares - upper)[at], 0.0)
        line = jnp.sum(both, axis=0, keepdims=True)
        out[p, used:, :] = jnp.where(iota((height - used, HD), 0) == 0, line, 0.0).astype(BF16)


def lightning_kernel(parts, decay, states, gain, out, turned, mixed, flat):
    rows, heads = states.shape[0], states.shape[1]
    used = 4 * rows * heads
    total = parts[0].astype(F32)
    for p in range(1, parts.shape[0]):
        total = total + parts[p].astype(F32)
    line = total[used:used + 1, :]
    sums = line + pltpu.roll(line, HD - rows, axis=1)
    block = 4 * rows
    pattern = iota((block, HD), 1) == lax.rem(iota((block, HD), 0), rows)
    squares = jnp.sum(jnp.where(pattern, sums, 0.0), axis=1, keepdims=True)
    scale = jnp.sqrt(squares / D + EPS)
    keep = jnp.exp(-decay[...])
    span = range(heads)
    mixing = [total[block * h:block * (h + 1), :] / scale for h in span]
    below = [1.0 + jnp.exp(-m) for m in mixing]
    silu = [m / b for m, b in zip(mixing, below)]
    gates = [1.0 / b[3 * rows:] for b in below]
    columns = [v[:2 * rows].T for v in silu]
    for h in span:
        mixed[h] = silu[h]
        turned[h] = columns[h]
    inner = [jnp.sum(v[:rows] * v[rows:2 * rows], axis=1, keepdims=True) for v in silu]
    for j in range(rows):
        for h in span:
            read = jnp.sum(columns[h][:, j:j + 1] * states[j, h], axis=0, keepdims=True)
            flat[j:j + 1, h * HD:(h + 1) * HD] = read
    read_squares = jnp.zeros((rows, 1), F32)
    for h in span:
        at = slice(h * HD, (h + 1) * HD)
        read = keep[:, h:h + 1] * flat[0:rows, at] + inner[h] * silu[h][2 * rows:3 * rows]
        read_squares = read_squares + jnp.sum(read * read, axis=1, keepdims=True)
        flat[0:rows, at] = read * gain[h:h + 1, :] * gates[h]
    size = heads * HD
    gated = flat[0:rows, 0:size].astype(BF16)
    upper, lower = halves(read_squares)
    lane = iota((rows, HD), 1)
    tail = jnp.where(lane == 0, upper, jnp.where(lane == 1, lower, 0.0)).astype(BF16)
    for p in range(out.shape[0]):
        out[p, :, :size] = gated
        out[p, :, size:] = tail


def renew_kernel(turned, mixed, decay, states, renewed):
    rows, heads = states.shape[0], states.shape[1]
    keep_row = jnp.exp(-decay[...])
    for h in range(heads):
        keep = keep_row[:, h:h + 1]
        for j in range(rows):
            value = mixed[h, 2 * rows + j:2 * rows + j + 1, :]
            renewed[j, h] = keep * states[j, h] + turned[h, :, rows + j:rows + j + 1] * value


def lightning_out_kernel(blocks, request, weight, out, flat):
    stacked(blocks, flat)
    n = request.shape[1]
    size = weight.shape[0]
    pick = (iota((n, n), 0) == request[...]).astype(F32).astype(BF16)
    placed = jnp.dot(pick, flat[...].astype(BF16), preferred_element_type=F32)
    out[0:n, :] = jnp.dot(placed[:, :size].astype(BF16), weight[...], preferred_element_type=F32)
    squares = as_row(placed[:, size:size + 1] + placed[:, size + 1:size + 2])
    out[n:, :] = jnp.zeros((out.shape[0] - n, out.shape[1]), F32)
    out[n:n + 1, 0:n] = squares


def pair_kernel(own, near, out):
    n = own.shape[0] - 8
    total = own[...] + near[...]
    out[0:n, :] = total[0:n].astype(BF16)
    upper, lower = halves(total[n:n + 1])
    line = iota((out.shape[0] - n, out.shape[1]), 0)
    out[n:, :] = jnp.where(line == 0, upper, jnp.where(line == 1, lower, 0.0)).astype(BF16)


def last_kernel(own, near, far, cross, middle, out):
    n = middle.shape[0]
    total = four(own, near, far, cross)
    squares = as_column(total[n:n + 1, 0:n] + total[n + 1:n + 2, 0:n])
    scale = 1.0 / jnp.sqrt(squares / (LH * HD) + EPS)
    out[...] = (middle[...].astype(F32) + total[0:n, :] * scale).astype(BF16)


def exchange(blocks):
    return lax.all_to_all(blocks, "kv", 0, 0, tiled=True)


def other_core(value):
    return lax.ppermute(value, "head", [(i, i ^ 1) for i in range(lax.axis_size("head"))])


def along_z(value):
    size = lax.axis_size("head")
    near = lax.ppermute(value, "head", [(i, i ^ 2) for i in range(size)])
    far = lax.ppermute(value, "head", [(i, (3 - i // 2) * 2 + i % 2) for i in range(size)])
    cross = lax.ppermute(value, "head", [(i, i ^ 4) for i in range(size)])
    return value, near, far, cross


def per_device(
    hidden_in,
    attn_gain,
    attn_weight,
    attn_out_weight,
    cache_keys,
    cache_values,
    stretch_counts,
    tail_tokens,
    slot_stretch,
    lin_gain,
    lin_weight,
    decay_rate,
    states,
    out_gain,
    lin_out_weight,
    state_request,
):
    peers = lax.axis_size("kv")
    requests, features = hidden_in.shape
    rows = requests // peers
    width = attn_weight.shape[1]
    slots = cache_keys.shape[0]
    heads = decay_rate.shape[0]
    lin_width = lin_weight.shape[1]
    size = heads * HD
    S = jax.ShapeDtypeStruct
    request = state_request[None, :]

    chunks = features // HD
    keys = cache_keys.reshape(slots, CH, HD)
    values = cache_values.reshape(slots, CH, HD)
    plan = stretch_counts[None, :], tail_tokens[None, :], slot_stretch[None, :]

    parts, info = kernel_call(
        project_kernel,
        (S((peers, rows, width + HD), F32), S((2, slots), jnp.int32)),
        [HBM] * 6, 8 * MIB, 2 * requests * features * width, 2 * features * width,
        [
            pltpu.VMEM((requests, features), BF16),
            pltpu.VMEM((chunks, HD), F32),
            pltpu.VMEM((features, width), BF16),
            pltpu.VMEM((1, requests), jnp.int32),
            pltpu.VMEM((1, requests), jnp.int32),
            pltpu.VMEM((1, slots), jnp.int32),
            pltpu.SemaphoreType.DMA((5 + chunks,)),
        ],
    )(
        in_hbm(hidden_in), in_hbm(attn_gain.reshape(chunks, HD)), in_hbm(attn_weight),
        *(in_hbm(row) for row in plan),
    )
    queries, own = kernel_call(
        normalise_kernel,
        (S((peers, rows, GQ, HD), BF16), S((rows, GQ + 2, HD), F32)),
        [VMEM] + [HBM] * 2, 8 * MIB, 0, 8 * peers * rows * width,
    )(
        exchange(parts), in_hbm(keys), in_hbm(values)
    )
    queries = exchange(queries).reshape(requests, GQ, HD)
    tiles = [pltpu.VMEM((slots, GQ, HD), F32)] * 3 + [pltpu.VMEM((requests + 1, GQ, HD), F32)] * 3
    partial = kernel_call(
        attention_kernel,
        S((peers, rows * GQ + 16, HD), BF16),
        [VMEM, VMEM, VMEM, SMEM], 24 * MIB, 4 * slots * GQ * CH * HD, 4 * slots * CH * HD, tiles,
    )(queries, keys, values, info)
    attended = kernel_call(
        finish_kernel,
        S((peers, rows, GQ * HD), BF16),
        [VMEM, VMEM], 8 * MIB, 0, 8 * peers * rows * GQ * HD,
        [pltpu.VMEM((8, GQ * HD), F32), pltpu.VMEM((8, HD), F32)],
    )(exchange(partial), own)
    first = kernel_call(
        attention_out_kernel,
        S((requests, features), F32),
        [VMEM, VMEM], 8 * MIB, 2 * requests * GQ * HD * features, 2 * GQ * HD * features,
        [pltpu.VMEM((requests, GQ * HD), F32)],
    )(exchange(attended), attn_out_weight)
    height = rows * (lin_width // HD) + 16
    mixing, middle = kernel_call(
        mixing_kernel,
        (S((peers, height, HD), BF16), S((requests, features), BF16)),
        [VMEM] * 8, 16 * MIB, 2 * requests * features * lin_width, 2 * features * lin_width,
        [pltpu.VMEM((peers, 4 * rows, HD), F32)],
    )(*along_z((first + other_core(first)).astype(BF16)), hidden_in, lin_gain.reshape(chunks, HD), request, lin_weight)
    decay = decay_rate[None, :]
    gated, turned, mixed = kernel_call(
        lightning_kernel,
        (
            S((peers, rows, size + HD), BF16),
            S((heads, HD, 2 * rows), F32),
            S((heads, 4 * rows, HD), F32),
        ),
        [VMEM] * 4, 16 * MIB, 0, 8 * rows * size * HD,
        [pltpu.VMEM((8, size), F32)],
    )(exchange(mixing), decay, states, out_gain.reshape(heads, HD))
    second = kernel_call(
        lightning_out_kernel,
        S((requests + 8, features), F32),
        [VMEM] * 3, 8 * MIB, 2 * requests * size * features, 2 * size * features,
        [pltpu.VMEM((requests, size + HD), F32)],
    )(exchange(gated), request, lin_out_weight)
    pair = kernel_call(
        pair_kernel, S((requests + 16, features), BF16), [VMEM] * 2, 4 * MIB, 0, 16 * requests * features,
    )(second, other_core(second))
    renewed = kernel_call(
        renew_kernel, S(states.shape, F32), [VMEM] * 4, 8 * MIB, 0, 8 * rows * size * HD,
    )(turned, mixed, decay, states)
    hidden_out = kernel_call(
        last_kernel,
        S((requests, features), BF16),
        [VMEM] * 5, 4 * MIB, 0, 16 * requests * features,
    )(*along_z(pair), middle)
    return hidden_out, renewed


def solution(mesh):
    placed = (
        P(None, "kv"),
        P("kv"),
        P("kv", "head"),
        P("head", "kv"),
        P("kv", "head", None, None),
        P("kv", "head", None, None),
        P(),
        P(),
        P("kv"),
        P("kv"),
        P("kv", "head"),
        P("head"),
        P("kv", "head", None, None),
        P("head"),
        P("head", "kv"),
        P(),
    )
    return jax.shard_map(
        per_device,
        mesh=mesh,
        in_specs=placed,
        out_specs=(P(None, "kv"), P("kv", "head", None, None)),
        check_vma=False,
    )
```

```python
import functools
import math

import jax
import jax.numpy as jnp
from jax import lax
from jax.experimental import pallas as pl
from jax.experimental.pallas import tpu as pltpu
from jax.sharding import PartitionSpec as P

D = 6144
HD = 128
LH = 64
CH = 256
GQ = 8
REQ = 64
EPS = 1e-05
NEGATIVE = -1e30
F32 = jnp.float32
BF16 = jnp.bfloat16
MIB = 1 << 20
LINES = 16


def iota(shape, dim):
    return lax.broadcasted_iota(jnp.int32, shape, dim)


def as_column(row):
    n = row.shape[1]
    eye = iota((n, n), 0) == iota((n, n), 1)
    return jnp.sum(jnp.where(eye, row, jnp.zeros_like(row)), axis=1, keepdims=True)


def as_row(column):
    n = column.shape[0]
    eye = iota((n, n), 0) == iota((n, n), 1)
    return jnp.sum(jnp.where(eye, column, jnp.zeros_like(column)), axis=0, keepdims=True)


def kernel_call(body, outs, ins, limit, flops, moved, scratch=()):
    return pl.pallas_call(
        body,
        out_shape=outs,
        in_specs=ins,
        out_specs=jax.tree.map(lambda _: pl.BlockSpec(memory_space=pltpu.VMEM), outs),
        scratch_shapes=scratch,
        compiler_params=pltpu.CompilerParams(vmem_limit_bytes=limit),
        cost_estimate=pl.CostEstimate(flops=flops, bytes_accessed=moved, transcendentals=0),
    )


VMEM = pl.BlockSpec(memory_space=pltpu.VMEM)
SMEM = pl.BlockSpec(memory_space=pltpu.SMEM)
HBM = pl.BlockSpec(memory_space=pltpu.HBM)


def in_hbm(value):
    return pltpu.with_memory_space_constraint(value, pltpu.HBM)


def halves(value):
    upper = value.astype(BF16).astype(F32)
    return upper, (value - upper).astype(BF16).astype(F32)


def project_kernel(
    hidden_hbm, gain_hbm, weight_hbm, counts_hbm, tails_hbm, slots_hbm, out, info,
    hidden, gain, weight, counts, tails, slots, sems,
):
    chunks = gain.shape[0]
    first = [(hidden_hbm, hidden), (gain_hbm, gain)]
    blocks = [
        (weight_hbm.at[c * HD:(c + 1) * HD, :], weight.at[c * HD:(c + 1) * HD, :]) for c in range(chunks)
    ]
    last = [(counts_hbm, counts), (tails_hbm, tails), (slots_hbm, slots)]
    copies = [
        pltpu.make_async_copy(source, target, sems.at[k])
        for k, (source, target) in enumerate(first + blocks + last)
    ]
    for copy in copies:
        copy.start()
    for copy in copies[:2] + copies[2 + chunks:]:
        copy.wait()
    x = hidden[...].astype(F32)
    squares = jnp.sum(x * x, axis=1, keepdims=True)
    scaled = [(x[:, c * HD:(c + 1) * HD] * gain[c:c + 1, :]).astype(BF16) for c in range(chunks)]
    number = counts[...]
    n = number.shape[1]
    below = iota((n, n), 1) <= iota((n, n), 0)
    ends = jnp.sum(jnp.where(below, number, 0), axis=1, keepdims=True)
    count = as_column(number)
    starts = ends - count
    limits = count * CH - as_column(tails[...])
    slot = slots[...]
    owner = jnp.sum((slot >= ends).astype(jnp.int32), axis=0, keepdims=True)
    hits = iota((n, slot.shape[1]), 0) == owner
    begin = jnp.sum(jnp.where(hits, starts, 0), axis=0, keepdims=True)
    limit = jnp.sum(jnp.where(hits, limits, 0), axis=0, keepdims=True)
    live = jnp.clip(limit - (slot - begin) * CH, 0, CH)
    info[0:1, :] = owner
    info[1:2, :] = jnp.where(owner < n, live, 0)
    y = jnp.zeros((x.shape[0], weight.shape[1]), F32)
    for c in range(chunks):
        copies[2 + c].wait()
        y = y + jnp.dot(scaled[c], weight[c * HD:(c + 1) * HD, :], preferred_element_type=F32)
    groups, rows, _ = out.shape
    width = weight.shape[1]
    wide = jnp.broadcast_to(squares, (x.shape[0], HD))
    for p in range(groups):
        out[p, :, :width] = y[p * rows:(p + 1) * rows]
        out[p, :, width:] = wide[p * rows:(p + 1) * rows]


def normalise_kernel(parts, keys, values, out, own):
    total = parts[0]
    for p in range(1, parts.shape[0]):
        total = total + parts[p]
    width = own.shape[1] * HD
    mean = total[:, width:width + 1] / D
    projected = (total[:, :width] / jnp.sqrt(mean + EPS)).astype(BF16).astype(F32)
    for g in range(own.shape[1]):
        own[:, g, :] = projected[:, g * HD:(g + 1) * HD]
    queries = own[:, :GQ, :].astype(BF16)
    for p in range(out.shape[0]):
        out[p] = queries


def attention_kernel(queries, keys, values, info, own, out, slot_max, slot_sum, slot_value, best, summed, mixed):
    slots, rows = keys.shape[0], own.shape[0]
    best[...] = jnp.full(best.shape, NEGATIVE, F32)
    summed[...] = jnp.zeros(summed.shape, F32)
    mixed[...] = jnp.zeros(mixed.shape, F32)
    token = iota((GQ, CH), 1)
    scale = 1.0 / math.sqrt(HD)
    batch = 32
    mine = lax.axis_index("kv") * rows

    @pl.loop(0, slots, step=batch)
    def _(base):
        span = [base + u for u in range(batch)]
        owners = [info[0, s] for s in span]
        scores = [
            lax.dot_general(
                queries[jnp.minimum(r, REQ - 1)], keys[s], (((1,), (1,)), ((), ())),
                preferred_element_type=F32,
            ) * scale
            for r, s in zip(owners, span)
        ]
        live = [token < info[1, s] for s in span]
        scores = [jnp.where(m, x, NEGATIVE) for m, x in zip(live, scores)]
        tops = [jnp.max(x, axis=1, keepdims=True) for x in scores]
        weights = [jnp.where(m, jnp.exp(x - t), 0.0) for m, x, t in zip(live, scores, tops)]
        totals = [jnp.sum(w, axis=1, keepdims=True) for w in weights]
        mixes = [
            jnp.dot(w.astype(BF16), values[s], preferred_element_type=F32) for w, s in zip(weights, span)
        ]
        for r, s, top, total, mix in zip(owners, span, tops, totals, mixes):
            wide = jnp.broadcast_to(top, (GQ, HD))
            best[r] = jnp.maximum(best[r], wide)
            slot_max[s] = wide
            slot_sum[s] = jnp.broadcast_to(total, (GQ, HD))
            slot_value[s] = mix

    fresh = [
        jnp.broadcast_to(
            jnp.sum(own[i, :GQ, :] * own[i, GQ:GQ + 1, :], axis=1, keepdims=True) / math.sqrt(HD), (GQ, HD)
        )
        for i in range(rows)
    ]
    for i in range(rows):
        best[mine + i] = jnp.maximum(best[mine + i], fresh[i])
    upper, lower = halves(best[...])
    best[...] = upper + lower
    for i in range(rows):
        factor = jnp.exp(fresh[i] - best[mine + i])
        summed[mine + i] = factor
        mixed[mine + i] = factor * own[i, GQ + 1:GQ + 2, :]
    step = 8

    @pl.loop(0, slots, step=step)
    def _(base):
        for u in range(step):
            s = base + u
            r = info[0, s]
            factor = jnp.exp(slot_max[s] - best[r])
            summed[r] = summed[r] + factor * slot_sum[s]
            mixed[r] = mixed[r] + factor * slot_value[s]

    lane, sub = iota((GQ, HD), 1), iota((GQ, HD), 0)
    line = iota((LINES, HD), 0)
    stats = jnp.zeros((LINES, HD), F32)
    for i in range(LINES):
        packed = jnp.zeros((GQ, HD), F32)
        for c in range(REQ // LINES):
            r = c * LINES + i
            for k, part in enumerate(halves(best[r]) + halves(summed[r])):
                packed = jnp.where(lane == sub + (4 * c + k) * GQ, part, packed)
        stats = jnp.where(line == i, jnp.sum(packed, axis=0, keepdims=True), stats)
    out[:REQ * GQ, :] = mixed[0:REQ].reshape(REQ * GQ, HD).astype(BF16)
    out[REQ * GQ:, :] = stats.astype(BF16)


def merge_weights(parts):
    lines = [part[REQ * GQ:, :].astype(F32) for part in parts]
    tops = [x + pltpu.roll(x, HD - GQ, axis=1) for x in lines]
    sums = [pltpu.roll(x, HD - 2 * GQ, axis=1) for x in tops]
    top = jnp.maximum(jnp.maximum(tops[0], tops[1]), jnp.maximum(tops[2], tops[3]))
    factors = [jnp.exp(x - top) for x in tops]
    terms = [f * x for f, x in zip(factors, sums)]
    return top, factors, (terms[0] + terms[1]) + (terms[2] + terms[3])


def weighted(parts, factors, store):
    columns = [f.T for f in factors]
    for r in range(0, REQ, 2):
        c, i = r // LINES, r % LINES
        blocks = [part[r * GQ:(r + 2) * GQ, :].astype(F32) for part in parts]
        pair = []
        for u in range(2):
            at = slice(4 * c * GQ, (4 * c + 1) * GQ)
            terms = [t[at, i + u:i + u + 1] * b[u * GQ:(u + 1) * GQ] for t, b in zip(columns, blocks)]
            pair.append((terms[0] + terms[1]) + (terms[2] + terms[3]))
        store(r, jnp.concatenate(pair, axis=0))


def merge_kernel(own, near, far, cross, out):
    parts = own, near, far, cross
    top, factors, total = merge_weights(parts)

    def store(r, value):
        out[r * GQ:(r + 2) * GQ, :] = value.astype(BF16)

    weighted(parts, factors, store)
    place = lax.rem(iota((LINES, HD), 1), 4 * GQ)
    packed = jnp.zeros((LINES, HD), F32)
    for k, part in enumerate(halves(top) + halves(total)):
        moved = part if k == 0 else pltpu.roll(part, k * GQ, axis=1)
        packed = jnp.where((place >= k * GQ) & (place < (k + 1) * GQ), moved, packed)
    out[REQ * GQ:, :] = packed.astype(BF16)


def attention_out_kernel(own, near, far, cross, weight, out, tall, flat):
    parts = own, near, far, cross
    _, factors, total = merge_weights(parts)

    def store(r, value):
        tall[r * GQ:(r + 2) * GQ, :] = value

    weighted(parts, [f / total for f in factors], store)
    for g in range(GQ):
        flat[:, g * HD:(g + 1) * HD] = tall[pl.ds(g, REQ, stride=GQ), :].astype(BF16)
    out[...] = jnp.dot(flat[...], weight[...], preferred_element_type=F32)


def stacked(blocks, flat):
    peers, rows, _ = blocks.shape
    for p in range(peers):
        flat[p * rows:(p + 1) * rows, :] = blocks[p].astype(F32)


def four(own, near, far, cross):
    return (own[...].astype(F32) + near[...].astype(F32)) + (far[...].astype(F32) + cross[...].astype(F32))


def mixing_kernel(own, near, far, cross, hidden, gain, request, weight, out, middle, turned):
    total = hidden[...].astype(F32) + four(own, near, far, cross)
    inner = total.astype(BF16)
    middle[...] = inner
    n = request.shape[1]
    pick = (as_column(request[...]) == iota((n, n), 1)).astype(F32).astype(BF16)
    ordered = jnp.dot(pick, inner, preferred_element_type=F32)
    squares = jnp.sum(ordered * ordered, axis=1, keepdims=True)
    upper = squares.astype(BF16).astype(F32)
    scaled = jnp.concatenate(
        [(ordered[:, c * HD:(c + 1) * HD] * gain[c:c + 1, :]).astype(BF16) for c in range(gain.shape[0])], axis=1
    )
    groups, height, _ = out.shape
    rows = n // groups
    width = weight.shape[1]
    used = rows * (width // HD)
    step = 4
    for c in range(0, width // HD, step):
        y = jnp.dot(scaled, weight[:, c * HD:(c + step) * HD], preferred_element_type=F32)
        for p in range(groups):
            for k in range(step):
                turned[p, k * rows:(k + 1) * rows, :] = y[p * rows:(p + 1) * rows, k * HD:(k + 1) * HD]
        for p in range(groups):
            out[p, c * rows:(c + step) * rows, :] = turned[p].astype(BF16)
    lane, sub = iota((rows, HD), 1), iota((rows, HD), 0)
    for p in range(groups):
        at = slice(p * rows, (p + 1) * rows)
        both = jnp.where(lane == sub, upper[at], 0.0) + jnp.where(lane == sub + rows, (squares - upper)[at], 0.0)
        line = jnp.sum(both, axis=0, keepdims=True)
        out[p, used:, :] = jnp.where(iota((height - used, HD), 0) == 0, line, 0.0).astype(BF16)


def lightning_kernel(parts, decay, states, gain, out, turned, mixed, flat):
    rows, heads = states.shape[0], states.shape[1]
    used = 4 * rows * heads
    total = parts[0].astype(F32)
    for p in range(1, parts.shape[0]):
        total = total + parts[p].astype(F32)
    line = total[used:used + 1, :]
    sums = line + pltpu.roll(line, HD - rows, axis=1)
    block = 4 * rows
    pattern = iota((block, HD), 1) == lax.rem(iota((block, HD), 0), rows)
    squares = jnp.sum(jnp.where(pattern, sums, 0.0), axis=1, keepdims=True)
    scale = jnp.sqrt(squares / D + EPS)
    keep = jnp.exp(-decay[...])
    span = range(heads)
    mixing = [total[block * h:block * (h + 1), :] / scale for h in span]
    below = [1.0 + jnp.exp(-m) for m in mixing]
    silu = [m / b for m, b in zip(mixing, below)]
    gates = [1.0 / b[3 * rows:] for b in below]
    columns = [v[:2 * rows].T for v in silu]
    for h in span:
        mixed[h] = silu[h]
        turned[h] = columns[h]
    inner = [jnp.sum(v[:rows] * v[rows:2 * rows], axis=1, keepdims=True) for v in silu]
    for j in range(rows):
        for h in span:
            read = jnp.sum(columns[h][:, j:j + 1] * states[j, h], axis=0, keepdims=True)
            flat[j:j + 1, h * HD:(h + 1) * HD] = read
    read_squares = jnp.zeros((rows, 1), F32)
    for h in span:
        at = slice(h * HD, (h + 1) * HD)
        read = keep[:, h:h + 1] * flat[0:rows, at] + inner[h] * silu[h][2 * rows:3 * rows]
        read_squares = read_squares + jnp.sum(read * read, axis=1, keepdims=True)
        flat[0:rows, at] = read * gain[h:h + 1, :] * gates[h]
    size = heads * HD
    gated = flat[0:rows, 0:size].astype(BF16)
    upper, lower = halves(read_squares)
    lane = iota((rows, HD), 1)
    tail = jnp.where(lane == 0, upper, jnp.where(lane == 1, lower, 0.0)).astype(BF16)
    for p in range(out.shape[0]):
        out[p, :, :size] = gated
        out[p, :, size:] = tail


def renew_kernel(turned, mixed, decay, states, renewed):
    rows, heads = states.shape[0], states.shape[1]
    keep_row = jnp.exp(-decay[...])
    for h in range(heads):
        keep = keep_row[:, h:h + 1]
        for j in range(rows):
            value = mixed[h, 2 * rows + j:2 * rows + j + 1, :]
            renewed[j, h] = keep * states[j, h] + turned[h, :, rows + j:rows + j + 1] * value


def lightning_out_kernel(blocks, request, weight, out, flat):
    stacked(blocks, flat)
    n = request.shape[1]
    size = weight.shape[0]
    pick = (iota((n, n), 0) == request[...]).astype(F32).astype(BF16)
    placed = jnp.dot(pick, flat[...].astype(BF16), preferred_element_type=F32)
    out[0:n, :] = jnp.dot(placed[:, :size].astype(BF16), weight[...], preferred_element_type=F32)
    squares = as_row(placed[:, size:size + 1] + placed[:, size + 1:size + 2])
    out[n:, :] = jnp.zeros((out.shape[0] - n, out.shape[1]), F32)
    out[n:n + 1, 0:n] = squares


def pair_kernel(own, near, out):
    n = own.shape[0] - 8
    total = own[...] + near[...]
    out[0:n, :] = total[0:n].astype(BF16)
    upper, lower = halves(total[n:n + 1])
    line = iota((out.shape[0] - n, out.shape[1]), 0)
    out[n:, :] = jnp.where(line == 0, upper, jnp.where(line == 1, lower, 0.0)).astype(BF16)


def last_kernel(own, near, far, cross, middle, out):
    n = middle.shape[0]
    total = four(own, near, far, cross)
    squares = as_column(total[n:n + 1, 0:n] + total[n + 1:n + 2, 0:n])
    scale = 1.0 / jnp.sqrt(squares / (LH * HD) + EPS)
    out[...] = (middle[...].astype(F32) + total[0:n, :] * scale).astype(BF16)


def exchange(blocks):
    return lax.all_to_all(blocks, "kv", 0, 0, tiled=True)


def other_core(value):
    return lax.ppermute(value, "head", [(i, i ^ 1) for i in range(lax.axis_size("head"))])


def along(value, axis, stride):
    size = lax.axis_size(axis)

    def place(i):
        return i // stride % 4

    near = [(i, i ^ stride) for i in range(size)]
    far = [(i, i + (3 - 2 * place(i)) * stride) for i in range(size)]
    cross = [(i, i ^ (2 * stride)) for i in range(size)]
    return (value, *(lax.ppermute(value, axis, pairs) for pairs in (near, far, cross)))


def per_device(
    hidden_in,
    attn_gain,
    attn_weight,
    attn_out_weight,
    cache_keys,
    cache_values,
    stretch_counts,
    tail_tokens,
    slot_stretch,
    lin_gain,
    lin_weight,
    decay_rate,
    states,
    out_gain,
    lin_out_weight,
    state_request,
):
    peers = lax.axis_size("kv")
    requests, features = hidden_in.shape
    rows = requests // peers
    width = attn_weight.shape[1]
    slots = cache_keys.shape[0]
    heads = decay_rate.shape[0]
    lin_width = lin_weight.shape[1]
    size = heads * HD
    S = jax.ShapeDtypeStruct
    request = state_request[None, :]

    chunks = features // HD
    keys = cache_keys.reshape(slots, CH, HD)
    values = cache_values.reshape(slots, CH, HD)
    plan = stretch_counts[None, :], tail_tokens[None, :], slot_stretch[None, :]

    parts, info = kernel_call(
        project_kernel,
        (S((peers, rows, width + HD), F32), S((2, slots), jnp.int32)),
        [HBM] * 6, 8 * MIB, 2 * requests * features * width, 2 * features * width,
        [
            pltpu.VMEM((requests, features), BF16),
            pltpu.VMEM((chunks, HD), F32),
            pltpu.VMEM((features, width), BF16),
            pltpu.VMEM((1, requests), jnp.int32),
            pltpu.VMEM((1, requests), jnp.int32),
            pltpu.VMEM((1, slots), jnp.int32),
            pltpu.SemaphoreType.DMA((5 + chunks,)),
        ],
    )(
        in_hbm(hidden_in), in_hbm(attn_gain.reshape(chunks, HD)), in_hbm(attn_weight),
        *(in_hbm(row) for row in plan),
    )
    queries, own = kernel_call(
        normalise_kernel,
        (S((peers, rows, GQ, HD), BF16), S((rows, GQ + 2, HD), F32)),
        [VMEM] + [HBM] * 2, 8 * MIB, 0, 8 * peers * rows * width,
    )(
        exchange(parts), in_hbm(keys), in_hbm(values)
    )
    queries = exchange(queries).reshape(requests, GQ, HD)
    tiles = [pltpu.VMEM((slots, GQ, HD), F32)] * 3 + [pltpu.VMEM((requests + 1, GQ, HD), F32)] * 3
    partial = S((requests * GQ + LINES, HD), BF16)
    part = kernel_call(
        attention_kernel, partial,
        [VMEM, VMEM, VMEM, SMEM, VMEM], 24 * MIB, 4 * slots * GQ * CH * HD, 4 * slots * CH * HD, tiles,
    )(queries, keys, values, info, own)
    part = kernel_call(
        merge_kernel, partial, [VMEM] * 4, 8 * MIB, 0, 10 * requests * GQ * HD,
    )(*along(part, "kv", 1))
    first = kernel_call(
        attention_out_kernel,
        S((requests, features), F32),
        [VMEM] * 5, 8 * MIB, 2 * requests * GQ * HD * features, 2 * GQ * HD * features,
        [pltpu.VMEM((requests * GQ, HD), F32), pltpu.VMEM((requests, GQ * HD), BF16)],
    )(*along(part, "kv", 4), attn_out_weight)
    height = rows * (lin_width // HD) + 16
    mixing, middle = kernel_call(
        mixing_kernel,
        (S((peers, height, HD), BF16), S((requests, features), BF16)),
        [VMEM] * 8, 16 * MIB, 2 * requests * features * lin_width, 2 * features * lin_width,
        [pltpu.VMEM((peers, 4 * rows, HD), F32)],
    )(*along((first + other_core(first)).astype(BF16), "head", 2), hidden_in, lin_gain.reshape(chunks, HD), request, lin_weight)
    decay = decay_rate[None, :]
    gated, turned, mixed = kernel_call(
        lightning_kernel,
        (
            S((peers, rows, size + HD), BF16),
            S((heads, HD, 2 * rows), F32),
            S((heads, 4 * rows, HD), F32),
        ),
        [VMEM] * 4, 16 * MIB, 0, 8 * rows * size * HD,
        [pltpu.VMEM((8, size), F32)],
    )(exchange(mixing), decay, states, out_gain.reshape(heads, HD))
    second = kernel_call(
        lightning_out_kernel,
        S((requests + 8, features), F32),
        [VMEM] * 3, 8 * MIB, 2 * requests * size * features, 2 * size * features,
        [pltpu.VMEM((requests, size + HD), F32)],
    )(exchange(gated), request, lin_out_weight)
    pair = kernel_call(
        pair_kernel, S((requests + 16, features), BF16), [VMEM] * 2, 4 * MIB, 0, 16 * requests * features,
    )(second, other_core(second))
    renewed = kernel_call(
        renew_kernel, S(states.shape, F32), [VMEM] * 4, 8 * MIB, 0, 8 * rows * size * HD,
    )(turned, mixed, decay, states)
    hidden_out = kernel_call(
        last_kernel,
        S((requests, features), BF16),
        [VMEM] * 5, 4 * MIB, 0, 16 * requests * features,
    )(*along(pair, "head", 2), middle)
    return hidden_out, renewed


def solution(mesh):
    placed = (
        P(None, "kv"),
        P("kv"),
        P("kv", "head"),
        P("head", "kv"),
        P("kv", "head", None, None),
        P("kv", "head", None, None),
        P(),
        P(),
        P("kv"),
        P("kv"),
        P("kv", "head"),
        P("head"),
        P("kv", "head", None, None),
        P("head"),
        P("head", "kv"),
        P(),
    )
    return jax.shard_map(
        per_device,
        mesh=mesh,
        in_specs=placed,
        out_specs=(P(None, "kv"), P("kv", "head", None, None)),
        check_vma=False,
    )
```

```python
import functools
import math

import jax
import jax.numpy as jnp
from jax import lax
from jax.experimental import pallas as pl
from jax.experimental.pallas import tpu as pltpu
from jax.sharding import PartitionSpec as P

D = 6144
HD = 128
LH = 64
CH = 256
GQ = 8
REQ = 64
EPS = 1e-05
NEGATIVE = -1e30
F32 = jnp.float32
BF16 = jnp.bfloat16
MIB = 1 << 20
LINES = 16


def iota(shape, dim):
    return lax.broadcasted_iota(jnp.int32, shape, dim)


def as_column(row):
    n = row.shape[1]
    eye = iota((n, n), 0) == iota((n, n), 1)
    return jnp.sum(jnp.where(eye, row, jnp.zeros_like(row)), axis=1, keepdims=True)


def as_row(column):
    n = column.shape[0]
    eye = iota((n, n), 0) == iota((n, n), 1)
    return jnp.sum(jnp.where(eye, column, jnp.zeros_like(column)), axis=0, keepdims=True)


def kernel_call(body, outs, ins, limit, flops, moved, scratch=()):
    return pl.pallas_call(
        body,
        out_shape=outs,
        in_specs=ins,
        out_specs=jax.tree.map(lambda _: pl.BlockSpec(memory_space=pltpu.VMEM), outs),
        scratch_shapes=scratch,
        compiler_params=pltpu.CompilerParams(vmem_limit_bytes=limit),
        cost_estimate=pl.CostEstimate(flops=flops, bytes_accessed=moved, transcendentals=0),
    )


VMEM = pl.BlockSpec(memory_space=pltpu.VMEM)
SMEM = pl.BlockSpec(memory_space=pltpu.SMEM)
HBM = pl.BlockSpec(memory_space=pltpu.HBM)


def in_hbm(value):
    return pltpu.with_memory_space_constraint(value, pltpu.HBM)


def halves(value):
    upper = value.astype(BF16).astype(F32)
    return upper, (value - upper).astype(BF16).astype(F32)


def project_kernel(
    hidden_hbm, gain_hbm, weight_hbm, counts_hbm, tails_hbm, slots_hbm, out, info,
    hidden, gain, weight, counts, tails, slots, sems,
):
    chunks = gain.shape[0]
    first = [(hidden_hbm, hidden), (gain_hbm, gain)]
    blocks = [
        (weight_hbm.at[c * HD:(c + 1) * HD, :], weight.at[c * HD:(c + 1) * HD, :]) for c in range(chunks)
    ]
    last = [(counts_hbm, counts), (tails_hbm, tails), (slots_hbm, slots)]
    copies = [
        pltpu.make_async_copy(source, target, sems.at[k])
        for k, (source, target) in enumerate(first + blocks + last)
    ]
    for copy in copies:
        copy.start()
    for copy in copies[:2] + copies[2 + chunks:]:
        copy.wait()
    x = hidden[...].astype(F32)
    squares = jnp.sum(x * x, axis=1, keepdims=True)
    scaled = [(x[:, c * HD:(c + 1) * HD] * gain[c:c + 1, :]).astype(BF16) for c in range(chunks)]
    number = counts[...]
    n = number.shape[1]
    below = iota((n, n), 1) <= iota((n, n), 0)
    ends = jnp.sum(jnp.where(below, number, 0), axis=1, keepdims=True)
    count = as_column(number)
    starts = ends - count
    limits = count * CH - as_column(tails[...])
    slot = slots[...]
    owner = jnp.sum((slot >= ends).astype(jnp.int32), axis=0, keepdims=True)
    hits = iota((n, slot.shape[1]), 0) == owner
    begin = jnp.sum(jnp.where(hits, starts, 0), axis=0, keepdims=True)
    limit = jnp.sum(jnp.where(hits, limits, 0), axis=0, keepdims=True)
    live = jnp.clip(limit - (slot - begin) * CH, 0, CH)
    info[0:1, :] = owner
    info[1:2, :] = jnp.where(owner < n, live, 0)
    y = jnp.zeros((x.shape[0], weight.shape[1]), F32)
    for c in range(chunks):
        copies[2 + c].wait()
        y = y + jnp.dot(scaled[c], weight[c * HD:(c + 1) * HD, :], preferred_element_type=F32)
    groups, rows, _ = out.shape
    width = weight.shape[1]
    wide = jnp.broadcast_to(squares, (x.shape[0], HD))
    for p in range(groups):
        out[p, :, :width] = y[p * rows:(p + 1) * rows]
        out[p, :, width:] = wide[p * rows:(p + 1) * rows]


def normalise_kernel(parts, keys, values, out, own):
    total = parts[0]
    for p in range(1, parts.shape[0]):
        total = total + parts[p]
    width = own.shape[1] * HD
    mean = total[:, width:width + 1] / D
    projected = (total[:, :width] / jnp.sqrt(mean + EPS)).astype(BF16).astype(F32)
    for g in range(own.shape[1]):
        own[:, g, :] = projected[:, g * HD:(g + 1) * HD]
    queries = own[:, :GQ, :].reshape(own.shape[0] * GQ, HD).astype(BF16)
    for p in range(out.shape[0]):
        out[p] = queries


def attention_kernel(queries, keys, values, info, own, out, slot_max, slot_sum, slot_value, best, summed, mixed):
    slots, rows = keys.shape[0], own.shape[0]
    best[...] = jnp.full(best.shape, NEGATIVE, F32)
    summed[...] = jnp.zeros(summed.shape, F32)
    mixed[...] = jnp.zeros(mixed.shape, F32)
    token = iota((GQ, CH), 1)
    scale = 1.0 / math.sqrt(HD)
    batch = 64
    mine = lax.axis_index("kv") * rows

    @pl.loop(0, slots, step=batch)
    def _(base):
        span = [base + u for u in range(batch)]
        owners = [info[0, s] for s in span]
        scores = [
            lax.dot_general(
                queries[jnp.minimum(r, REQ - 1)], keys[s], (((1,), (1,)), ((), ())),
                preferred_element_type=F32,
            ) * scale
            for r, s in zip(owners, span)
        ]
        live = [token < info[1, s] for s in span]
        scores = [jnp.where(m, x, NEGATIVE) for m, x in zip(live, scores)]
        tops = [jnp.max(x, axis=1, keepdims=True) for x in scores]
        weights = [jnp.where(m, jnp.exp(x - t), 0.0) for m, x, t in zip(live, scores, tops)]
        totals = [jnp.sum(w, axis=1, keepdims=True) for w in weights]
        mixes = [
            jnp.dot(w.astype(BF16), values[s], preferred_element_type=F32) for w, s in zip(weights, span)
        ]
        for r, s, top, total, mix in zip(owners, span, tops, totals, mixes):
            wide = jnp.broadcast_to(top, (GQ, HD))
            best[r] = jnp.maximum(best[r], wide)
            slot_max[s] = wide
            slot_sum[s] = jnp.broadcast_to(total, (GQ, HD))
            slot_value[s] = mix

    fresh = [
        jnp.broadcast_to(
            jnp.sum(own[i, :GQ, :] * own[i, GQ:GQ + 1, :], axis=1, keepdims=True) / math.sqrt(HD), (GQ, HD)
        )
        for i in range(rows)
    ]
    for i in range(rows):
        best[mine + i] = jnp.maximum(best[mine + i], fresh[i])
    upper, lower = halves(best[...])
    best[...] = upper + lower
    for i in range(rows):
        factor = jnp.exp(fresh[i] - best[mine + i])
        summed[mine + i] = factor
        mixed[mine + i] = factor * own[i, GQ + 1:GQ + 2, :]
    step = 8

    @pl.loop(0, slots, step=step)
    def _(base):
        for u in range(step):
            s = base + u
            r = info[0, s]
            factor = jnp.exp(slot_max[s] - best[r])
            summed[r] = summed[r] + factor * slot_sum[s]
            mixed[r] = mixed[r] + factor * slot_value[s]

    lane, sub = iota((GQ, HD), 1), iota((GQ, HD), 0)
    line = iota((LINES, HD), 0)
    stats = jnp.zeros((LINES, HD), F32)
    for i in range(LINES):
        packed = jnp.zeros((GQ, HD), F32)
        for c in range(REQ // LINES):
            r = c * LINES + i
            for k, part in enumerate(halves(best[r]) + halves(summed[r])):
                packed = jnp.where(lane == sub + (4 * c + k) * GQ, part, packed)
        stats = jnp.where(line == i, jnp.sum(packed, axis=0, keepdims=True), stats)
    out[:REQ * GQ, :] = mixed[0:REQ].reshape(REQ * GQ, HD).astype(BF16)
    out[REQ * GQ:, :] = stats.astype(BF16)


def merge_weights(parts):
    lines = [part[REQ * GQ:, :].astype(F32) for part in parts]
    tops = [x + pltpu.roll(x, HD - GQ, axis=1) for x in lines]
    sums = [pltpu.roll(x, HD - 2 * GQ, axis=1) for x in tops]
    top = jnp.maximum(jnp.maximum(tops[0], tops[1]), jnp.maximum(tops[2], tops[3]))
    factors = [jnp.exp(x - top) for x in tops]
    terms = [f * x for f, x in zip(factors, sums)]
    return top, factors, (terms[0] + terms[1]) + (terms[2] + terms[3])


def weighted(parts, factors, store):
    columns = [f.T for f in factors]
    for r in range(0, REQ, 2):
        c, i = r // LINES, r % LINES
        blocks = [part[r * GQ:(r + 2) * GQ, :].astype(F32) for part in parts]
        pair = []
        for u in range(2):
            at = slice(4 * c * GQ, (4 * c + 1) * GQ)
            terms = [t[at, i + u:i + u + 1] * b[u * GQ:(u + 1) * GQ] for t, b in zip(columns, blocks)]
            pair.append((terms[0] + terms[1]) + (terms[2] + terms[3]))
        store(r, jnp.concatenate(pair, axis=0))


def merge_kernel(own, near, far, cross, out):
    parts = own, near, far, cross
    top, factors, total = merge_weights(parts)

    def store(r, value):
        out[r * GQ:(r + 2) * GQ, :] = value.astype(BF16)

    weighted(parts, factors, store)
    place = lax.rem(iota((LINES, HD), 1), 4 * GQ)
    packed = jnp.zeros((LINES, HD), F32)
    for k, part in enumerate(halves(top) + halves(total)):
        moved = part if k == 0 else pltpu.roll(part, k * GQ, axis=1)
        packed = jnp.where((place >= k * GQ) & (place < (k + 1) * GQ), moved, packed)
    out[REQ * GQ:, :] = packed.astype(BF16)


def attention_out_kernel(own, near, far, cross, weight, out, tall, flat):
    parts = own, near, far, cross
    _, factors, total = merge_weights(parts)

    def store(r, value):
        tall[r * GQ:(r + 2) * GQ, :] = value

    weighted(parts, [f / total for f in factors], store)
    for g in range(GQ):
        flat[:, g * HD:(g + 1) * HD] = tall[pl.ds(g, REQ, stride=GQ), :].astype(BF16)
    out[...] = jnp.dot(flat[...], weight[...], preferred_element_type=F32)


def stacked(blocks, flat):
    peers, rows, _ = blocks.shape
    for p in range(peers):
        flat[p * rows:(p + 1) * rows, :] = blocks[p].astype(F32)


def four(own, near, far, cross):
    return (own[...].astype(F32) + near[...].astype(F32)) + (far[...].astype(F32) + cross[...].astype(F32))


def mixing_kernel(own, near, far, cross, hidden, gain, request, weight, out, middle):
    total = hidden[...].astype(F32) + four(own, near, far, cross)
    inner = total.astype(BF16)
    middle[...] = inner
    n = request.shape[1]
    pick = (as_column(request[...]) == iota((n, n), 1)).astype(F32).astype(BF16)
    ordered = jnp.dot(pick, inner, preferred_element_type=F32)
    upper, lower = halves(jnp.sum(ordered * ordered, axis=1, keepdims=True))
    lane = iota((n, HD), 1)
    tail = jnp.where(lane == 0, upper, jnp.where(lane == 1, lower, 0.0))
    scaled = jnp.concatenate(
        [(ordered[:, c * HD:(c + 1) * HD] * gain[c:c + 1, :]).astype(BF16) for c in range(gain.shape[0])], axis=1
    )
    groups, rows, _ = out.shape
    width = weight.shape[1]
    step = 4 * HD
    for c in range(0, width, step):
        y = jnp.dot(scaled, weight[:, c:c + step], preferred_element_type=F32)
        for p in range(groups):
            out[p, :, c:c + step] = y[p * rows:(p + 1) * rows].astype(BF16)
    for p in range(groups):
        out[p, :, width:] = tail[p * rows:(p + 1) * rows].astype(BF16)


def lightning_kernel(parts, decay, states, gain, out, turned, mixed, flat, wide):
    rows, heads = states.shape[0], states.shape[1]
    total = parts[0].astype(F32)
    for p in range(1, parts.shape[0]):
        total = total + parts[p].astype(F32)
    width = 4 * heads * HD
    scale = jnp.sqrt((total[:, width:width + 1] + total[:, width + 1:width + 2]) / D + EPS)
    wide[0:rows, :] = total[:, :width] / scale
    for h in range(heads):
        for k in range(4):
            mixed[h, k * rows:(k + 1) * rows, :] = wide[0:rows, (4 * h + k) * HD:(4 * h + k + 1) * HD]
    keep = jnp.exp(-decay[...])
    span = range(heads)
    mixing = [mixed[h] for h in span]
    below = [1.0 + jnp.exp(-m) for m in mixing]
    silu = [m / b for m, b in zip(mixing, below)]
    gates = [1.0 / b[3 * rows:] for b in below]
    columns = [v[:2 * rows].T for v in silu]
    for h in span:
        mixed[h] = silu[h]
        turned[h] = columns[h]
    inner = [jnp.sum(v[:rows] * v[rows:2 * rows], axis=1, keepdims=True) for v in silu]
    for j in range(rows):
        for h in span:
            read = jnp.sum(columns[h][:, j:j + 1] * states[j, h], axis=0, keepdims=True)
            flat[j:j + 1, h * HD:(h + 1) * HD] = read
    read_squares = jnp.zeros((rows, 1), F32)
    for h in span:
        at = slice(h * HD, (h + 1) * HD)
        read = keep[:, h:h + 1] * flat[0:rows, at] + inner[h] * silu[h][2 * rows:3 * rows]
        read_squares = read_squares + jnp.sum(read * read, axis=1, keepdims=True)
        flat[0:rows, at] = read * gain[h:h + 1, :] * gates[h]
    size = heads * HD
    gated = flat[0:rows, 0:size].astype(BF16)
    upper, lower = halves(read_squares)
    lane = iota((rows, HD), 1)
    tail = jnp.where(lane == 0, upper, jnp.where(lane == 1, lower, 0.0)).astype(BF16)
    for p in range(out.shape[0]):
        out[p, :, :size] = gated
        out[p, :, size:] = tail


def renew_kernel(turned, mixed, decay, states, renewed):
    rows, heads = states.shape[0], states.shape[1]
    keep_row = jnp.exp(-decay[...])
    for h in range(heads):
        keep = keep_row[:, h:h + 1]
        for j in range(rows):
            value = mixed[h, 2 * rows + j:2 * rows + j + 1, :]
            renewed[j, h] = keep * states[j, h] + turned[h, :, rows + j:rows + j + 1] * value


def lightning_out_kernel(blocks, request, weight, out, flat):
    stacked(blocks, flat)
    n = request.shape[1]
    size = weight.shape[0]
    pick = (iota((n, n), 0) == request[...]).astype(F32).astype(BF16)
    placed = jnp.dot(pick, flat[...].astype(BF16), preferred_element_type=F32)
    out[0:n, :] = jnp.dot(placed[:, :size].astype(BF16), weight[...], preferred_element_type=F32)
    squares = as_row(placed[:, size:size + 1] + placed[:, size + 1:size + 2])
    out[n:, :] = jnp.zeros((out.shape[0] - n, out.shape[1]), F32)
    out[n:n + 1, 0:n] = squares


def pair_kernel(own, near, out):
    n = own.shape[0] - 8
    total = own[...] + near[...]
    out[0:n, :] = total[0:n].astype(BF16)
    upper, lower = halves(total[n:n + 1])
    line = iota((out.shape[0] - n, out.shape[1]), 0)
    out[n:, :] = jnp.where(line == 0, upper, jnp.where(line == 1, lower, 0.0)).astype(BF16)


def last_kernel(own, near, far, cross, middle, out):
    n = middle.shape[0]
    total = four(own, near, far, cross)
    squares = as_column(total[n:n + 1, 0:n] + total[n + 1:n + 2, 0:n])
    scale = 1.0 / jnp.sqrt(squares / (LH * HD) + EPS)
    out[...] = (middle[...].astype(F32) + total[0:n, :] * scale).astype(BF16)


def exchange(blocks):
    return lax.all_to_all(blocks, "kv", 0, 0, tiled=True)


def other_core(value):
    return lax.ppermute(value, "head", [(i, i ^ 1) for i in range(lax.axis_size("head"))])


def along(value, axis, stride):
    size = lax.axis_size(axis)

    def place(i):
        return i // stride % 4

    near = [(i, i ^ stride) for i in range(size)]
    far = [(i, i + (3 - 2 * place(i)) * stride) for i in range(size)]
    cross = [(i, i ^ (2 * stride)) for i in range(size)]
    return (value, *(lax.ppermute(value, axis, pairs) for pairs in (near, far, cross)))


def per_device(
    hidden_in,
    attn_gain,
    attn_weight,
    attn_out_weight,
    cache_keys,
    cache_values,
    stretch_counts,
    tail_tokens,
    slot_stretch,
    lin_gain,
    lin_weight,
    decay_rate,
    states,
    out_gain,
    lin_out_weight,
    state_request,
):
    peers = lax.axis_size("kv")
    requests, features = hidden_in.shape
    rows = requests // peers
    width = attn_weight.shape[1]
    slots = cache_keys.shape[0]
    heads = decay_rate.shape[0]
    lin_width = lin_weight.shape[1]
    size = heads * HD
    S = jax.ShapeDtypeStruct
    request = state_request[None, :]

    chunks = features // HD
    keys = cache_keys.reshape(slots, CH, HD)
    values = cache_values.reshape(slots, CH, HD)
    plan = stretch_counts[None, :], tail_tokens[None, :], slot_stretch[None, :]

    parts, info = kernel_call(
        project_kernel,
        (S((peers, rows, width + HD), F32), S((2, slots), jnp.int32)),
        [HBM] * 6, 8 * MIB, 2 * requests * features * width, 2 * features * width,
        [
            pltpu.VMEM((requests, features), BF16),
            pltpu.VMEM((chunks, HD), F32),
            pltpu.VMEM((features, width), BF16),
            pltpu.VMEM((1, requests), jnp.int32),
            pltpu.VMEM((1, requests), jnp.int32),
            pltpu.VMEM((1, slots), jnp.int32),
            pltpu.SemaphoreType.DMA((5 + chunks,)),
        ],
    )(
        in_hbm(hidden_in), in_hbm(attn_gain.reshape(chunks, HD)), in_hbm(attn_weight),
        *(in_hbm(row) for row in plan),
    )
    queries, own = kernel_call(
        normalise_kernel,
        (S((peers, rows * GQ, HD), BF16), S((rows, GQ + 2, HD), F32)),
        [VMEM] + [HBM] * 2, 8 * MIB, 0, 8 * peers * rows * width,
    )(
        exchange(parts), in_hbm(keys), in_hbm(values)
    )
    queries = exchange(queries).reshape(requests, GQ, HD)
    tiles = [pltpu.VMEM((slots, GQ, HD), F32)] * 3 + [pltpu.VMEM((requests + 1, GQ, HD), F32)] * 3
    partial = S((requests * GQ + LINES, HD), BF16)
    part = kernel_call(
        attention_kernel, partial,
        [VMEM, VMEM, VMEM, SMEM, VMEM], 24 * MIB, 4 * slots * GQ * CH * HD, 4 * slots * CH * HD, tiles,
    )(queries, keys, values, info, own)
    part = kernel_call(
        merge_kernel, partial, [VMEM] * 4, 8 * MIB, 0, 10 * requests * GQ * HD,
    )(*along(part, "kv", 1))
    first = kernel_call(
        attention_out_kernel,
        S((requests, features), F32),
        [VMEM] * 5, 8 * MIB, 2 * requests * GQ * HD * features, 2 * GQ * HD * features,
        [pltpu.VMEM((requests * GQ, HD), F32), pltpu.VMEM((requests, GQ * HD), BF16)],
    )(*along(part, "kv", 4), attn_out_weight)
    mixing, middle = kernel_call(
        mixing_kernel,
        (S((peers, rows, lin_width + HD), BF16), S((requests, features), BF16)),
        [VMEM] * 8, 16 * MIB, 2 * requests * features * lin_width, 2 * features * lin_width,
    )(*along((first + other_core(first)).astype(BF16), "head", 2), hidden_in, lin_gain.reshape(chunks, HD), request, lin_weight)
    decay = decay_rate[None, :]
    gated, turned, mixed = kernel_call(
        lightning_kernel,
        (
            S((peers, rows, size + HD), BF16),
            S((heads, HD, 2 * rows), F32),
            S((heads, 4 * rows, HD), F32),
        ),
        [VMEM] * 4, 16 * MIB, 0, 8 * rows * size * HD,
        [pltpu.VMEM((8, size), F32), pltpu.VMEM((8, lin_width), F32)],
    )(exchange(mixing), decay, states, out_gain.reshape(heads, HD))
    second = kernel_call(
        lightning_out_kernel,
        S((requests + 8, features), F32),
        [VMEM] * 3, 8 * MIB, 2 * requests * size * features, 2 * size * features,
        [pltpu.VMEM((requests, size + HD), F32)],
    )(exchange(gated), request, lin_out_weight)
    pair = kernel_call(
        pair_kernel, S((requests + 16, features), BF16), [VMEM] * 2, 4 * MIB, 0, 16 * requests * features,
    )(second, other_core(second))
    renewed = kernel_call(
        renew_kernel, S(states.shape, F32), [VMEM] * 4, 8 * MIB, 0, 8 * rows * size * HD,
    )(turned, mixed, decay, states)
    hidden_out = kernel_call(
        last_kernel,
        S((requests, features), BF16),
        [VMEM] * 5, 4 * MIB, 0, 16 * requests * features,
    )(*along(pair, "head", 2), middle)
    return hidden_out, renewed


def solution(mesh):
    placed = (
        P(None, "kv"),
        P("kv"),
        P("kv", "head"),
        P("head", "kv"),
        P("kv", "head", None, None),
        P("kv", "head", None, None),
        P(),
        P(),
        P("kv"),
        P("kv"),
        P("kv", "head"),
        P("head"),
        P("kv", "head", None, None),
        P("head"),
        P("head", "kv"),
        P(),
    )
    return jax.shard_map(
        per_device,
        mesh=mesh,
        in_specs=placed,
        out_specs=(P(None, "kv"), P("kv", "head", None, None)),
        check_vma=False,
    )
```

```python
import functools
import math

import jax
import jax.numpy as jnp
from jax import lax
from jax.experimental import pallas as pl
from jax.experimental.pallas import tpu as pltpu
from jax.sharding import PartitionSpec as P

D = 6144
HD = 128
LH = 64
CH = 256
GQ = 8
REQ = 64
EPS = 1e-05
NEGATIVE = -1e30
F32 = jnp.float32
BF16 = jnp.bfloat16
MIB = 1 << 20
LINES = 16


def iota(shape, dim):
    return lax.broadcasted_iota(jnp.int32, shape, dim)


def as_column(row):
    n = row.shape[1]
    eye = iota((n, n), 0) == iota((n, n), 1)
    return jnp.sum(jnp.where(eye, row, jnp.zeros_like(row)), axis=1, keepdims=True)


def as_row(column):
    n = column.shape[0]
    eye = iota((n, n), 0) == iota((n, n), 1)
    return jnp.sum(jnp.where(eye, column, jnp.zeros_like(column)), axis=0, keepdims=True)


def kernel_call(body, outs, ins, limit, flops, moved, scratch=(), space=pltpu.VMEM):
    return pl.pallas_call(
        body,
        out_shape=outs,
        in_specs=ins,
        out_specs=jax.tree.map(lambda _: pl.BlockSpec(memory_space=space), outs),
        scratch_shapes=scratch,
        compiler_params=pltpu.CompilerParams(vmem_limit_bytes=limit),
        cost_estimate=pl.CostEstimate(flops=flops, bytes_accessed=moved, transcendentals=0),
    )


VMEM = pl.BlockSpec(memory_space=pltpu.VMEM)
SMEM = pl.BlockSpec(memory_space=pltpu.SMEM)
HBM = pl.BlockSpec(memory_space=pltpu.HBM)


def in_hbm(value):
    return pltpu.with_memory_space_constraint(value, pltpu.HBM)


def halves(value):
    upper = value.astype(BF16).astype(F32)
    return upper, (value - upper).astype(BF16).astype(F32)


def project_kernel(
    hidden_hbm, gain_hbm, weight_hbm, counts_hbm, tails_hbm, slots_hbm, out, info,
    hidden, gain, weight, counts, tails, slots, sems,
):
    chunks = gain.shape[0]
    first = [(hidden_hbm, hidden), (gain_hbm, gain)]
    blocks = [
        (weight_hbm.at[c * HD:(c + 1) * HD, :], weight.at[c * HD:(c + 1) * HD, :]) for c in range(chunks)
    ]
    last = [(counts_hbm, counts), (tails_hbm, tails), (slots_hbm, slots)]
    copies = [
        pltpu.make_async_copy(source, target, sems.at[k])
        for k, (source, target) in enumerate(first + blocks + last)
    ]
    for copy in copies:
        copy.start()
    for copy in copies[:2] + copies[2 + chunks:]:
        copy.wait()
    x = hidden[...].astype(F32)
    squares = jnp.sum(x * x, axis=1, keepdims=True)
    scaled = [(x[:, c * HD:(c + 1) * HD] * gain[c:c + 1, :]).astype(BF16) for c in range(chunks)]
    number = counts[...]
    n = number.shape[1]
    below = iota((n, n), 1) <= iota((n, n), 0)
    ends = jnp.sum(jnp.where(below, number, 0), axis=1, keepdims=True)
    count = as_column(number)
    starts = ends - count
    limits = count * CH - as_column(tails[...])
    slot = slots[...]
    owner = jnp.sum((slot >= ends).astype(jnp.int32), axis=0, keepdims=True)
    hits = iota((n, slot.shape[1]), 0) == owner
    begin = jnp.sum(jnp.where(hits, starts, 0), axis=0, keepdims=True)
    limit = jnp.sum(jnp.where(hits, limits, 0), axis=0, keepdims=True)
    live = jnp.clip(limit - (slot - begin) * CH, 0, CH)
    info[0:1, :] = owner
    info[1:2, :] = jnp.where(owner < n, live, 0)
    y = jnp.zeros((x.shape[0], weight.shape[1]), F32)
    for c in range(chunks):
        copies[2 + c].wait()
        y = y + jnp.dot(scaled[c], weight[c * HD:(c + 1) * HD, :], preferred_element_type=F32)
    groups, rows, _ = out.shape
    width = weight.shape[1]
    wide = jnp.broadcast_to(squares, (x.shape[0], HD))
    for p in range(groups):
        out[p, :, :width] = y[p * rows:(p + 1) * rows]
        out[p, :, width:] = wide[p * rows:(p + 1) * rows]


def normalise_kernel(parts, keys, values, out, own):
    total = parts[0]
    for p in range(1, parts.shape[0]):
        total = total + parts[p]
    width = own.shape[1] * HD
    mean = total[:, width:width + 1] / D
    projected = (total[:, :width] / jnp.sqrt(mean + EPS)).astype(BF16).astype(F32)
    for g in range(own.shape[1]):
        own[:, g, :] = projected[:, g * HD:(g + 1) * HD]
    queries = own[:, :GQ, :].reshape(own.shape[0] * GQ, HD).astype(BF16)
    for p in range(out.shape[0]):
        out[p] = queries


def attention_kernel(queries, keys, values, info, own, out, slot_max, slot_sum, slot_value, best, summed, mixed):
    slots, rows = keys.shape[0], own.shape[0]
    best[...] = jnp.full(best.shape, NEGATIVE, F32)
    summed[...] = jnp.zeros(summed.shape, F32)
    mixed[...] = jnp.zeros(mixed.shape, F32)
    token = iota((GQ, CH), 1)
    scale = 1.0 / math.sqrt(HD)
    mine = lax.axis_index("kv") * rows
    span = range(slots)
    owners = [info[0, s] for s in span]
    scores = [
        lax.dot_general(
            queries[jnp.minimum(r, REQ - 1)], keys[s], (((1,), (1,)), ((), ())), preferred_element_type=F32
        ) * scale
        for r, s in zip(owners, span)
    ]
    live = [token < info[1, s] for s in span]
    scores = [jnp.where(m, x, NEGATIVE) for m, x in zip(live, scores)]
    tops = [jnp.max(x, axis=1, keepdims=True) for x in scores]
    weights = [jnp.where(m, jnp.exp(x - t), 0.0) for m, x, t in zip(live, scores, tops)]
    totals = [jnp.sum(w, axis=1, keepdims=True) for w in weights]
    mixes = [jnp.dot(w.astype(BF16), values[s], preferred_element_type=F32) for w, s in zip(weights, span)]
    for r, s, top, total, mix in zip(owners, span, tops, totals, mixes):
        wide = jnp.broadcast_to(top, (GQ, HD))
        best[r] = jnp.maximum(best[r], wide)
        slot_max[s] = wide
        slot_sum[s] = jnp.broadcast_to(total, (GQ, HD))
        slot_value[s] = mix

    fresh = [
        jnp.broadcast_to(
            jnp.sum(own[i, :GQ, :] * own[i, GQ:GQ + 1, :], axis=1, keepdims=True) / math.sqrt(HD), (GQ, HD)
        )
        for i in range(rows)
    ]
    for i in range(rows):
        best[mine + i] = jnp.maximum(best[mine + i], fresh[i])
    upper, lower = halves(best[...])
    best[...] = upper + lower
    for i in range(rows):
        factor = jnp.exp(fresh[i] - best[mine + i])
        summed[mine + i] = factor
        mixed[mine + i] = factor * own[i, GQ + 1:GQ + 2, :]
    for r, s in zip(owners, span):
        factor = jnp.exp(slot_max[s] - best[r])
        summed[r] = summed[r] + factor * slot_sum[s]
        mixed[r] = mixed[r] + factor * slot_value[s]

    lane, sub = iota((GQ, HD), 1), iota((GQ, HD), 0)
    line = iota((LINES, HD), 0)
    stats = jnp.zeros((LINES, HD), F32)
    for i in range(LINES):
        packed = jnp.zeros((GQ, HD), F32)
        for c in range(REQ // LINES):
            r = c * LINES + i
            for k, part in enumerate(halves(best[r]) + halves(summed[r])):
                packed = jnp.where(lane == sub + (4 * c + k) * GQ, part, packed)
        stats = jnp.where(line == i, jnp.sum(packed, axis=0, keepdims=True), stats)
    out[:REQ * GQ, :] = mixed[0:REQ].reshape(REQ * GQ, HD).astype(BF16)
    out[REQ * GQ:, :] = stats.astype(BF16)


def merge_weights(parts):
    lines = [part[REQ * GQ:, :].astype(F32) for part in parts]
    tops = [x + pltpu.roll(x, HD - GQ, axis=1) for x in lines]
    sums = [pltpu.roll(x, HD - 2 * GQ, axis=1) for x in tops]
    top = jnp.maximum(jnp.maximum(tops[0], tops[1]), jnp.maximum(tops[2], tops[3]))
    factors = [jnp.exp(x - top) for x in tops]
    terms = [f * x for f, x in zip(factors, sums)]
    return top, factors, (terms[0] + terms[1]) + (terms[2] + terms[3])


def weighted(parts, factors, store):
    columns = [f.T for f in factors]
    for r in range(0, REQ, 2):
        c, i = r // LINES, r % LINES
        blocks = [part[r * GQ:(r + 2) * GQ, :].astype(F32) for part in parts]
        pair = []
        for u in range(2):
            at = slice(4 * c * GQ, (4 * c + 1) * GQ)
            terms = [t[at, i + u:i + u + 1] * b[u * GQ:(u + 1) * GQ] for t, b in zip(columns, blocks)]
            pair.append((terms[0] + terms[1]) + (terms[2] + terms[3]))
        store(r, jnp.concatenate(pair, axis=0))


def merge_kernel(own, near, far, cross, out):
    parts = own, near, far, cross
    top, factors, total = merge_weights(parts)

    def store(r, value):
        out[r * GQ:(r + 2) * GQ, :] = value.astype(BF16)

    weighted(parts, factors, store)
    place = lax.rem(iota((LINES, HD), 1), 4 * GQ)
    packed = jnp.zeros((LINES, HD), F32)
    for k, part in enumerate(halves(top) + halves(total)):
        moved = part if k == 0 else pltpu.roll(part, k * GQ, axis=1)
        packed = jnp.where((place >= k * GQ) & (place < (k + 1) * GQ), moved, packed)
    out[REQ * GQ:, :] = packed.astype(BF16)


def attention_out_kernel(own, near, far, cross, weight, out, tall, flat):
    parts = own, near, far, cross
    _, factors, total = merge_weights(parts)

    def store(r, value):
        tall[r * GQ:(r + 2) * GQ, :] = value

    weighted(parts, [f / total for f in factors], store)
    for g in range(GQ):
        flat[:, g * HD:(g + 1) * HD] = tall[pl.ds(g, REQ, stride=GQ), :].astype(BF16)
    out[...] = jnp.dot(flat[...], weight[...], preferred_element_type=F32)


def stacked(blocks, flat):
    peers, rows, _ = blocks.shape
    for p in range(peers):
        flat[p * rows:(p + 1) * rows, :] = blocks[p].astype(F32)


def four(own, near, far, cross):
    return (own[...].astype(F32) + near[...].astype(F32)) + (far[...].astype(F32) + cross[...].astype(F32))


def mixing_kernel(own, near, far, cross, hidden, gain, request, weight, out, middle):
    total = hidden[...].astype(F32) + four(own, near, far, cross)
    inner = total.astype(BF16)
    middle[...] = inner
    n = request.shape[1]
    pick = (as_column(request[...]) == iota((n, n), 1)).astype(F32).astype(BF16)
    ordered = jnp.dot(pick, inner, preferred_element_type=F32)
    upper, lower = halves(jnp.sum(ordered * ordered, axis=1, keepdims=True))
    lane = iota((n, HD), 1)
    tail = jnp.where(lane == 0, upper, jnp.where(lane == 1, lower, 0.0))
    scaled = jnp.concatenate(
        [(ordered[:, c * HD:(c + 1) * HD] * gain[c:c + 1, :]).astype(BF16) for c in range(gain.shape[0])], axis=1
    )
    groups, rows, _ = out.shape
    width = weight.shape[1]
    step = 4 * HD
    for c in range(0, width, step):
        y = jnp.dot(scaled, weight[:, c:c + step], preferred_element_type=F32)
        for p in range(groups):
            out[p, :, c:c + step] = y[p * rows:(p + 1) * rows].astype(BF16)
    for p in range(groups):
        out[p, :, width:] = tail[p * rows:(p + 1) * rows].astype(BF16)


def lightning_kernel(parts, decay, states, gain, out, turned, mixed, flat, wide):
    rows, heads = states.shape[0], states.shape[1]
    total = parts[0].astype(F32)
    for p in range(1, parts.shape[0]):
        total = total + parts[p].astype(F32)
    width = 4 * heads * HD
    scale = jnp.sqrt((total[:, width:width + 1] + total[:, width + 1:width + 2]) / D + EPS)
    wide[0:rows, :] = total[:, :width] / scale
    for h in range(heads):
        for k in range(4):
            mixed[h, k * rows:(k + 1) * rows, :] = wide[0:rows, (4 * h + k) * HD:(4 * h + k + 1) * HD]
    keep = jnp.exp(-decay[...])
    span = range(heads)
    mixing = [mixed[h] for h in span]
    below = [1.0 + jnp.exp(-m) for m in mixing]
    silu = [m / b for m, b in zip(mixing, below)]
    gates = [1.0 / b[3 * rows:] for b in below]
    columns = jnp.concatenate([v[:2 * rows] for v in silu], axis=0).T
    turned[...] = columns
    for h in span:
        mixed[h] = silu[h]
    inner = [jnp.sum(v[:rows] * v[rows:2 * rows], axis=1, keepdims=True) for v in silu]
    for j in range(rows):
        for h in span:
            at = 2 * rows * h + j
            read = jnp.sum(columns[:, at:at + 1] * states[j, h], axis=0, keepdims=True)
            flat[j:j + 1, h * HD:(h + 1) * HD] = read
    read_squares = jnp.zeros((rows, 1), F32)
    for h in span:
        at = slice(h * HD, (h + 1) * HD)
        read = keep[:, h:h + 1] * flat[0:rows, at] + inner[h] * silu[h][2 * rows:3 * rows]
        read_squares = read_squares + jnp.sum(read * read, axis=1, keepdims=True)
        flat[0:rows, at] = read * gain[h:h + 1, :] * gates[h]
    size = heads * HD
    gated = flat[0:rows, 0:size].astype(BF16)
    upper, lower = halves(read_squares)
    lane = iota((rows, HD), 1)
    tail = jnp.where(lane == 0, upper, jnp.where(lane == 1, lower, 0.0)).astype(BF16)
    for p in range(out.shape[0]):
        out[p, :, :size] = gated
        out[p, :, size:] = tail


def renew_kernel(turned, mixed, decay, states, renewed, block, sems):
    rows, heads = states.shape[0], states.shape[1]
    keep = jnp.exp(-decay[...])
    copies = [pltpu.make_async_copy(block.at[j], renewed.at[j], sems.at[j]) for j in range(rows)]
    for j in range(rows):
        for h in range(heads):
            value = mixed[h, 2 * rows + j:2 * rows + j + 1, :]
            at = 2 * rows * h + rows + j
            block[j, h] = keep[:, h:h + 1] * states[j, h] + turned[:, at:at + 1] * value
        copies[j].start()
    for copy in copies:
        copy.wait()


def lightning_out_kernel(blocks, request, weight, out, flat):
    stacked(blocks, flat)
    n = request.shape[1]
    size = weight.shape[0]
    pick = (iota((n, n), 0) == request[...]).astype(F32).astype(BF16)
    placed = jnp.dot(pick, flat[...].astype(BF16), preferred_element_type=F32)
    out[0:n, :] = jnp.dot(placed[:, :size].astype(BF16), weight[...], preferred_element_type=F32)
    squares = as_row(placed[:, size:size + 1] + placed[:, size + 1:size + 2])
    out[n:, :] = jnp.zeros((out.shape[0] - n, out.shape[1]), F32)
    out[n:n + 1, 0:n] = squares


def pair_kernel(own, near, out):
    n = own.shape[0] - 8
    total = own[...] + near[...]
    out[0:n, :] = total[0:n].astype(BF16)
    upper, lower = halves(total[n:n + 1])
    line = iota((out.shape[0] - n, out.shape[1]), 0)
    out[n:, :] = jnp.where(line == 0, upper, jnp.where(line == 1, lower, 0.0)).astype(BF16)


def last_kernel(own, near, far, cross, middle, out):
    n = middle.shape[0]
    total = four(own, near, far, cross)
    squares = as_column(total[n:n + 1, 0:n] + total[n + 1:n + 2, 0:n])
    scale = 1.0 / jnp.sqrt(squares / (LH * HD) + EPS)
    out[...] = (middle[...].astype(F32) + total[0:n, :] * scale).astype(BF16)


def exchange(blocks):
    return lax.all_to_all(blocks, "kv", 0, 0, tiled=True)


def other_core(value):
    return lax.ppermute(value, "head", [(i, i ^ 1) for i in range(lax.axis_size("head"))])


def along(value, axis, stride):
    size = lax.axis_size(axis)

    def place(i):
        return i // stride % 4

    near = [(i, i ^ stride) for i in range(size)]
    far = [(i, i + (3 - 2 * place(i)) * stride) for i in range(size)]
    cross = [(i, i ^ (2 * stride)) for i in range(size)]
    return (value, *(lax.ppermute(value, axis, pairs) for pairs in (near, far, cross)))


def per_device(
    hidden_in,
    attn_gain,
    attn_weight,
    attn_out_weight,
    cache_keys,
    cache_values,
    stretch_counts,
    tail_tokens,
    slot_stretch,
    lin_gain,
    lin_weight,
    decay_rate,
    states,
    out_gain,
    lin_out_weight,
    state_request,
):
    peers = lax.axis_size("kv")
    requests, features = hidden_in.shape
    rows = requests // peers
    width = attn_weight.shape[1]
    slots = cache_keys.shape[0]
    heads = decay_rate.shape[0]
    lin_width = lin_weight.shape[1]
    size = heads * HD
    S = jax.ShapeDtypeStruct
    request = state_request[None, :]

    chunks = features // HD
    keys = cache_keys.reshape(slots, CH, HD)
    values = cache_values.reshape(slots, CH, HD)
    plan = stretch_counts[None, :], tail_tokens[None, :], slot_stretch[None, :]

    parts, info = kernel_call(
        project_kernel,
        (S((peers, rows, width + HD), F32), S((2, slots), jnp.int32)),
        [HBM] * 6, 8 * MIB, 2 * requests * features * width, 2 * features * width,
        [
            pltpu.VMEM((requests, features), BF16),
            pltpu.VMEM((chunks, HD), F32),
            pltpu.VMEM((features, width), BF16),
            pltpu.VMEM((1, requests), jnp.int32),
            pltpu.VMEM((1, requests), jnp.int32),
            pltpu.VMEM((1, slots), jnp.int32),
            pltpu.SemaphoreType.DMA((5 + chunks,)),
        ],
    )(
        in_hbm(hidden_in), in_hbm(attn_gain.reshape(chunks, HD)), in_hbm(attn_weight),
        *(in_hbm(row) for row in plan),
    )
    queries, own = kernel_call(
        normalise_kernel,
        (S((peers, rows * GQ, HD), BF16), S((rows, GQ + 2, HD), F32)),
        [VMEM] + [HBM] * 2, 8 * MIB, 0, 8 * peers * rows * width,
    )(
        exchange(parts), in_hbm(keys), in_hbm(values)
    )
    queries = exchange(queries).reshape(requests, GQ, HD)
    tiles = [pltpu.VMEM((slots, GQ, HD), F32)] * 3 + [pltpu.VMEM((requests + 1, GQ, HD), F32)] * 3
    partial = S((requests * GQ + LINES, HD), BF16)
    part = kernel_call(
        attention_kernel, partial,
        [VMEM, VMEM, VMEM, SMEM, VMEM], 24 * MIB, 4 * slots * GQ * CH * HD, 4 * slots * CH * HD, tiles,
    )(queries, keys, values, info, own)
    part = kernel_call(
        merge_kernel, partial, [VMEM] * 4, 8 * MIB, 0, 10 * requests * GQ * HD,
    )(*along(part, "kv", 1))
    first = kernel_call(
        attention_out_kernel,
        S((requests, features), F32),
        [VMEM] * 5, 8 * MIB, 2 * requests * GQ * HD * features, 2 * GQ * HD * features,
        [pltpu.VMEM((requests * GQ, HD), F32), pltpu.VMEM((requests, GQ * HD), BF16)],
    )(*along(part, "kv", 4), attn_out_weight)
    mixing, middle = kernel_call(
        mixing_kernel,
        (S((peers, rows, lin_width + HD), BF16), S((requests, features), BF16)),
        [VMEM] * 8, 16 * MIB, 2 * requests * features * lin_width, 2 * features * lin_width,
    )(*along((first + other_core(first)).astype(BF16), "head", 2), hidden_in, lin_gain.reshape(chunks, HD), request, lin_weight)
    decay = decay_rate[None, :]
    gated, turned, mixed = kernel_call(
        lightning_kernel,
        (
            S((peers, rows, size + HD), BF16),
            S((HD, 2 * rows * heads), F32),
            S((heads, 4 * rows, HD), F32),
        ),
        [VMEM] * 4, 16 * MIB, 0, 8 * rows * size * HD,
        [pltpu.VMEM((8, size), F32), pltpu.VMEM((8, lin_width), F32)],
    )(exchange(mixing), decay, states, out_gain.reshape(heads, HD))
    second = kernel_call(
        lightning_out_kernel,
        S((requests + 8, features), F32),
        [VMEM] * 3, 8 * MIB, 2 * requests * size * features, 2 * size * features,
        [pltpu.VMEM((requests, size + HD), F32)],
    )(exchange(gated), request, lin_out_weight)
    pair = kernel_call(
        pair_kernel, S((requests + 16, features), BF16), [VMEM] * 2, 4 * MIB, 0, 16 * requests * features,
    )(second, other_core(second))
    renewed = kernel_call(
        renew_kernel, S(states.shape, F32), [VMEM] * 4, 8 * MIB, 0, 8 * rows * size * HD,
        [pltpu.VMEM(states.shape, F32), pltpu.SemaphoreType.DMA((rows,))], pltpu.HBM,
    )(turned, mixed, decay, states)
    hidden_out = kernel_call(
        last_kernel,
        S((requests, features), BF16),
        [VMEM] * 5, 4 * MIB, 0, 16 * requests * features,
    )(*along(pair, "head", 2), middle)
    return hidden_out, renewed


def solution(mesh):
    placed = (
        P(None, "kv"),
        P("kv"),
        P("kv", "head"),
        P("head", "kv"),
        P("kv", "head", None, None),
        P("kv", "head", None, None),
        P(),
        P(),
        P("kv"),
        P("kv"),
        P("kv", "head"),
        P("head"),
        P("kv", "head", None, None),
        P("head"),
        P("head", "kv"),
        P(),
    )
    return jax.shard_map(
        per_device,
        mesh=mesh,
        in_specs=placed,
        out_specs=(P(None, "kv"), P("kv", "head", None, None)),
        check_vma=False,
    )
```

```python
import functools
import math

import jax
import jax.numpy as jnp
from jax import lax
from jax.experimental import pallas as pl
from jax.experimental.pallas import tpu as pltpu
from jax.sharding import PartitionSpec as P

D = 6144
HD = 128
LH = 64
CH = 256
GQ = 8
REQ = 64
EPS = 1e-05
NEGATIVE = -1e30
F32 = jnp.float32
BF16 = jnp.bfloat16
MIB = 1 << 20
LINES = 16


def iota(shape, dim):
    return lax.broadcasted_iota(jnp.int32, shape, dim)


def as_column(row):
    n = row.shape[1]
    eye = iota((n, n), 0) == iota((n, n), 1)
    return jnp.sum(jnp.where(eye, row, jnp.zeros_like(row)), axis=1, keepdims=True)


def as_row(column):
    n = column.shape[0]
    eye = iota((n, n), 0) == iota((n, n), 1)
    return jnp.sum(jnp.where(eye, column, jnp.zeros_like(column)), axis=0, keepdims=True)


def kernel_call(body, outs, ins, limit, flops, moved, scratch=(), space=pltpu.VMEM):
    return pl.pallas_call(
        body,
        out_shape=outs,
        in_specs=ins,
        out_specs=jax.tree.map(lambda _: pl.BlockSpec(memory_space=space), outs),
        scratch_shapes=scratch,
        compiler_params=pltpu.CompilerParams(vmem_limit_bytes=limit),
        cost_estimate=pl.CostEstimate(flops=flops, bytes_accessed=moved, transcendentals=0),
    )


VMEM = pl.BlockSpec(memory_space=pltpu.VMEM)
SMEM = pl.BlockSpec(memory_space=pltpu.SMEM)
HBM = pl.BlockSpec(memory_space=pltpu.HBM)


def in_hbm(value):
    return pltpu.with_memory_space_constraint(value, pltpu.HBM)


def halves(value):
    upper = value.astype(BF16).astype(F32)
    return upper, (value - upper).astype(BF16).astype(F32)


def project_kernel(
    hidden_hbm, gain_hbm, weight_hbm, counts_hbm, tails_hbm, slots_hbm, own, cross, far, near, info,
    hidden, gain, weight, counts, tails, slots, whole, sems,
):
    chunks = gain.shape[0]
    first = [(hidden_hbm, hidden), (gain_hbm, gain)]
    blocks = [
        (weight_hbm.at[c * HD:(c + 1) * HD, :], weight.at[c * HD:(c + 1) * HD, :]) for c in range(chunks)
    ]
    last = [(counts_hbm, counts), (tails_hbm, tails), (slots_hbm, slots)]
    copies = [
        pltpu.make_async_copy(source, target, sems.at[k])
        for k, (source, target) in enumerate(first + blocks + last)
    ]
    for copy in copies:
        copy.start()
    for copy in copies[:2] + copies[2 + chunks:]:
        copy.wait()
    x = hidden[...].astype(F32)
    squares = jnp.sum(x * x, axis=1, keepdims=True)
    scaled = [(x[:, c * HD:(c + 1) * HD] * gain[c:c + 1, :]).astype(BF16) for c in range(chunks)]
    number = counts[...]
    n = number.shape[1]
    below = iota((n, n), 1) <= iota((n, n), 0)
    ends = jnp.sum(jnp.where(below, number, 0), axis=1, keepdims=True)
    count = as_column(number)
    starts = ends - count
    limits = count * CH - as_column(tails[...])
    slot = slots[...]
    owner = jnp.sum((slot >= ends).astype(jnp.int32), axis=0, keepdims=True)
    hits = iota((n, slot.shape[1]), 0) == owner
    begin = jnp.sum(jnp.where(hits, starts, 0), axis=0, keepdims=True)
    limit = jnp.sum(jnp.where(hits, limits, 0), axis=0, keepdims=True)
    live = jnp.clip(limit - (slot - begin) * CH, 0, CH)
    info[0:1, :] = owner
    info[1:2, :] = jnp.where(owner < n, live, 0)
    y = jnp.zeros((x.shape[0], weight.shape[1]), F32)
    for c in range(chunks):
        copies[2 + c].wait()
        y = y + jnp.dot(scaled[c], weight[c * HD:(c + 1) * HD, :], preferred_element_type=F32)
    width = weight.shape[1]
    whole[:, :width] = y
    whole[:, width:] = jnp.broadcast_to(squares, (x.shape[0], HD))
    place = lax.rem(lax.axis_index("kv"), 4)
    rows = own.shape[0]
    for k, part in enumerate((own, near, cross, far)):
        at = pl.multiple_of(jnp.bitwise_xor(place, k) * rows, rows)
        part[...] = whole[pl.ds(at, rows), :]


def sum_kernel(own, near, far, cross, keys, values, out):
    out[...] = four(own, near, far, cross)


def normalise_kernel(one, near, far, cross, out, own, tiles):
    total = four(one, near, far, cross)
    columns = own.shape[1]
    width = columns * HD
    scale = jnp.sqrt(total[:, width:width + 1] / D + EPS)
    projected = (total[:, :width] / scale).astype(BF16).astype(F32)
    for g in range(columns):
        tiles[:, g, :] = projected[:, g * HD:(g + 1) * HD]
    out[...] = tiles[:, :GQ, :].astype(BF16)
    rows = own.shape[0]
    own[...] = tiles[pl.ds(lax.div(lax.axis_index("kv"), 4) * rows, rows)]


def attention_kernel(
    one, near, far, cross, keys, values, info, own, out, slot_max, slot_sum, slot_value, best, summed, mixed, queries
):
    slots, rows = keys.shape[0], own.shape[0]
    best[...] = jnp.full(best.shape, NEGATIVE, F32)
    summed[...] = jnp.zeros(summed.shape, F32)
    mixed[...] = jnp.zeros(mixed.shape, F32)
    token = iota((GQ, CH), 1)
    scale = 1.0 / math.sqrt(HD)
    place = lax.rem(lax.axis_index("kv"), 4)
    quarter = one.shape[0]
    for k, part in enumerate((one, near, cross, far)):
        queries[pl.ds(jnp.bitwise_xor(place, k) * quarter, quarter)] = part[...]
    mine = place * quarter + lax.div(lax.axis_index("kv"), 4) * rows
    span = range(slots)
    owners = [info[0, s] for s in span]
    scores = [
        lax.dot_general(
            queries[jnp.minimum(r, REQ - 1)], keys[s], (((1,), (1,)), ((), ())), preferred_element_type=F32
        ) * scale
        for r, s in zip(owners, span)
    ]
    live = [token < info[1, s] for s in span]
    scores = [jnp.where(m, x, NEGATIVE) for m, x in zip(live, scores)]
    tops = [jnp.max(x, axis=1, keepdims=True) for x in scores]
    weights = [jnp.where(m, jnp.exp(x - t), 0.0) for m, x, t in zip(live, scores, tops)]
    totals = [jnp.sum(w, axis=1, keepdims=True) for w in weights]
    mixes = [jnp.dot(w.astype(BF16), values[s], preferred_element_type=F32) for w, s in zip(weights, span)]
    for r, s, top, total, mix in zip(owners, span, tops, totals, mixes):
        wide = jnp.broadcast_to(top, (GQ, HD))
        best[r] = jnp.maximum(best[r], wide)
        slot_max[s] = wide
        slot_sum[s] = jnp.broadcast_to(total, (GQ, HD))
        slot_value[s] = mix

    fresh = [
        jnp.broadcast_to(
            jnp.sum(own[i, :GQ, :] * own[i, GQ:GQ + 1, :], axis=1, keepdims=True) / math.sqrt(HD), (GQ, HD)
        )
        for i in range(rows)
    ]
    for i in range(rows):
        best[mine + i] = jnp.maximum(best[mine + i], fresh[i])
    upper, lower = halves(best[...])
    best[...] = upper + lower
    for i in range(rows):
        factor = jnp.exp(fresh[i] - best[mine + i])
        summed[mine + i] = factor
        mixed[mine + i] = factor * own[i, GQ + 1:GQ + 2, :]
    for r, s in zip(owners, span):
        factor = jnp.exp(slot_max[s] - best[r])
        summed[r] = summed[r] + factor * slot_sum[s]
        mixed[r] = mixed[r] + factor * slot_value[s]

    lane, sub = iota((GQ, HD), 1), iota((GQ, HD), 0)
    line = iota((LINES, HD), 0)
    stats = jnp.zeros((LINES, HD), F32)
    for i in range(LINES):
        packed = jnp.zeros((GQ, HD), F32)
        for c in range(REQ // LINES):
            r = c * LINES + i
            for k, part in enumerate(halves(best[r]) + halves(summed[r])):
                packed = jnp.where(lane == sub + (4 * c + k) * GQ, part, packed)
        stats = jnp.where(line == i, jnp.sum(packed, axis=0, keepdims=True), stats)
    out[:REQ * GQ, :] = mixed[0:REQ].reshape(REQ * GQ, HD).astype(BF16)
    out[REQ * GQ:, :] = stats.astype(BF16)


def merge_weights(parts):
    lines = [part[REQ * GQ:, :].astype(F32) for part in parts]
    tops = [x + pltpu.roll(x, HD - GQ, axis=1) for x in lines]
    sums = [pltpu.roll(x, HD - 2 * GQ, axis=1) for x in tops]
    top = jnp.maximum(jnp.maximum(tops[0], tops[1]), jnp.maximum(tops[2], tops[3]))
    factors = [jnp.exp(x - top) for x in tops]
    terms = [f * x for f, x in zip(factors, sums)]
    return top, factors, (terms[0] + terms[1]) + (terms[2] + terms[3])


def weighted(parts, factors, store):
    columns = [f.T for f in factors]
    for r in range(0, REQ, 2):
        c, i = r // LINES, r % LINES
        blocks = [part[r * GQ:(r + 2) * GQ, :].astype(F32) for part in parts]
        pair = []
        for u in range(2):
            at = slice(4 * c * GQ, (4 * c + 1) * GQ)
            terms = [t[at, i + u:i + u + 1] * b[u * GQ:(u + 1) * GQ] for t, b in zip(columns, blocks)]
            pair.append((terms[0] + terms[1]) + (terms[2] + terms[3]))
        store(r, jnp.concatenate(pair, axis=0))


def merge_kernel(own, near, far, cross, out):
    parts = own, near, far, cross
    top, factors, total = merge_weights(parts)

    def store(r, value):
        out[r * GQ:(r + 2) * GQ, :] = value.astype(BF16)

    weighted(parts, factors, store)
    place = lax.rem(iota((LINES, HD), 1), 4 * GQ)
    packed = jnp.zeros((LINES, HD), F32)
    for k, part in enumerate(halves(top) + halves(total)):
        moved = part if k == 0 else pltpu.roll(part, k * GQ, axis=1)
        packed = jnp.where((place >= k * GQ) & (place < (k + 1) * GQ), moved, packed)
    out[REQ * GQ:, :] = packed.astype(BF16)


def attention_out_kernel(own, near, far, cross, weight, out, tall, flat):
    parts = own, near, far, cross
    _, factors, total = merge_weights(parts)

    def store(r, value):
        tall[r * GQ:(r + 2) * GQ, :] = value

    weighted(parts, [f / total for f in factors], store)
    for g in range(GQ):
        flat[:, g * HD:(g + 1) * HD] = tall[pl.ds(g, REQ, stride=GQ), :].astype(BF16)
    out[...] = jnp.dot(flat[...], weight[...], preferred_element_type=F32)


def stacked(blocks, flat):
    peers, rows, _ = blocks.shape
    for p in range(peers):
        flat[p * rows:(p + 1) * rows, :] = blocks[p].astype(F32)


def four(own, near, far, cross):
    return (own[...].astype(F32) + near[...].astype(F32)) + (far[...].astype(F32) + cross[...].astype(F32))


def mixing_kernel(own, near, far, cross, hidden, gain, request, weight, out, middle):
    total = hidden[...].astype(F32) + four(own, near, far, cross)
    inner = total.astype(BF16)
    middle[...] = inner
    n = request.shape[1]
    pick = (as_column(request[...]) == iota((n, n), 1)).astype(F32).astype(BF16)
    ordered = jnp.dot(pick, inner, preferred_element_type=F32)
    upper, lower = halves(jnp.sum(ordered * ordered, axis=1, keepdims=True))
    lane = iota((n, HD), 1)
    tail = jnp.where(lane == 0, upper, jnp.where(lane == 1, lower, 0.0))
    scaled = jnp.concatenate(
        [(ordered[:, c * HD:(c + 1) * HD] * gain[c:c + 1, :]).astype(BF16) for c in range(gain.shape[0])], axis=1
    )
    groups, rows, _ = out.shape
    width = weight.shape[1]
    step = 4 * HD
    for c in range(0, width, step):
        y = jnp.dot(scaled, weight[:, c:c + step], preferred_element_type=F32)
        for p in range(groups):
            out[p, :, c:c + step] = y[p * rows:(p + 1) * rows].astype(BF16)
    for p in range(groups):
        out[p, :, width:] = tail[p * rows:(p + 1) * rows].astype(BF16)


def lightning_kernel(parts, decay, states, gain, out, turned, mixed, flat, wide):
    rows, heads = states.shape[0], states.shape[1]
    total = parts[0].astype(F32)
    for p in range(1, parts.shape[0]):
        total = total + parts[p].astype(F32)
    width = 4 * heads * HD
    scale = jnp.sqrt((total[:, width:width + 1] + total[:, width + 1:width + 2]) / D + EPS)
    wide[0:rows, :] = total[:, :width] / scale
    for h in range(heads):
        for k in range(4):
            mixed[h, k * rows:(k + 1) * rows, :] = wide[0:rows, (4 * h + k) * HD:(4 * h + k + 1) * HD]
    keep = jnp.exp(-decay[...])
    span = range(heads)
    mixing = [mixed[h] for h in span]
    below = [1.0 + jnp.exp(-m) for m in mixing]
    silu = [m / b for m, b in zip(mixing, below)]
    gates = [1.0 / b[3 * rows:] for b in below]
    columns = jnp.concatenate([v[:2 * rows] for v in silu], axis=0).T
    turned[...] = columns
    for h in span:
        mixed[h] = silu[h]
    inner = [jnp.sum(v[:rows] * v[rows:2 * rows], axis=1, keepdims=True) for v in silu]
    for j in range(rows):
        for h in span:
            at = 2 * rows * h + j
            read = jnp.sum(columns[:, at:at + 1] * states[j, h], axis=0, keepdims=True)
            flat[j:j + 1, h * HD:(h + 1) * HD] = read
    read_squares = jnp.zeros((rows, 1), F32)
    for h in span:
        at = slice(h * HD, (h + 1) * HD)
        read = keep[:, h:h + 1] * flat[0:rows, at] + inner[h] * silu[h][2 * rows:3 * rows]
        read_squares = read_squares + jnp.sum(read * read, axis=1, keepdims=True)
        flat[0:rows, at] = read * gain[h:h + 1, :] * gates[h]
    size = heads * HD
    gated = flat[0:rows, 0:size].astype(BF16)
    upper, lower = halves(read_squares)
    lane = iota((rows, HD), 1)
    tail = jnp.where(lane == 0, upper, jnp.where(lane == 1, lower, 0.0)).astype(BF16)
    for p in range(out.shape[0]):
        out[p, :, :size] = gated
        out[p, :, size:] = tail


def renew_kernel(turned, mixed, decay, states, renewed, block, sems):
    rows, heads = states.shape[0], states.shape[1]
    keep = jnp.exp(-decay[...])
    copies = [pltpu.make_async_copy(block.at[j], renewed.at[j], sems.at[j]) for j in range(rows)]
    for j in range(rows):
        for h in range(heads):
            value = mixed[h, 2 * rows + j:2 * rows + j + 1, :]
            at = 2 * rows * h + rows + j
            block[j, h] = keep[:, h:h + 1] * states[j, h] + turned[:, at:at + 1] * value
        copies[j].start()
    for copy in copies:
        copy.wait()


def lightning_out_kernel(blocks, request, weight, out, flat):
    stacked(blocks, flat)
    n = request.shape[1]
    size = weight.shape[0]
    pick = (iota((n, n), 0) == request[...]).astype(F32).astype(BF16)
    placed = jnp.dot(pick, flat[...].astype(BF16), preferred_element_type=F32)
    out[0:n, :] = jnp.dot(placed[:, :size].astype(BF16), weight[...], preferred_element_type=F32)
    squares = as_row(placed[:, size:size + 1] + placed[:, size + 1:size + 2])
    out[n:, :] = jnp.zeros((out.shape[0] - n, out.shape[1]), F32)
    out[n:n + 1, 0:n] = squares


def pair_kernel(own, near, out):
    n = own.shape[0] - 8
    total = own[...] + near[...]
    out[0:n, :] = total[0:n].astype(BF16)
    upper, lower = halves(total[n:n + 1])
    line = iota((out.shape[0] - n, out.shape[1]), 0)
    out[n:, :] = jnp.where(line == 0, upper, jnp.where(line == 1, lower, 0.0)).astype(BF16)


def last_kernel(own, near, far, cross, middle, out):
    n = middle.shape[0]
    total = four(own, near, far, cross)
    squares = as_column(total[n:n + 1, 0:n] + total[n + 1:n + 2, 0:n])
    scale = 1.0 / jnp.sqrt(squares / (LH * HD) + EPS)
    out[...] = (middle[...].astype(F32) + total[0:n, :] * scale).astype(BF16)


def exchange(blocks):
    return lax.all_to_all(blocks, "kv", 0, 0, tiled=True)


def other_core(value):
    return lax.ppermute(value, "head", [(i, i ^ 1) for i in range(lax.axis_size("head"))])


def spread(parts, axis, stride):
    size = lax.axis_size(axis)
    own, *others = parts
    return (
        own,
        *(
            lax.ppermute(part, axis, [(i, i ^ (k * stride)) for i in range(size)])
            for part, k in zip(others, (1, 3, 2))
        ),
    )


def along(value, axis, stride):
    return spread([value] * 4, axis, stride)


def per_device(
    hidden_in,
    attn_gain,
    attn_weight,
    attn_out_weight,
    cache_keys,
    cache_values,
    stretch_counts,
    tail_tokens,
    slot_stretch,
    lin_gain,
    lin_weight,
    decay_rate,
    states,
    out_gain,
    lin_out_weight,
    state_request,
):
    peers = lax.axis_size("kv")
    requests, features = hidden_in.shape
    rows = requests // peers
    width = attn_weight.shape[1]
    slots = cache_keys.shape[0]
    heads = decay_rate.shape[0]
    lin_width = lin_weight.shape[1]
    size = heads * HD
    S = jax.ShapeDtypeStruct
    request = state_request[None, :]

    chunks = features // HD
    keys = cache_keys.reshape(slots, CH, HD)
    values = cache_values.reshape(slots, CH, HD)
    plan = stretch_counts[None, :], tail_tokens[None, :], slot_stretch[None, :]

    quarter = requests // 4
    block = S((quarter, width + HD), F32)
    own, cross, far, near, info = kernel_call(
        project_kernel,
        (block, block, block, block, S((2, slots), jnp.int32)),
        [HBM] * 6, 8 * MIB, 2 * requests * features * width, 2 * features * width,
        [
            pltpu.VMEM((requests, features), BF16),
            pltpu.VMEM((chunks, HD), F32),
            pltpu.VMEM((features, width), BF16),
            pltpu.VMEM((1, requests), jnp.int32),
            pltpu.VMEM((1, requests), jnp.int32),
            pltpu.VMEM((1, slots), jnp.int32),
            pltpu.VMEM((requests, width + HD), F32),
            pltpu.SemaphoreType.DMA((5 + chunks,)),
        ],
    )(
        in_hbm(hidden_in), in_hbm(attn_gain.reshape(chunks, HD)), in_hbm(attn_weight),
        *(in_hbm(row) for row in plan),
    )
    parts = kernel_call(
        sum_kernel, block, [VMEM] * 4 + [HBM] * 2, 8 * MIB, 0, 20 * quarter * width,
    )(*spread((own, near, far, cross), "kv", 1), in_hbm(keys), in_hbm(values))
    queries, own = kernel_call(
        normalise_kernel,
        (S((quarter, GQ, HD), BF16), S((rows, GQ + 2, HD), F32)),
        [VMEM] * 4, 8 * MIB, 0, 20 * quarter * width,
        [pltpu.VMEM((quarter, GQ + 2, HD), F32)],
    )(*along(parts, "kv", 4))
    tiles = [pltpu.VMEM((slots, GQ, HD), F32)] * 3 + [pltpu.VMEM((requests + 1, GQ, HD), F32)] * 3
    tiles.append(pltpu.VMEM((requests, GQ, HD), BF16))
    partial = S((requests * GQ + LINES, HD), BF16)
    part = kernel_call(
        attention_kernel, partial,
        [VMEM] * 6 + [SMEM, VMEM], 24 * MIB, 4 * slots * GQ * CH * HD, 4 * slots * CH * HD, tiles,
    )(*along(queries, "kv", 1), keys, values, info, own)
    part = kernel_call(
        merge_kernel, partial, [VMEM] * 4, 8 * MIB, 0, 10 * requests * GQ * HD,
    )(*along(part, "kv", 1))
    first = kernel_call(
        attention_out_kernel,
        S((requests, features), F32),
        [VMEM] * 5, 8 * MIB, 2 * requests * GQ * HD * features, 2 * GQ * HD * features,
        [pltpu.VMEM((requests * GQ, HD), F32), pltpu.VMEM((requests, GQ * HD), BF16)],
    )(*along(part, "kv", 4), attn_out_weight)
    mixing, middle = kernel_call(
        mixing_kernel,
        (S((peers, rows, lin_width + HD), BF16), S((requests, features), BF16)),
        [VMEM] * 8, 16 * MIB, 2 * requests * features * lin_width, 2 * features * lin_width,
    )(*along((first + other_core(first)).astype(BF16), "head", 2), hidden_in, lin_gain.reshape(chunks, HD), request, lin_weight)
    decay = decay_rate[None, :]
    gated, turned, mixed = kernel_call(
        lightning_kernel,
        (
            S((peers, rows, size + HD), BF16),
            S((HD, 2 * rows * heads), F32),
            S((heads, 4 * rows, HD), F32),
        ),
        [VMEM] * 4, 16 * MIB, 0, 8 * rows * size * HD,
        [pltpu.VMEM((8, size), F32), pltpu.VMEM((8, lin_width), F32)],
    )(exchange(mixing), decay, states, out_gain.reshape(heads, HD))
    second = kernel_call(
        lightning_out_kernel,
        S((requests + 8, features), F32),
        [VMEM] * 3, 8 * MIB, 2 * requests * size * features, 2 * size * features,
        [pltpu.VMEM((requests, size + HD), F32)],
    )(exchange(gated), request, lin_out_weight)
    pair = kernel_call(
        pair_kernel, S((requests + 16, features), BF16), [VMEM] * 2, 4 * MIB, 0, 16 * requests * features,
    )(second, other_core(second))
    renewed = kernel_call(
        renew_kernel, S(states.shape, F32), [VMEM] * 4, 8 * MIB, 0, 8 * rows * size * HD,
        [pltpu.VMEM(states.shape, F32), pltpu.SemaphoreType.DMA((rows,))], pltpu.HBM,
    )(turned, mixed, decay, states)
    hidden_out = kernel_call(
        last_kernel,
        S((requests, features), BF16),
        [VMEM] * 5, 4 * MIB, 0, 16 * requests * features,
    )(*along(pair, "head", 2), middle)
    return hidden_out, renewed


def solution(mesh):
    placed = (
        P(None, "kv"),
        P("kv"),
        P("kv", "head"),
        P("head", "kv"),
        P("kv", "head", None, None),
        P("kv", "head", None, None),
        P(),
        P(),
        P("kv"),
        P("kv"),
        P("kv", "head"),
        P("head"),
        P("kv", "head", None, None),
        P("head"),
        P("head", "kv"),
        P(),
    )
    return jax.shard_map(
        per_device,
        mesh=mesh,
        in_specs=placed,
        out_specs=(P(None, "kv"), P("kv", "head", None, None)),
        check_vma=False,
    )
```

```python
import functools
import math

import jax
import jax.numpy as jnp
from jax import lax
from jax.experimental import pallas as pl
from jax.experimental.pallas import tpu as pltpu
from jax.sharding import PartitionSpec as P

D = 6144
HD = 128
LH = 64
CH = 256
GQ = 8
REQ = 64
EPS = 1e-05
NEGATIVE = -1e30
F32 = jnp.float32
BF16 = jnp.bfloat16
MIB = 1 << 20
LINES = 16


def iota(shape, dim):
    return lax.broadcasted_iota(jnp.int32, shape, dim)


def as_column(row):
    n = row.shape[1]
    eye = iota((n, n), 0) == iota((n, n), 1)
    return jnp.sum(jnp.where(eye, row, jnp.zeros_like(row)), axis=1, keepdims=True)


def as_row(column):
    n = column.shape[0]
    eye = iota((n, n), 0) == iota((n, n), 1)
    return jnp.sum(jnp.where(eye, column, jnp.zeros_like(column)), axis=0, keepdims=True)


def kernel_call(body, outs, ins, limit, flops, moved, scratch=(), space=pltpu.VMEM):
    return pl.pallas_call(
        body,
        out_shape=outs,
        in_specs=ins,
        out_specs=jax.tree.map(lambda _: pl.BlockSpec(memory_space=space), outs),
        scratch_shapes=scratch,
        compiler_params=pltpu.CompilerParams(vmem_limit_bytes=limit),
        cost_estimate=pl.CostEstimate(flops=flops, bytes_accessed=moved, transcendentals=0),
    )


VMEM = pl.BlockSpec(memory_space=pltpu.VMEM)
SMEM = pl.BlockSpec(memory_space=pltpu.SMEM)
HBM = pl.BlockSpec(memory_space=pltpu.HBM)


def in_hbm(value):
    return pltpu.with_memory_space_constraint(value, pltpu.HBM)


def halves(value):
    upper = value.astype(BF16).astype(F32)
    return upper, (value - upper).astype(BF16).astype(F32)


def project_kernel(
    hidden_hbm, gain_hbm, weight_hbm, counts_hbm, tails_hbm, slots_hbm, own, cross, far, near, info,
    hidden, gain, weight, counts, tails, slots, whole, sems,
):
    chunks = gain.shape[0]
    first = [(hidden_hbm, hidden), (gain_hbm, gain)]
    blocks = [
        (weight_hbm.at[c * HD:(c + 1) * HD, :], weight.at[c * HD:(c + 1) * HD, :]) for c in range(chunks)
    ]
    last = [(counts_hbm, counts), (tails_hbm, tails), (slots_hbm, slots)]
    copies = [
        pltpu.make_async_copy(source, target, sems.at[k])
        for k, (source, target) in enumerate(first + blocks + last)
    ]
    for copy in copies:
        copy.start()
    for copy in copies[:2] + copies[2 + chunks:]:
        copy.wait()
    x = hidden[...].astype(F32)
    squares = jnp.sum(x * x, axis=1, keepdims=True)
    scaled = [(x[:, c * HD:(c + 1) * HD] * gain[c:c + 1, :]).astype(BF16) for c in range(chunks)]
    number = counts[...]
    n = number.shape[1]
    below = iota((n, n), 1) <= iota((n, n), 0)
    ends = jnp.sum(jnp.where(below, number, 0), axis=1, keepdims=True)
    count = as_column(number)
    starts = ends - count
    limits = count * CH - as_column(tails[...])
    slot = slots[...]
    owner = jnp.sum((slot >= ends).astype(jnp.int32), axis=0, keepdims=True)
    hits = iota((n, slot.shape[1]), 0) == owner
    begin = jnp.sum(jnp.where(hits, starts, 0), axis=0, keepdims=True)
    limit = jnp.sum(jnp.where(hits, limits, 0), axis=0, keepdims=True)
    live = jnp.clip(limit - (slot - begin) * CH, 0, CH)
    info[0:1, :] = owner
    info[1:2, :] = jnp.where(owner < n, live, 0)
    y = jnp.zeros((x.shape[0], weight.shape[1]), F32)
    for c in range(chunks):
        copies[2 + c].wait()
        y = y + jnp.dot(scaled[c], weight[c * HD:(c + 1) * HD, :], preferred_element_type=F32)
    width = weight.shape[1]
    whole[:, :width] = y
    whole[:, width:] = jnp.broadcast_to(squares, (x.shape[0], HD))
    place = lax.rem(lax.axis_index("kv"), 4)
    rows = own.shape[0]
    for k, part in enumerate((own, near, cross, far)):
        at = pl.multiple_of(jnp.bitwise_xor(place, k) * rows, rows)
        part[...] = whole[pl.ds(at, rows), :]


def sum_kernel(own, near, far, cross, out):
    out[...] = four(own, near, far, cross)


def normalise_kernel(one, near, far, cross, keys, values, out, own, tiles):
    total = four(one, near, far, cross)
    columns = own.shape[1]
    width = columns * HD
    scale = jnp.sqrt(total[:, width:width + 1] / D + EPS)
    projected = (total[:, :width] / scale).astype(BF16).astype(F32)
    for g in range(columns):
        tiles[:, g, :] = projected[:, g * HD:(g + 1) * HD]
    out[...] = tiles[:, :GQ, :].astype(BF16)
    rows = own.shape[0]
    own[...] = tiles[pl.ds(lax.div(lax.axis_index("kv"), 4) * rows, rows)]


def attention_kernel(
    one, near, far, cross, keys, values, info, own, out, slot_max, slot_sum, slot_value, best, summed, mixed, queries
):
    slots, rows = keys.shape[0], own.shape[0]
    best[...] = jnp.full(best.shape, NEGATIVE, F32)
    summed[...] = jnp.zeros(summed.shape, F32)
    mixed[...] = jnp.zeros(mixed.shape, F32)
    token = iota((GQ, CH), 1)
    scale = 1.0 / math.sqrt(HD)
    place = lax.rem(lax.axis_index("kv"), 4)
    quarter = one.shape[0]
    for k, part in enumerate((one, near, cross, far)):
        queries[pl.ds(jnp.bitwise_xor(place, k) * quarter, quarter)] = part[...]
    mine = place * quarter + lax.div(lax.axis_index("kv"), 4) * rows
    span = range(slots)
    owners = [info[0, s] for s in span]
    scores = [
        lax.dot_general(
            queries[jnp.minimum(r, REQ - 1)], keys[s], (((1,), (1,)), ((), ())), preferred_element_type=F32
        ) * scale
        for r, s in zip(owners, span)
    ]
    live = [token < info[1, s] for s in span]
    scores = [jnp.where(m, x, NEGATIVE) for m, x in zip(live, scores)]
    tops = [jnp.max(x, axis=1, keepdims=True) for x in scores]
    weights = [jnp.where(m, jnp.exp(x - t), 0.0) for m, x, t in zip(live, scores, tops)]
    totals = [jnp.sum(w, axis=1, keepdims=True) for w in weights]
    mixes = [jnp.dot(w.astype(BF16), values[s], preferred_element_type=F32) for w, s in zip(weights, span)]
    for r, s, top, total, mix in zip(owners, span, tops, totals, mixes):
        wide = jnp.broadcast_to(top, (GQ, HD))
        best[r] = jnp.maximum(best[r], wide)
        slot_max[s] = wide
        slot_sum[s] = jnp.broadcast_to(total, (GQ, HD))
        slot_value[s] = mix

    fresh = [
        jnp.broadcast_to(
            jnp.sum(own[i, :GQ, :] * own[i, GQ:GQ + 1, :], axis=1, keepdims=True) / math.sqrt(HD), (GQ, HD)
        )
        for i in range(rows)
    ]
    for i in range(rows):
        best[mine + i] = jnp.maximum(best[mine + i], fresh[i])
    upper, lower = halves(best[...])
    best[...] = upper + lower
    for i in range(rows):
        factor = jnp.exp(fresh[i] - best[mine + i])
        summed[mine + i] = factor
        mixed[mine + i] = factor * own[i, GQ + 1:GQ + 2, :]
    for r, s in zip(owners, span):
        factor = jnp.exp(slot_max[s] - best[r])
        summed[r] = summed[r] + factor * slot_sum[s]
        mixed[r] = mixed[r] + factor * slot_value[s]

    lane, sub = iota((GQ, HD), 1), iota((GQ, HD), 0)
    line = iota((LINES, HD), 0)
    stats = jnp.zeros((LINES, HD), F32)
    for i in range(LINES):
        packed = jnp.zeros((GQ, HD), F32)
        for c in range(REQ // LINES):
            r = c * LINES + i
            for k, part in enumerate(halves(best[r]) + halves(summed[r])):
                packed = jnp.where(lane == sub + (4 * c + k) * GQ, part, packed)
        stats = jnp.where(line == i, jnp.sum(packed, axis=0, keepdims=True), stats)
    out[:REQ * GQ, :] = mixed[0:REQ].reshape(REQ * GQ, HD).astype(BF16)
    out[REQ * GQ:, :] = stats.astype(BF16)


def merge_weights(parts):
    lines = [part[REQ * GQ:, :].astype(F32) for part in parts]
    tops = [x + pltpu.roll(x, HD - GQ, axis=1) for x in lines]
    sums = [pltpu.roll(x, HD - 2 * GQ, axis=1) for x in tops]
    top = jnp.maximum(jnp.maximum(tops[0], tops[1]), jnp.maximum(tops[2], tops[3]))
    factors = [jnp.exp(x - top) for x in tops]
    terms = [f * x for f, x in zip(factors, sums)]
    return top, factors, (terms[0] + terms[1]) + (terms[2] + terms[3])


def weighted(parts, factors, store):
    columns = [f.T for f in factors]
    for r in range(0, REQ, 2):
        c, i = r // LINES, r % LINES
        blocks = [part[r * GQ:(r + 2) * GQ, :].astype(F32) for part in parts]
        pair = []
        for u in range(2):
            at = slice(4 * c * GQ, (4 * c + 1) * GQ)
            terms = [t[at, i + u:i + u + 1] * b[u * GQ:(u + 1) * GQ] for t, b in zip(columns, blocks)]
            pair.append((terms[0] + terms[1]) + (terms[2] + terms[3]))
        store(r, jnp.concatenate(pair, axis=0))


def merge_kernel(own, near, far, cross, out):
    parts = own, near, far, cross
    top, factors, total = merge_weights(parts)

    def store(r, value):
        out[r * GQ:(r + 2) * GQ, :] = value.astype(BF16)

    weighted(parts, factors, store)
    place = lax.rem(iota((LINES, HD), 1), 4 * GQ)
    packed = jnp.zeros((LINES, HD), F32)
    for k, part in enumerate(halves(top) + halves(total)):
        moved = part if k == 0 else pltpu.roll(part, k * GQ, axis=1)
        packed = jnp.where((place >= k * GQ) & (place < (k + 1) * GQ), moved, packed)
    out[REQ * GQ:, :] = packed.astype(BF16)


def attention_out_kernel(own, near, far, cross, weight, out, tall, flat):
    parts = own, near, far, cross
    _, factors, total = merge_weights(parts)

    def store(r, value):
        tall[r * GQ:(r + 2) * GQ, :] = value

    weighted(parts, [f / total for f in factors], store)
    for g in range(GQ):
        flat[:, g * HD:(g + 1) * HD] = tall[pl.ds(g, REQ, stride=GQ), :].astype(BF16)
    out[...] = jnp.dot(flat[...], weight[...], preferred_element_type=F32)


def stacked(blocks, flat):
    peers, rows, _ = blocks.shape
    for p in range(peers):
        flat[p * rows:(p + 1) * rows, :] = blocks[p].astype(F32)


def four(own, near, far, cross):
    return (own[...].astype(F32) + near[...].astype(F32)) + (far[...].astype(F32) + cross[...].astype(F32))


def mixing_kernel(own, near, far, cross, hidden, gain, request, weight, out, middle):
    total = hidden[...].astype(F32) + four(own, near, far, cross)
    inner = total.astype(BF16)
    middle[...] = inner
    n = request.shape[1]
    pick = (as_column(request[...]) == iota((n, n), 1)).astype(F32).astype(BF16)
    ordered = jnp.dot(pick, inner, preferred_element_type=F32)
    upper, lower = halves(jnp.sum(ordered * ordered, axis=1, keepdims=True))
    lane = iota((n, HD), 1)
    tail = jnp.where(lane == 0, upper, jnp.where(lane == 1, lower, 0.0))
    scaled = jnp.concatenate(
        [(ordered[:, c * HD:(c + 1) * HD] * gain[c:c + 1, :]).astype(BF16) for c in range(gain.shape[0])], axis=1
    )
    groups, rows, _ = out.shape
    width = weight.shape[1]
    step = 4 * HD
    for c in range(0, width, step):
        y = jnp.dot(scaled, weight[:, c:c + step], preferred_element_type=F32)
        for p in range(groups):
            out[p, :, c:c + step] = y[p * rows:(p + 1) * rows].astype(BF16)
    for p in range(groups):
        out[p, :, width:] = tail[p * rows:(p + 1) * rows].astype(BF16)


def lightning_kernel(parts, decay, states, gain, out, turned, mixed, flat, wide):
    rows, heads = states.shape[0], states.shape[1]
    total = parts[0].astype(F32)
    for p in range(1, parts.shape[0]):
        total = total + parts[p].astype(F32)
    width = 4 * heads * HD
    scale = jnp.sqrt((total[:, width:width + 1] + total[:, width + 1:width + 2]) / D + EPS)
    wide[0:rows, :] = total[:, :width] / scale
    for h in range(heads):
        for k in range(4):
            mixed[h, k * rows:(k + 1) * rows, :] = wide[0:rows, (4 * h + k) * HD:(4 * h + k + 1) * HD]
    keep = jnp.exp(-decay[...])
    span = range(heads)
    mixing = [mixed[h] for h in span]
    below = [1.0 + jnp.exp(-m) for m in mixing]
    silu = [m / b for m, b in zip(mixing, below)]
    gates = [1.0 / b[3 * rows:] for b in below]
    columns = jnp.concatenate([v[:2 * rows] for v in silu], axis=0).T
    turned[...] = columns
    for h in span:
        mixed[h] = silu[h]
    inner = [jnp.sum(v[:rows] * v[rows:2 * rows], axis=1, keepdims=True) for v in silu]
    for j in range(rows):
        for h in span:
            at = 2 * rows * h + j
            read = jnp.sum(columns[:, at:at + 1] * states[j, h], axis=0, keepdims=True)
            flat[j:j + 1, h * HD:(h + 1) * HD] = read
    read_squares = jnp.zeros((rows, 1), F32)
    for h in span:
        at = slice(h * HD, (h + 1) * HD)
        read = keep[:, h:h + 1] * flat[0:rows, at] + inner[h] * silu[h][2 * rows:3 * rows]
        read_squares = read_squares + jnp.sum(read * read, axis=1, keepdims=True)
        flat[0:rows, at] = read * gain[h:h + 1, :] * gates[h]
    size = heads * HD
    gated = flat[0:rows, 0:size].astype(BF16)
    upper, lower = halves(read_squares)
    lane = iota((rows, HD), 1)
    tail = jnp.where(lane == 0, upper, jnp.where(lane == 1, lower, 0.0)).astype(BF16)
    for p in range(out.shape[0]):
        out[p, :, :size] = gated
        out[p, :, size:] = tail


def renew_kernel(turned, mixed, decay, states, renewed, block, sems):
    rows, heads = states.shape[0], states.shape[1]
    keep = jnp.exp(-decay[...])
    copies = [pltpu.make_async_copy(block.at[j], renewed.at[j], sems.at[j]) for j in range(rows)]
    for j in range(rows):
        for h in range(heads):
            value = mixed[h, 2 * rows + j:2 * rows + j + 1, :]
            at = 2 * rows * h + rows + j
            block[j, h] = keep[:, h:h + 1] * states[j, h] + turned[:, at:at + 1] * value
        copies[j].start()
    for copy in copies:
        copy.wait()


def lightning_out_kernel(blocks, request, weight, out, flat):
    stacked(blocks, flat)
    n = request.shape[1]
    size = weight.shape[0]
    pick = (iota((n, n), 0) == request[...]).astype(F32).astype(BF16)
    placed = jnp.dot(pick, flat[...].astype(BF16), preferred_element_type=F32)
    out[0:n, :] = jnp.dot(placed[:, :size].astype(BF16), weight[...], preferred_element_type=F32)
    squares = as_row(placed[:, size:size + 1] + placed[:, size + 1:size + 2])
    out[n:, :] = jnp.zeros((out.shape[0] - n, out.shape[1]), F32)
    out[n:n + 1, 0:n] = squares


def pair_kernel(own, near, out):
    n = own.shape[0] - 8
    total = own[...] + near[...]
    out[0:n, :] = total[0:n].astype(BF16)
    upper, lower = halves(total[n:n + 1])
    line = iota((out.shape[0] - n, out.shape[1]), 0)
    out[n:, :] = jnp.where(line == 0, upper, jnp.where(line == 1, lower, 0.0)).astype(BF16)


def last_kernel(own, near, far, cross, middle, out):
    n = middle.shape[0]
    total = four(own, near, far, cross)
    squares = as_column(total[n:n + 1, 0:n] + total[n + 1:n + 2, 0:n])
    scale = 1.0 / jnp.sqrt(squares / (LH * HD) + EPS)
    out[...] = (middle[...].astype(F32) + total[0:n, :] * scale).astype(BF16)


def exchange(blocks):
    return lax.all_to_all(blocks, "kv", 0, 0, tiled=True)


def other_core(value):
    return lax.ppermute(value, "head", [(i, i ^ 1) for i in range(lax.axis_size("head"))])


def spread(parts, axis, stride):
    size = lax.axis_size(axis)
    own, *others = parts
    return (
        own,
        *(
            lax.ppermute(part, axis, [(i, i ^ (k * stride)) for i in range(size)])
            for part, k in zip(others, (1, 3, 2))
        ),
    )


def along(value, axis, stride):
    return spread([value] * 4, axis, stride)


def per_device(
    hidden_in,
    attn_gain,
    attn_weight,
    attn_out_weight,
    cache_keys,
    cache_values,
    stretch_counts,
    tail_tokens,
    slot_stretch,
    lin_gain,
    lin_weight,
    decay_rate,
    states,
    out_gain,
    lin_out_weight,
    state_request,
):
    peers = lax.axis_size("kv")
    requests, features = hidden_in.shape
    rows = requests // peers
    width = attn_weight.shape[1]
    slots = cache_keys.shape[0]
    heads = decay_rate.shape[0]
    lin_width = lin_weight.shape[1]
    size = heads * HD
    S = jax.ShapeDtypeStruct
    request = state_request[None, :]

    chunks = features // HD
    keys = cache_keys.reshape(slots, CH, HD)
    values = cache_values.reshape(slots, CH, HD)
    plan = stretch_counts[None, :], tail_tokens[None, :], slot_stretch[None, :]

    quarter = requests // 4
    block = S((quarter, width + HD), F32)
    own, cross, far, near, info = kernel_call(
        project_kernel,
        (block, block, block, block, S((2, slots), jnp.int32)),
        [HBM] * 6, 8 * MIB, 2 * requests * features * width, 2 * features * width,
        [
            pltpu.VMEM((requests, features), BF16),
            pltpu.VMEM((chunks, HD), F32),
            pltpu.VMEM((features, width), BF16),
            pltpu.VMEM((1, requests), jnp.int32),
            pltpu.VMEM((1, requests), jnp.int32),
            pltpu.VMEM((1, slots), jnp.int32),
            pltpu.VMEM((requests, width + HD), F32),
            pltpu.SemaphoreType.DMA((5 + chunks,)),
        ],
    )(
        in_hbm(hidden_in), in_hbm(attn_gain.reshape(chunks, HD)), in_hbm(attn_weight),
        *(in_hbm(row) for row in plan),
    )
    parts = kernel_call(
        sum_kernel, block, [VMEM] * 4, 8 * MIB, 0, 20 * quarter * width,
    )(*spread((own, near, far, cross), "kv", 1))
    queries, own = kernel_call(
        normalise_kernel,
        (S((quarter, GQ, HD), BF16), S((rows, GQ + 2, HD), F32)),
        [VMEM] * 4 + [HBM] * 2, 8 * MIB, 0, 20 * quarter * width,
        [pltpu.VMEM((quarter, GQ + 2, HD), F32)],
    )(*along(parts, "kv", 4), in_hbm(keys), in_hbm(values))
    tiles = [pltpu.VMEM((slots, GQ, HD), F32)] * 3 + [pltpu.VMEM((requests + 1, GQ, HD), F32)] * 3
    tiles.append(pltpu.VMEM((requests, GQ, HD), BF16))
    partial = S((requests * GQ + LINES, HD), BF16)
    part = kernel_call(
        attention_kernel, partial,
        [VMEM] * 6 + [SMEM, VMEM], 24 * MIB, 4 * slots * GQ * CH * HD, 4 * slots * CH * HD, tiles,
    )(*along(queries, "kv", 1), keys, values, info, own)
    part = kernel_call(
        merge_kernel, partial, [VMEM] * 4, 8 * MIB, 0, 10 * requests * GQ * HD,
    )(*along(part, "kv", 1))
    first = kernel_call(
        attention_out_kernel,
        S((requests, features), F32),
        [VMEM] * 5, 8 * MIB, 2 * requests * GQ * HD * features, 2 * GQ * HD * features,
        [pltpu.VMEM((requests * GQ, HD), F32), pltpu.VMEM((requests, GQ * HD), BF16)],
    )(*along(part, "kv", 4), attn_out_weight)
    mixing, middle = kernel_call(
        mixing_kernel,
        (S((peers, rows, lin_width + HD), BF16), S((requests, features), BF16)),
        [VMEM] * 8, 16 * MIB, 2 * requests * features * lin_width, 2 * features * lin_width,
    )(*along((first + other_core(first)).astype(BF16), "head", 2), hidden_in, lin_gain.reshape(chunks, HD), request, lin_weight)
    decay = decay_rate[None, :]
    gated, turned, mixed = kernel_call(
        lightning_kernel,
        (
            S((peers, rows, size + HD), BF16),
            S((HD, 2 * rows * heads), F32),
            S((heads, 4 * rows, HD), F32),
        ),
        [VMEM] * 4, 16 * MIB, 0, 8 * rows * size * HD,
        [pltpu.VMEM((8, size), F32), pltpu.VMEM((8, lin_width), F32)],
    )(exchange(mixing), decay, states, out_gain.reshape(heads, HD))
    second = kernel_call(
        lightning_out_kernel,
        S((requests + 8, features), F32),
        [VMEM] * 3, 8 * MIB, 2 * requests * size * features, 2 * size * features,
        [pltpu.VMEM((requests, size + HD), F32)],
    )(exchange(gated), request, lin_out_weight)
    pair = kernel_call(
        pair_kernel, S((requests + 16, features), BF16), [VMEM] * 2, 4 * MIB, 0, 16 * requests * features,
    )(second, other_core(second))
    renewed = kernel_call(
        renew_kernel, S(states.shape, F32), [VMEM] * 4, 8 * MIB, 0, 8 * rows * size * HD,
        [pltpu.VMEM(states.shape, F32), pltpu.SemaphoreType.DMA((rows,))], pltpu.HBM,
    )(turned, mixed, decay, states)
    hidden_out = kernel_call(
        last_kernel,
        S((requests, features), BF16),
        [VMEM] * 5, 4 * MIB, 0, 16 * requests * features,
    )(*along(pair, "head", 2), middle)
    return hidden_out, renewed


def solution(mesh):
    placed = (
        P(None, "kv"),
        P("kv"),
        P("kv", "head"),
        P("head", "kv"),
        P("kv", "head", None, None),
        P("kv", "head", None, None),
        P(),
        P(),
        P("kv"),
        P("kv"),
        P("kv", "head"),
        P("head"),
        P("kv", "head", None, None),
        P("head"),
        P("head", "kv"),
        P(),
    )
    return jax.shard_map(
        per_device,
        mesh=mesh,
        in_specs=placed,
        out_specs=(P(None, "kv"), P("kv", "head", None, None)),
        check_vma=False,
    )
```

```python
import functools
import math

import jax
import jax.numpy as jnp
from jax import lax
from jax.experimental import pallas as pl
from jax.experimental.pallas import tpu as pltpu
from jax.sharding import PartitionSpec as P

D = 6144
HD = 128
LH = 64
CH = 256
GQ = 8
REQ = 64
EPS = 1e-05
NEGATIVE = -1e30
F32 = jnp.float32
BF16 = jnp.bfloat16
MIB = 1 << 20
LINES = 16


def iota(shape, dim):
    return lax.broadcasted_iota(jnp.int32, shape, dim)


def as_column(row):
    n = row.shape[1]
    eye = iota((n, n), 0) == iota((n, n), 1)
    return jnp.sum(jnp.where(eye, row, jnp.zeros_like(row)), axis=1, keepdims=True)


def as_row(column):
    n = column.shape[0]
    eye = iota((n, n), 0) == iota((n, n), 1)
    return jnp.sum(jnp.where(eye, column, jnp.zeros_like(column)), axis=0, keepdims=True)


def kernel_call(body, outs, ins, limit, flops, moved, scratch=(), space=pltpu.VMEM):
    return pl.pallas_call(
        body,
        out_shape=outs,
        in_specs=ins,
        out_specs=jax.tree.map(lambda _: pl.BlockSpec(memory_space=space), outs),
        scratch_shapes=scratch,
        compiler_params=pltpu.CompilerParams(vmem_limit_bytes=limit),
        cost_estimate=pl.CostEstimate(flops=flops, bytes_accessed=moved, transcendentals=0),
    )


VMEM = pl.BlockSpec(memory_space=pltpu.VMEM)
SMEM = pl.BlockSpec(memory_space=pltpu.SMEM)
HBM = pl.BlockSpec(memory_space=pltpu.HBM)


def in_hbm(value):
    return pltpu.with_memory_space_constraint(value, pltpu.HBM)


def halves(value):
    upper = value.astype(BF16).astype(F32)
    return upper, (value - upper).astype(BF16).astype(F32)


def project_kernel(
    hidden_hbm, gain_hbm, weight_hbm, counts_hbm, tails_hbm, slots_hbm, own, cross, far, near, info,
    hidden, gain, weight, counts, tails, slots, whole, sems,
):
    chunks = gain.shape[0]
    first = [(hidden_hbm, hidden), (gain_hbm, gain)]
    blocks = [
        (weight_hbm.at[c * HD:(c + 1) * HD, :], weight.at[c * HD:(c + 1) * HD, :]) for c in range(chunks)
    ]
    last = [(counts_hbm, counts), (tails_hbm, tails), (slots_hbm, slots)]
    copies = [
        pltpu.make_async_copy(source, target, sems.at[k])
        for k, (source, target) in enumerate(first + blocks + last)
    ]
    for copy in copies:
        copy.start()
    for copy in copies[:2] + copies[2 + chunks:]:
        copy.wait()
    x = hidden[...].astype(F32)
    squares = jnp.sum(x * x, axis=1, keepdims=True)
    scaled = [(x[:, c * HD:(c + 1) * HD] * gain[c:c + 1, :]).astype(BF16) for c in range(chunks)]
    number = counts[...]
    n = number.shape[1]
    below = iota((n, n), 1) <= iota((n, n), 0)
    ends = jnp.sum(jnp.where(below, number, 0), axis=1, keepdims=True)
    count = as_column(number)
    starts = ends - count
    limits = count * CH - as_column(tails[...])
    slot = slots[...]
    owner = jnp.sum((slot >= ends).astype(jnp.int32), axis=0, keepdims=True)
    hits = iota((n, slot.shape[1]), 0) == owner
    begin = jnp.sum(jnp.where(hits, starts, 0), axis=0, keepdims=True)
    limit = jnp.sum(jnp.where(hits, limits, 0), axis=0, keepdims=True)
    live = jnp.clip(limit - (slot - begin) * CH, 0, CH)
    info[0:1, :] = owner
    info[1:2, :] = jnp.where(owner < n, live, 0)
    y = jnp.zeros((x.shape[0], weight.shape[1]), F32)
    for c in range(chunks):
        copies[2 + c].wait()
        y = y + jnp.dot(scaled[c], weight[c * HD:(c + 1) * HD, :], preferred_element_type=F32)
    width = weight.shape[1]
    whole[:, :width] = y
    whole[:, width:] = jnp.broadcast_to(squares, (x.shape[0], HD))
    place = lax.rem(lax.axis_index("kv"), 4)
    rows = own.shape[0]
    for k, part in enumerate((own, near, cross, far)):
        at = pl.multiple_of(jnp.bitwise_xor(place, k) * rows, rows)
        part[...] = whole[pl.ds(at, rows), :]


def sum_kernel(own, near, far, cross, out):
    out[...] = four(own, near, far, cross)


def normalise_kernel(one, near, far, cross, keys, values, out, own, tiles):
    total = four(one, near, far, cross)
    columns = own.shape[1]
    width = columns * HD
    scale = jnp.sqrt(total[:, width:width + 1] / D + EPS)
    projected = (total[:, :width] / scale).astype(BF16).astype(F32)
    for g in range(columns):
        tiles[:, g, :] = projected[:, g * HD:(g + 1) * HD]
    out[...] = tiles[:, :GQ, :].astype(BF16)
    rows = own.shape[0]
    own[...] = tiles[pl.ds(lax.div(lax.axis_index("kv"), 4) * rows, rows)]


def attention_kernel(
    one, near, far, cross, keys, values, info, own, out, slot_max, slot_sum, slot_value, best, summed, mixed, queries
):
    slots, rows = keys.shape[0], own.shape[0]
    best[...] = jnp.full(best.shape, NEGATIVE, F32)
    summed[...] = jnp.zeros(summed.shape, F32)
    mixed[...] = jnp.zeros(mixed.shape, F32)
    token = iota((GQ, CH), 1)
    scale = 1.0 / math.sqrt(HD)
    place = lax.rem(lax.axis_index("kv"), 4)
    quarter = one.shape[0]
    for k, part in enumerate((one, near, cross, far)):
        queries[pl.ds(jnp.bitwise_xor(place, k) * quarter, quarter)] = part[...]
    mine = place * quarter + lax.div(lax.axis_index("kv"), 4) * rows
    span = range(slots)
    owners = [info[0, s] for s in span]
    scores = [
        lax.dot_general(
            queries[jnp.minimum(r, REQ - 1)], keys[s], (((1,), (1,)), ((), ())), preferred_element_type=F32
        ) * scale
        for r, s in zip(owners, span)
    ]
    live = [token < info[1, s] for s in span]
    scores = [jnp.where(m, x, NEGATIVE) for m, x in zip(live, scores)]
    tops = [jnp.max(x, axis=1, keepdims=True) for x in scores]
    weights = [jnp.where(m, jnp.exp(x - t), 0.0) for m, x, t in zip(live, scores, tops)]
    totals = [jnp.sum(w, axis=1, keepdims=True) for w in weights]
    mixes = [jnp.dot(w.astype(BF16), values[s], preferred_element_type=F32) for w, s in zip(weights, span)]
    for r, s, top, total, mix in zip(owners, span, tops, totals, mixes):
        wide = jnp.broadcast_to(top, (GQ, HD))
        best[r] = jnp.maximum(best[r], wide)
        slot_max[s] = wide
        slot_sum[s] = jnp.broadcast_to(total, (GQ, HD))
        slot_value[s] = mix

    fresh = [
        jnp.broadcast_to(
            jnp.sum(own[i, :GQ, :] * own[i, GQ:GQ + 1, :], axis=1, keepdims=True) / math.sqrt(HD), (GQ, HD)
        )
        for i in range(rows)
    ]
    for i in range(rows):
        best[mine + i] = jnp.maximum(best[mine + i], fresh[i])
    upper, lower = halves(best[...])
    best[...] = upper + lower
    for i in range(rows):
        factor = jnp.exp(fresh[i] - best[mine + i])
        summed[mine + i] = factor
        mixed[mine + i] = factor * own[i, GQ + 1:GQ + 2, :]
    for r, s in zip(owners, span):
        factor = jnp.exp(slot_max[s] - best[r])
        summed[r] = summed[r] + factor * slot_sum[s]
        mixed[r] = mixed[r] + factor * slot_value[s]

    lane, sub = iota((GQ, HD), 1), iota((GQ, HD), 0)
    line = iota((LINES, HD), 0)
    stats = jnp.zeros((LINES, HD), F32)
    for i in range(LINES):
        packed = jnp.zeros((GQ, HD), F32)
        for c in range(REQ // LINES):
            r = c * LINES + i
            for k, part in enumerate(halves(best[r]) + halves(summed[r])):
                packed = jnp.where(lane == sub + (4 * c + k) * GQ, part, packed)
        stats = jnp.where(line == i, jnp.sum(packed, axis=0, keepdims=True), stats)
    out[:REQ * GQ, :] = mixed[0:REQ].reshape(REQ * GQ, HD).astype(BF16)
    out[REQ * GQ:, :] = stats.astype(BF16)


def merge_weights(parts):
    lines = [part[REQ * GQ:, :].astype(F32) for part in parts]
    tops = [x + pltpu.roll(x, HD - GQ, axis=1) for x in lines]
    sums = [pltpu.roll(x, HD - 2 * GQ, axis=1) for x in tops]
    top = jnp.maximum(jnp.maximum(tops[0], tops[1]), jnp.maximum(tops[2], tops[3]))
    factors = [jnp.exp(x - top) for x in tops]
    terms = [f * x for f, x in zip(factors, sums)]
    return top, factors, (terms[0] + terms[1]) + (terms[2] + terms[3])


def weighted(parts, factors, store):
    columns = [f.T for f in factors]
    for r in range(0, REQ, 2):
        c, i = r // LINES, r % LINES
        blocks = [part[r * GQ:(r + 2) * GQ, :].astype(F32) for part in parts]
        pair = []
        for u in range(2):
            at = slice(4 * c * GQ, (4 * c + 1) * GQ)
            terms = [t[at, i + u:i + u + 1] * b[u * GQ:(u + 1) * GQ] for t, b in zip(columns, blocks)]
            pair.append((terms[0] + terms[1]) + (terms[2] + terms[3]))
        store(r, jnp.concatenate(pair, axis=0))


def merge_kernel(own, near, far, cross, out):
    parts = own, near, far, cross
    top, factors, total = merge_weights(parts)

    def store(r, value):
        out[r * GQ:(r + 2) * GQ, :] = value.astype(BF16)

    weighted(parts, factors, store)
    place = lax.rem(iota((LINES, HD), 1), 4 * GQ)
    packed = jnp.zeros((LINES, HD), F32)
    for k, part in enumerate(halves(top) + halves(total)):
        moved = part if k == 0 else pltpu.roll(part, k * GQ, axis=1)
        packed = jnp.where((place >= k * GQ) & (place < (k + 1) * GQ), moved, packed)
    out[REQ * GQ:, :] = packed.astype(BF16)


def attention_out_kernel(own, near, far, cross, weight, out, tall, flat):
    parts = own, near, far, cross
    _, factors, total = merge_weights(parts)

    def store(r, value):
        tall[r * GQ:(r + 2) * GQ, :] = value

    weighted(parts, [f / total for f in factors], store)
    for g in range(GQ):
        flat[:, g * HD:(g + 1) * HD] = tall[pl.ds(g, REQ, stride=GQ), :].astype(BF16)
    out[...] = jnp.dot(flat[...], weight[...], preferred_element_type=F32)


def stacked(blocks, flat):
    peers, rows, _ = blocks.shape
    for p in range(peers):
        flat[p * rows:(p + 1) * rows, :] = blocks[p].astype(F32)


def four(own, near, far, cross):
    return (own[...].astype(F32) + near[...].astype(F32)) + (far[...].astype(F32) + cross[...].astype(F32))


def mixing_kernel(own, near, far, cross, hidden, gain, request, weight, out, middle):
    total = hidden[...].astype(F32) + four(own, near, far, cross)
    inner = total.astype(BF16)
    middle[...] = inner
    n = request.shape[1]
    pick = (as_column(request[...]) == iota((n, n), 1)).astype(F32).astype(BF16)
    ordered = jnp.dot(pick, inner, preferred_element_type=F32)
    upper, lower = halves(jnp.sum(ordered * ordered, axis=1, keepdims=True))
    lane = iota((n, HD), 1)
    tail = jnp.where(lane == 0, upper, jnp.where(lane == 1, lower, 0.0))
    scaled = jnp.concatenate(
        [(ordered[:, c * HD:(c + 1) * HD] * gain[c:c + 1, :]).astype(BF16) for c in range(gain.shape[0])], axis=1
    )
    groups, rows, _ = out.shape
    width = weight.shape[1]
    step = 4 * HD
    for c in range(0, width, step):
        y = jnp.dot(scaled, weight[:, c:c + step], preferred_element_type=F32)
        for p in range(groups):
            out[p, :, c:c + step] = y[p * rows:(p + 1) * rows].astype(BF16)
    for p in range(groups):
        out[p, :, width:] = tail[p * rows:(p + 1) * rows].astype(BF16)


def lightning_kernel(parts, decay, states, gain, out, turned, mixed, flat):
    rows, heads = states.shape[0], states.shape[1]
    total = parts[0].astype(F32)
    for p in range(1, parts.shape[0]):
        total = total + parts[p].astype(F32)
    width = 4 * heads * HD
    scale = 1.0 / jnp.sqrt((total[:, width:width + 1] + total[:, width + 1:width + 2]) / D + EPS)
    for h in range(heads):
        for k in range(4):
            at = (4 * h + k) * HD
            mixed[h, k * rows:(k + 1) * rows, :] = total[:, at:at + HD] * scale
    keep = jnp.exp(-decay[...])
    span = range(heads)
    mixing = [mixed[h] for h in span]
    below = [1.0 + jnp.exp(-m) for m in mixing]
    silu = [m / b for m, b in zip(mixing, below)]
    gates = [1.0 / b[3 * rows:] for b in below]
    columns = jnp.concatenate([v[:2 * rows] for v in silu], axis=0).T
    turned[...] = columns
    for h in span:
        mixed[h] = silu[h]
    inner = [jnp.sum(v[:rows] * v[rows:2 * rows], axis=1, keepdims=True) for v in silu]
    for j in range(rows):
        for h in span:
            at = 2 * rows * h + j
            read = jnp.sum(columns[:, at:at + 1] * states[j, h], axis=0, keepdims=True)
            flat[j:j + 1, h * HD:(h + 1) * HD] = read
    read_squares = jnp.zeros((rows, 1), F32)
    for h in span:
        at = slice(h * HD, (h + 1) * HD)
        read = keep[:, h:h + 1] * flat[0:rows, at] + inner[h] * silu[h][2 * rows:3 * rows]
        read_squares = read_squares + jnp.sum(read * read, axis=1, keepdims=True)
        flat[0:rows, at] = read * gain[h:h + 1, :] * gates[h]
    size = heads * HD
    gated = flat[0:rows, 0:size].astype(BF16)
    upper, lower = halves(read_squares)
    lane = iota((rows, HD), 1)
    tail = jnp.where(lane == 0, upper, jnp.where(lane == 1, lower, 0.0)).astype(BF16)
    for p in range(out.shape[0]):
        out[p, :, :size] = gated
        out[p, :, size:] = tail


def renew_kernel(turned, mixed, decay, states, renewed, block, sems):
    rows, heads = states.shape[0], states.shape[1]
    keep = jnp.exp(-decay[...])
    copies = [pltpu.make_async_copy(block.at[j], renewed.at[j], sems.at[j]) for j in range(rows)]
    for j in range(rows):
        for h in range(heads):
            value = mixed[h, 2 * rows + j:2 * rows + j + 1, :]
            at = 2 * rows * h + rows + j
            block[j, h] = keep[:, h:h + 1] * states[j, h] + turned[:, at:at + 1] * value
        copies[j].start()
    for copy in copies:
        copy.wait()


def lightning_out_kernel(blocks, request, weight, out, flat):
    stacked(blocks, flat)
    n = request.shape[1]
    size = weight.shape[0]
    pick = (iota((n, n), 0) == request[...]).astype(F32).astype(BF16)
    placed = jnp.dot(pick, flat[...].astype(BF16), preferred_element_type=F32)
    out[0:n, :] = jnp.dot(placed[:, :size].astype(BF16), weight[...], preferred_element_type=F32)
    squares = as_row(placed[:, size:size + 1] + placed[:, size + 1:size + 2])
    out[n:, :] = jnp.zeros((out.shape[0] - n, out.shape[1]), F32)
    out[n:n + 1, 0:n] = squares


def pair_kernel(own, near, out):
    n = own.shape[0] - 8
    total = own[...] + near[...]
    out[0:n, :] = total[0:n].astype(BF16)
    upper, lower = halves(total[n:n + 1])
    line = iota((out.shape[0] - n, out.shape[1]), 0)
    out[n:, :] = jnp.where(line == 0, upper, jnp.where(line == 1, lower, 0.0)).astype(BF16)


def last_kernel(own, near, far, cross, middle, out):
    n = middle.shape[0]
    total = four(own, near, far, cross)
    squares = as_column(total[n:n + 1, 0:n] + total[n + 1:n + 2, 0:n])
    scale = 1.0 / jnp.sqrt(squares / (LH * HD) + EPS)
    out[...] = (middle[...].astype(F32) + total[0:n, :] * scale).astype(BF16)


def exchange(blocks):
    return lax.all_to_all(blocks, "kv", 0, 0, tiled=True)


def other_core(value):
    return lax.ppermute(value, "head", [(i, i ^ 1) for i in range(lax.axis_size("head"))])


def spread(parts, axis, stride):
    size = lax.axis_size(axis)
    own, *others = parts
    return (
        own,
        *(
            lax.ppermute(part, axis, [(i, i ^ (k * stride)) for i in range(size)])
            for part, k in zip(others, (1, 3, 2))
        ),
    )


def along(value, axis, stride):
    return spread([value] * 4, axis, stride)


def per_device(
    hidden_in,
    attn_gain,
    attn_weight,
    attn_out_weight,
    cache_keys,
    cache_values,
    stretch_counts,
    tail_tokens,
    slot_stretch,
    lin_gain,
    lin_weight,
    decay_rate,
    states,
    out_gain,
    lin_out_weight,
    state_request,
):
    peers = lax.axis_size("kv")
    requests, features = hidden_in.shape
    rows = requests // peers
    width = attn_weight.shape[1]
    slots = cache_keys.shape[0]
    heads = decay_rate.shape[0]
    lin_width = lin_weight.shape[1]
    size = heads * HD
    S = jax.ShapeDtypeStruct
    request = state_request[None, :]

    chunks = features // HD
    keys = cache_keys.reshape(slots, CH, HD)
    values = cache_values.reshape(slots, CH, HD)
    plan = stretch_counts[None, :], tail_tokens[None, :], slot_stretch[None, :]

    quarter = requests // 4
    block = S((quarter, width + HD), F32)
    own, cross, far, near, info = kernel_call(
        project_kernel,
        (block, block, block, block, S((2, slots), jnp.int32)),
        [HBM] * 6, 8 * MIB, 2 * requests * features * width, 2 * features * width,
        [
            pltpu.VMEM((requests, features), BF16),
            pltpu.VMEM((chunks, HD), F32),
            pltpu.VMEM((features, width), BF16),
            pltpu.VMEM((1, requests), jnp.int32),
            pltpu.VMEM((1, requests), jnp.int32),
            pltpu.VMEM((1, slots), jnp.int32),
            pltpu.VMEM((requests, width + HD), F32),
            pltpu.SemaphoreType.DMA((5 + chunks,)),
        ],
    )(
        in_hbm(hidden_in), in_hbm(attn_gain.reshape(chunks, HD)), in_hbm(attn_weight),
        *(in_hbm(row) for row in plan),
    )
    parts = kernel_call(
        sum_kernel, block, [VMEM] * 4, 8 * MIB, 0, 20 * quarter * width,
    )(*spread((own, near, far, cross), "kv", 1))
    queries, own = kernel_call(
        normalise_kernel,
        (S((quarter, GQ, HD), BF16), S((rows, GQ + 2, HD), F32)),
        [VMEM] * 4 + [HBM] * 2, 8 * MIB, 0, 20 * quarter * width,
        [pltpu.VMEM((quarter, GQ + 2, HD), F32)],
    )(*along(parts, "kv", 4), in_hbm(keys), in_hbm(values))
    tiles = [pltpu.VMEM((slots, GQ, HD), F32)] * 3 + [pltpu.VMEM((requests + 1, GQ, HD), F32)] * 3
    tiles.append(pltpu.VMEM((requests, GQ, HD), BF16))
    partial = S((requests * GQ + LINES, HD), BF16)
    part = kernel_call(
        attention_kernel, partial,
        [VMEM] * 6 + [SMEM, VMEM], 24 * MIB, 4 * slots * GQ * CH * HD, 4 * slots * CH * HD, tiles,
    )(*along(queries, "kv", 1), keys, values, info, own)
    part = kernel_call(
        merge_kernel, partial, [VMEM] * 4, 8 * MIB, 0, 10 * requests * GQ * HD,
    )(*along(part, "kv", 1))
    first = kernel_call(
        attention_out_kernel,
        S((requests, features), F32),
        [VMEM] * 5, 8 * MIB, 2 * requests * GQ * HD * features, 2 * GQ * HD * features,
        [pltpu.VMEM((requests * GQ, HD), F32), pltpu.VMEM((requests, GQ * HD), BF16)],
    )(*along(part, "kv", 4), attn_out_weight)
    mixing, middle = kernel_call(
        mixing_kernel,
        (S((peers, rows, lin_width + HD), BF16), S((requests, features), BF16)),
        [VMEM] * 8, 16 * MIB, 2 * requests * features * lin_width, 2 * features * lin_width,
    )(*along((first + other_core(first)).astype(BF16), "head", 2), hidden_in, lin_gain.reshape(chunks, HD), request, lin_weight)
    decay = decay_rate[None, :]
    gated, turned, mixed = kernel_call(
        lightning_kernel,
        (
            S((peers, rows, size + HD), BF16),
            S((HD, 2 * rows * heads), F32),
            S((heads, 4 * rows, HD), F32),
        ),
        [VMEM] * 4, 16 * MIB, 0, 8 * rows * size * HD,
        [pltpu.VMEM((8, size), F32)],
    )(exchange(mixing), decay, states, out_gain.reshape(heads, HD))
    second = kernel_call(
        lightning_out_kernel,
        S((requests + 8, features), F32),
        [VMEM] * 3, 8 * MIB, 2 * requests * size * features, 2 * size * features,
        [pltpu.VMEM((requests, size + HD), F32)],
    )(exchange(gated), request, lin_out_weight)
    pair = kernel_call(
        pair_kernel, S((requests + 16, features), BF16), [VMEM] * 2, 4 * MIB, 0, 16 * requests * features,
    )(second, other_core(second))
    renewed = kernel_call(
        renew_kernel, S(states.shape, F32), [VMEM] * 4, 8 * MIB, 0, 8 * rows * size * HD,
        [pltpu.VMEM(states.shape, F32), pltpu.SemaphoreType.DMA((rows,))], pltpu.HBM,
    )(turned, mixed, decay, states)
    hidden_out = kernel_call(
        last_kernel,
        S((requests, features), BF16),
        [VMEM] * 5, 4 * MIB, 0, 16 * requests * features,
    )(*along(pair, "head", 2), middle)
    return hidden_out, renewed


def solution(mesh):
    placed = (
        P(None, "kv"),
        P("kv"),
        P("kv", "head"),
        P("head", "kv"),
        P("kv", "head", None, None),
        P("kv", "head", None, None),
        P(),
        P(),
        P("kv"),
        P("kv"),
        P("kv", "head"),
        P("head"),
        P("kv", "head", None, None),
        P("head"),
        P("head", "kv"),
        P(),
    )
    return jax.shard_map(
        per_device,
        mesh=mesh,
        in_specs=placed,
        out_specs=(P(None, "kv"), P("kv", "head", None, None)),
        check_vma=False,
    )
```
